128 devices in a mesh: blk: 32 (over z, y, x_hi), narrow: 4 (over x_lo, core).
Axes of the slice: x: 4 (x_hi: 2, x_lo: 2; x = x_hi * 2 + x_lo), y: 4, z: 4, core: 2. Of those that a mesh axis runs over, the one named last changes fastest.
Arguments:
- tokens: bfloat16 [16384, 1536], P(('blk', 'narrow')), may hold values from -6 to 6
- segments: int32 [16384], P(('blk', 'narrow')), may hold values from 0 to 15, never falling along the last dimension, each value on 1 to 2000 neighbouring positions
- attn_gain: float32 [1536], replicated, may hold values from 0.5 to 1.5
- w_query: bfloat16 [1536, 1536], P('blk', 'narrow'), may hold values from -0.15625 to 0.15625
- key_projection_weight: bfloat16 [1536, 512], P('blk', 'narrow'), may hold values from -0.15625 to 0.15625
- value_projection_weight: bfloat16 [1536, 512], P('blk', 'narrow'), may hold values from -0.15625 to 0.15625
- query_gain: float32 [64], replicated, may hold values from 0.1 to 1.9
- key_gain: float32 [64], replicated, may hold values from 0.1 to 1.9
- w_out: bfloat16 [1536, 1536], P('narrow', 'blk'), may hold values from -1.75 to 1.75
- ffn_gain: float32 [1536], replicated, may hold values from 0.5 to 1.5
- w_gate: bfloat16 [1536, 6912], P('blk', 'narrow'), may hold values from -0.15625 to 0.15625
- w_up: bfloat16 [1536, 6912], P('blk', 'narrow'), may hold values from -0.15625 to 0.15625
- w_down: bfloat16 [6912, 1536], P('narrow', 'blk'), may hold values from -0.078125 to 0.078125
- out_grad: bfloat16 [16384, 1536], P(('blk', 'narrow')), may hold values from -6 to 6
Outputs:
- result: bfloat16 [16384, 1536], P(('blk', 'narrow'))
- grad_tokens: bfloat16 [16384, 1536], P(('blk', 'narrow'))
- grad_attn_gain: float32 [1536], replicated
- grad_query: float32 [1536, 1536], P('blk', 'narrow')
- grad_key: float32 [1536, 512], P('blk', 'narrow')
- grad_value: float32 [1536, 512], P('blk', 'narrow')
- grad_query_gain: float32 [64], replicated
- grad_key_gain: float32 [64], replicated
- grad_out: float32 [1536, 1536], P('narrow', 'blk')
- grad_ffn_gain: float32 [1536], replicated
- grad_gate: float32 [1536, 6912], P('blk', 'narrow')
- grad_up: float32 [1536, 6912], P('blk', 'narrow')
- grad_down: float32 [6912, 1536], P('narrow', 'blk')
The draws below stay inside these ranges and needn't reach their ends.
Inputs may be any that keep to these rules, and one draw needn't show every extreme that they name: `segments`: segment numbers never fall along the sequence; each document holds 1 to 2000 tokens, one exactly 2000.
All inputs are finite; a program needn't handle non-finite values.
Results may differ from the reference program's by a relative error of at most 0.02.
Values may be sent and summed in bfloat16 or wider, within the bound.
A program may use at most 192 MiB of HBM per device.

```python
import math
import jax
import jax.numpy as jnp
import numpy as np
from jax import lax

MODEL_WIDTH = 1536
QUERY_HEADS = 24
KEY_VALUE_HEADS = 8
HEAD_SIZE_DIM = 64
FF = 6912
DOC_MOST = 2000
TOKENS = 16384
DOCS = 16


def block_scale(rng, extent, cuts, smallest, top_value):
    level = 1.0
    for axis_at, parts in cuts:
        draws = jax.random.uniform(jax.random.fold_in(jax.random.fold_in(rng, 6), axis_at), (parts,), jnp.float32, smallest / len(cuts), top_value / len(cuts))
        level = level * jnp.repeat(jnp.exp(draws), extent[axis_at] // parts).reshape((-1,) + (1,) * (len(extent) - 1 - axis_at))
    return level


def profile(count, total, reach, skew):
    loads = [(1 << 20) // math.isqrt(rank ** skew) + 1 for rank in range(2, count + 1)]
    rest, holding = total - reach - (count - 1), [1] * (count - 1)
    while rest > 0:
        movable = [i for i in range(count - 1) if holding[i] < reach]
        mass, budget = sum([loads[i] for i in movable]), rest
        for i in movable:
            addition = min(reach - holding[i], max(1, budget * loads[i] // mass), rest)
            holding[i] = holding[i] + addition
            rest = rest - addition
    return np.array([reach] + holding)


def uneven(rng, count, total, bound, lean):
    if count == 2:
        one = jax.random.randint(rng, (), max(1, total - bound), min(bound, total - 1) + 1)
        return jnp.stack([one, total - one])
    tallies = jnp.asarray(profile(count, total, bound, lean), jnp.int32)
    pairs = (count - 1) // 2
    donor, taker = tallies[1:1 + 2 * pairs:2], tallies[2:2 + 2 * pairs:2]
    room = jnp.minimum(donor - 1, bound - taker)
    moved = jax.random.randint(jax.random.fold_in(rng, 1), (pairs,), 0, 1 << 20) % (room + 1)
    tallies = tallies.at[1:1 + 2 * pairs:2].set(donor - moved).at[2:2 + 2 * pairs:2].set(taker + moved)
    return tallies[jax.random.permutation(jax.random.fold_in(rng, 2), count)]


def bell_draw(rng, extent, spread, bound, pieces=(), held_as=jnp.bfloat16):
    factor_of = block_scale(rng, extent, pieces, -0.22, 0.18) if pieces else 1.0
    values = jax.random.normal(rng, extent, jnp.float32) * spread * factor_of
    return jnp.minimum(jnp.maximum(values, -bound), bound).astype(held_as)


def setup_inputs(seed: int = 0) -> dict:
    arg_keys = jax.random.split(jax.random.key(seed), 15)
    tokens = bell_draw(arg_keys[0], (TOKENS, MODEL_WIDTH), 1.0, 6.0, ((0, 128),))
    segments = jnp.searchsorted(jnp.cumsum(uneven(arg_keys[1], DOCS, TOKENS, DOC_MOST, 1)), jnp.arange(TOKENS), side="right").astype(jnp.int32)
    attn_gain = jnp.clip(1.0 + 0.1 * jax.random.normal(arg_keys[2], (MODEL_WIDTH,), jnp.float32), 0.5, 1.5)
    w_query = bell_draw(arg_keys[3], (MODEL_WIDTH, QUERY_HEADS * HEAD_SIZE_DIM), MODEL_WIDTH ** -0.5, 0.15625, ((0, 32), (1, 4)))
    key_projection_weight = bell_draw(arg_keys[4], (MODEL_WIDTH, KEY_VALUE_HEADS * HEAD_SIZE_DIM), MODEL_WIDTH ** -0.5, 0.15625, ((0, 32), (1, 4)))
    value_projection_weight = bell_draw(arg_keys[5], (MODEL_WIDTH, KEY_VALUE_HEADS * HEAD_SIZE_DIM), MODEL_WIDTH ** -0.5, 0.15625, ((0, 32), (1, 4)))
    query_gain = jnp.clip(1.0 + 0.18 * jax.random.normal(arg_keys[6], (HEAD_SIZE_DIM,), jnp.float32), 0.1, 1.9)
    key_gain = jnp.clip(1.0 + 0.18 * jax.random.normal(arg_keys[7], (HEAD_SIZE_DIM,), jnp.float32), 0.1, 1.9)
    w_out = bell_draw(arg_keys[8], (QUERY_HEADS * HEAD_SIZE_DIM, MODEL_WIDTH), (max(QUERY_HEADS * HEAD_SIZE_DIM // 128, 1)) ** -0.5, 1.75, ((0, 4), (1, 32)))
    ffn_gain = jnp.clip(1.0 + 0.1 * jax.random.normal(arg_keys[9], (MODEL_WIDTH,), jnp.float32), 0.5, 1.5)
    w_gate = bell_draw(arg_keys[10], (MODEL_WIDTH, FF), MODEL_WIDTH ** -0.5, 0.15625, ((0, 32), (1, 4)))
    w_up = bell_draw(arg_keys[11], (MODEL_WIDTH, FF), MODEL_WIDTH ** -0.5, 0.15625, ((0, 32), (1, 4)))
    w_down = bell_draw(arg_keys[12], (FF, MODEL_WIDTH), FF ** -0.5, 0.078125, ((0, 4), (1, 32)))
    out_grad = bell_draw(arg_keys[13], (TOKENS, MODEL_WIDTH), 1.0, 6.0, ((0, 128),))
    return dict(tokens=tokens, segments=segments, attn_gain=attn_gain, w_query=w_query, key_projection_weight=key_projection_weight, value_projection_weight=value_projection_weight, query_gain=query_gain, key_gain=key_gain, w_out=w_out, ffn_gain=ffn_gain, w_gate=w_gate, w_up=w_up, w_down=w_down, out_grad=out_grad)


EPS = 1e-05
THETA = 1000000.0
NEG = -1e+30

@jax.custom_vjp
def lower_bound(v):
    return lax.optimization_barrier(v.astype(jnp.bfloat16)).astype(jnp.float32)

@jax.custom_vjp
def lower_bound_backward(v):
    return v

def low_keep(v):
    return (lower_bound(v), None)

def low_pass(kept, grad):
    return (grad,)

def back_keep(v):
    return (v, None)

def back_low(kept, grad):
    return (lower_bound(grad),)
lower_bound.defvjp(low_keep, low_pass)
lower_bound_backward.defvjp(back_keep, back_low)

def rms_scale(values, gain):
    inverse = lax.rsqrt(lax.optimization_barrier(jnp.mean(values * values, axis=-1, keepdims=True)) + EPS)
    return values * inverse * gain

def rotate(values, positions):
    half = values.shape[-1] // 2
    steps = jnp.arange(half, dtype=jnp.float32) * (2.0 / values.shape[-1])
    freqs = jnp.exp(-jnp.log(THETA) * steps)
    angles = positions[:, None] * freqs[None, :]
    cosine = jnp.cos(angles)[:, None, :]
    sine = jnp.sin(angles)[:, None, :]
    first_index = values[..., :half]
    second = values[..., half:]
    return jnp.concatenate([first_index * cosine - second * sine, second * cosine + first_index * sine], axis=-1)

def head_prepare(raw, gain, positions):
    return rotate(rms_scale(raw, gain), positions)

def matrix_product(left, right):
    return jnp.dot(left, right, precision=lax.Precision.HIGHEST, preferred_element_type=jnp.float32)

def reference(tokens, segments, attn_gain, w_query, key_projection_weight, value_projection_weight, query_gain, key_gain, w_out, ffn_gain, w_gate, w_up, w_down, out_grad):
    single_float = jnp.float32
    token_count = tokens.shape[0]
    query_block_tile = min(512, token_count)
    attention_span = -(-DOC_MOST // query_block_tile) * query_block_tile
    blocks = token_count // query_block_tile
    query_group = QUERY_HEADS // KEY_VALUE_HEADS
    scale = HEAD_SIZE_DIM ** (-0.5)
    positions = jnp.arange(token_count, dtype=jnp.int32)
    float_pos = positions.astype(single_float)
    pad_seg = jnp.concatenate([jnp.full((attention_span,), -1, jnp.int32), segments.astype(jnp.int32)])
    pad_pos = jnp.concatenate([jnp.full((attention_span,), -1, jnp.int32), positions])

    def attend(query_rows_full, key_rows_full, value_rows_full):
        key_padded = jnp.concatenate([jnp.zeros((attention_span, KEY_VALUE_HEADS, HEAD_SIZE_DIM), single_float), key_rows_full])
        value_padded = jnp.concatenate([jnp.zeros((attention_span, KEY_VALUE_HEADS, HEAD_SIZE_DIM), single_float), value_rows_full])

        def one(index):
            first_index = (index * query_block_tile).astype(jnp.int32)
            query_portion = lax.dynamic_slice_in_dim(query_rows_full, first_index, query_block_tile).reshape(query_block_tile, KEY_VALUE_HEADS, query_group, HEAD_SIZE_DIM)
            k_part = lax.dynamic_slice_in_dim(key_padded, first_index, attention_span + query_block_tile)
            v_part = lax.dynamic_slice_in_dim(value_padded, first_index, attention_span + query_block_tile)
            seg_q = lax.dynamic_slice_in_dim(segments.astype(jnp.int32), first_index, query_block_tile)
            pos_q = lax.dynamic_slice_in_dim(positions, first_index, query_block_tile)
            seg_k = lax.dynamic_slice_in_dim(pad_seg, first_index, attention_span + query_block_tile)
            pos_k = lax.dynamic_slice_in_dim(pad_pos, first_index, attention_span + query_block_tile)
            allowed = (seg_q[:, None] == seg_k[None, :]) & (pos_k[None, :] <= pos_q[:, None])
            raw = jnp.einsum('qhgd,khd->hgqk', query_portion, k_part, precision=lax.Precision.HIGHEST) * scale
            raw = lower_bound_backward(raw)
            probs = jax.nn.softmax(jnp.where(allowed[None, None], raw, NEG), axis=-1)
            out = jnp.einsum('hgqk,khd->qhgd', lower_bound(probs), v_part, precision=lax.Precision.HIGHEST)
            return out.reshape(query_block_tile, QUERY_HEADS * HEAD_SIZE_DIM)
        mapped = lax.map(jax.checkpoint(one), jnp.arange(blocks, dtype=jnp.int32))
        return mapped.reshape(token_count, QUERY_HEADS * HEAD_SIZE_DIM)

    def layer(x, g_one, wq, key_matrix, value_matrix, qg, kg, wo, g_two, wg, wu, wd):
        first_normalized = lower_bound(rms_scale(x, g_one))
        q_raw = lower_bound_backward(matrix_product(first_normalized, wq)).reshape(token_count, QUERY_HEADS, HEAD_SIZE_DIM)
        key_unrotated = lower_bound_backward(matrix_product(first_normalized, key_matrix)).reshape(token_count, KEY_VALUE_HEADS, HEAD_SIZE_DIM)
        value_rows_full = lower_bound_backward(lower_bound(matrix_product(first_normalized, value_matrix))).reshape(token_count, KEY_VALUE_HEADS, HEAD_SIZE_DIM)
        query_rows_full = lower_bound_backward(lower_bound(head_prepare(q_raw, qg, float_pos)))
        key_rows_full = lower_bound_backward(lower_bound(head_prepare(key_unrotated, kg, float_pos)))
        attended = lower_bound_backward(lower_bound(attend(query_rows_full, key_rows_full, value_rows_full)))
        mid = x + lower_bound_backward(matrix_product(attended, wo))
        normed_two = lower_bound(rms_scale(mid, g_two))
        gate = lower_bound_backward(matrix_product(normed_two, wg))
        up = lower_bound_backward(matrix_product(normed_two, wu))
        hidden = lower_bound(jax.nn.silu(gate) * up)
        return mid + lower_bound_backward(matrix_product(hidden, wd))
    result, back = jax.vjp(layer, tokens.astype(single_float), attn_gain.astype(single_float), w_query.astype(single_float), key_projection_weight.astype(single_float), value_projection_weight.astype(single_float), query_gain.astype(single_float), key_gain.astype(single_float), w_out.astype(single_float), ffn_gain.astype(single_float), w_gate.astype(single_float), w_up.astype(single_float), w_down.astype(single_float))
    grads = back(out_grad.astype(single_float))
    return (result.astype(jnp.bfloat16), grads[0].astype(jnp.bfloat16), grads[1], grads[2], grads[3], grads[4], grads[5], grads[6], grads[7], grads[8], grads[9], grads[10], grads[11])
```

```python
from functools import partial

import jax
import jax.numpy as jnp
from jax import lax
from jax.experimental import pallas as pl
from jax.experimental.pallas import tpu as pltpu
from jax.sharding import Mesh
from jax.sharding import PartitionSpec as P

EPS = 1e-05
THETA = 1000000.0
LOG2E = 1.4426950408889634
MESH = pl.DeviceIdType.MESH
BF = jnp.bfloat16
F32 = jnp.float32
HI = lax.Precision.HIGHEST
AXES = ("z", "y", "xh", "xl", "core")

D = 1536
HID = 864
HP = 896
CF = 3 * HP
CA = 512
ROWS = 1024
TILE = 256
NT = ((1,), (1,)), ((), ())
NN = ((1,), (0,)), ((), ())
TN = ((0,), (0,)), ((), ())


def mm(a, b, dims, precision=None):
    return lax.dot_general(a, b, dims, precision=precision, preferred_element_type=F32)


class Pos:
    def __init__(s):
        ax = lax.axis_index
        s.z, s.y, s.xh, s.xl, s.c = ax("z"), ax("y"), ax("xh"), ax("xl"), ax("core")
        s.x = s.xh * 2 + s.xl
        s.sb = s.z * 4 + s.y
        s.sib = s.at_x(0, 1 - s.c)

    def at_x(s, d, c=None):
        x = lax.rem(s.x + d, 4)
        return {"xh": x // 2, "xl": lax.rem(x, 2), "core": s.c if c is None else c}

    def at(s, axis, d):
        return {axis: lax.rem(getattr(s, axis) + d, 4)}

    def at_sb(s, d):
        t = lax.rem(s.sb + d + 16, 16)
        return {"z": t // 4, "y": lax.rem(t, 4)}


def barrier(p):
    b = pltpu.get_barrier_semaphore()
    peers = [p.at("y", 1), p.at("y", 2), p.at("y", 3), p.at("z", 1), p.at("z", 2), p.at("z", 3)]
    peers += [p.at_sb(d) for d in (1, 2, -1, -2)]
    peers += [p.at_x(d, cc) for d in (1, 2, 3) for cc in (p.c, 1 - p.c)] + [p.sib]
    for q in peers:
        pl.semaphore_signal(b, inc=1, device_id=q, device_id_type=MESH)
    pl.semaphore_wait(b, len(peers))


def rcopy(src, dst, ss, rs, dev):
    return pltpu.make_async_remote_copy(
        src_ref=src, dst_ref=dst, send_sem=ss, recv_sem=rs, device_id=dev, device_id_type=MESH
    )


def ds(start, n):
    return pl.ds(pl.multiple_of(start, 16), n)


class Half:
    def __init__(s, p, w, off, a, b, ss, rs):
        s.p, s.w, s.off, s.a, s.b, s.ss, s.rs = p, w, off, a, b, ss, rs
        s.sent = []

    def unit(s, ra, rb):
        ia = lax.rem(getattr(s.p, s.a) + ra, 4)
        ib = lax.rem(getattr(s.p, s.b) + rb, 4)
        zz, yy = (ia, ib) if s.a == "z" else (ib, ia)
        return s.w.at[ds((zz * 4 + yy) * 96 + s.off, 48)]

    def send(s, ra, rb, axis, d, rid):
        u = s.unit(ra, rb)
        k = rcopy(u, u, s.ss.at[len(s.sent)], s.rs.at[rid], s.p.at(axis, d))
        s.sent.append(k)
        k.start()

    def got(s, ra, rb, rid):
        u = s.unit(ra, rb)
        rcopy(u, u, s.ss.at[0], s.rs.at[rid], s.p.at(s.a, 1)).wait_recv()

    def own(s):
        s.send(0, 0, s.a, 1, 0)
        s.send(0, 0, s.a, 3, 1)
        s.send(0, 0, s.b, 1, 3)
        s.send(0, 0, s.b, 3, 7)

    def step(s, i):
        if i == 0:
            s.got(3, 0, 0)
            s.send(3, 0, s.a, 1, 2)
            s.send(3, 0, s.b, 1, 6)
            s.send(3, 0, s.b, 3, 10)
            s.got(1, 0, 1)
            s.send(1, 0, s.b, 1, 4)
            s.send(1, 0, s.b, 3, 8)
        if i == 1:
            s.got(0, 3, 3)
            s.send(0, 3, s.b, 1, 11)
            s.got(2, 0, 2)
            s.send(2, 0, s.b, 1, 5)
            s.send(2, 0, s.b, 3, 9)
        if i == 2:
            s.got(3, 1, 10)
            s.send(3, 1, s.b, 3, 14)
            s.got(1, 3, 4)
            s.send(1, 3, s.b, 1, 12)
        if i == 3:
            s.got(2, 1, 9)
            s.send(2, 1, s.b, 3, 13)
        if i == 4:
            s.got(0, 1, 7)
            s.got(1, 1, 8)
            s.got(2, 3, 5)
            s.got(3, 3, 6)
        if i == 5:
            for ra in range(4):
                s.got(ra, 2, 11 + ra)
            for k in s.sent:
                k.wait_send()


class Weights:
    def __init__(s, p, mine, theirs, w, xs, ls, ss, rs):
        s.p, s.mine, s.theirs, s.w, s.xs, s.ls = p, mine, theirs, w, xs, ls
        s.oo, s.po = p.xh * 48, (1 - p.xh) * 48
        s.A = Half(p, w, s.oo, "y", "z", ss.at[0], rs.at[0])
        s.B = Half(p, w, s.po, "z", "y", ss.at[1], rs.at[1])

    def exchange(s):
        p = s.p
        dst = s.w.at[ds(p.sb * 96 + s.oo, 48)]
        s.xk = rcopy(s.theirs, dst, s.xs.at[0], s.xs.at[1], p.at_x(2))
        s.xk.start()
        k = pltpu.make_async_copy(s.mine, dst, s.ls)
        k.start()
        k.wait()

    def own(s):
        p = s.p
        s.A.own()
        got = s.w.at[ds(p.sb * 96 + s.po, 48)]
        rcopy(s.theirs, got, s.xs.at[0], s.xs.at[1], p.at_x(2)).wait_recv()
        s.B.own()

    def step(s, i):
        s.A.step(i)
        s.B.step(i)
        if i == 5:
            s.xk.wait_send()


class GatherX:
    def __init__(s, p, buf, ss, rs):
        s.p, s.buf, s.ss, s.rs, s.sent = p, buf, ss, rs, []

    def shard(s, d, c, lo=0, n=128):
        x = lax.rem(s.p.x + d, 4)
        return s.buf.at[ds((x * 2 + c) * 128 + lo, n)]

    def send(s, d, lo, n, dev, rid):
        u = s.shard(d, s.p.c, lo, n)
        k = rcopy(u, u, s.ss.at[len(s.sent)], s.rs.at[rid], dev)
        s.sent.append(k)
        k.start()

    def got(s, d, c, lo, n, rid):
        u = s.shard(d, c, lo, n)
        rcopy(u, u, s.ss.at[0], s.rs.at[rid], s.p.at_x(1)).wait_recv()

    def own(s):
        p = s.p
        s.send(0, 0, 128, p.at_x(1), 0)
        s.send(0, 0, 128, p.at_x(3), 1)
        s.send(0, 0, 128, p.sib, 4)

    def step(s, i):
        p = s.p
        o = 1 - p.c
        if i == 0:
            s.got(3, p.c, 0, 128, 0)
            s.send(3, 0, 64, p.at_x(1), 2)
            s.send(3, 0, 128, p.sib, 5)
            s.got(1, p.c, 0, 128, 1)
            s.send(1, 64, 64, p.at_x(3), 3)
            s.send(1, 0, 128, p.sib, 6)
        if i == 1:
            s.got(2, p.c, 0, 64, 2)
            s.send(2, 0, 64, p.sib, 7)
            s.got(2, p.c, 64, 64, 3)
            s.send(2, 64, 64, p.sib, 8)
        if i == 2:
            s.got(0, o, 0, 128, 4)
        if i == 3:
            s.got(3, o, 0, 128, 5)
        if i == 4:
            s.got(1, o, 0, 128, 6)
        if i == 5:
            s.got(2, o, 0, 64, 7)
            s.got(2, o, 64, 64, 8)
            for k in s.sent:
                k.wait_send()


class ReduceX:
    def __init__(s, p, buf, sib, half, full, ss, rs):
        s.p, s.buf, s.sib, s.half, s.full, s.ss, s.rs, s.sent = p, buf, sib, half, full, ss, rs, []

    def rows(s, d, c, lo=0, n=128):
        x = lax.rem(s.p.x + d, 4)
        return ds((x * 2 + c) * 128 + lo, n)

    def send(s, src, dst, rid, dev):
        k = rcopy(src, dst, s.ss.at[rid], s.rs.at[rid], dev)
        s.sent.append(k)
        k.start()

    def wait(s, dst, rid):
        rcopy(dst, dst, s.ss.at[rid], s.rs.at[rid], s.p.sib).wait_recv()

    def to_sib(s, d):
        s.send(s.buf.at[s.rows(d, 1 - s.p.c)], s.sib.at[d], d, s.p.sib)

    def add_sib(s, d):
        s.wait(s.sib.at[d], d)
        r = s.rows(d, s.p.c)
        s.buf[r] = (s.buf[r].astype(F32) + s.sib[d].astype(F32)).astype(BF)

    def far(s):
        s.add_sib(2)
        s.send(s.buf.at[s.rows(2, s.p.c, 0, 64)], s.half.at[0], 4, s.p.at_x(1))
        s.send(s.buf.at[s.rows(2, s.p.c, 64, 64)], s.half.at[1], 5, s.p.at_x(3))

    def near(s):
        s.add_sib(1)
        s.add_sib(3)
        s.wait(s.half.at[0], 4)
        r = s.rows(1, s.p.c, 0, 64)
        s.buf[r] = (s.buf[r].astype(F32) + s.half[0].astype(F32)).astype(BF)
        s.send(s.buf.at[s.rows(1, s.p.c)], s.full.at[0], 6, s.p.at_x(1))
        s.wait(s.half.at[1], 5)
        r = s.rows(3, s.p.c, 64, 64)
        s.buf[r] = (s.buf[r].astype(F32) + s.half[1].astype(F32)).astype(BF)
        s.send(s.buf.at[s.rows(3, s.p.c)], s.full.at[1], 7, s.p.at_x(3))

    def final(s):
        s.wait(s.sib.at[0], 0)
        s.wait(s.full.at[0], 6)
        s.wait(s.full.at[1], 7)
        for k in s.sent:
            k.wait_send()
        r = s.rows(0, s.p.c)
        return (s.buf[r].astype(F32) + s.sib[0].astype(F32)) + (
            s.full[0].astype(F32) + s.full[1].astype(F32)
        )


class ReduceHalf:
    def __init__(s, p, g, off, a, b, rbuf, ss, rs):
        s.p, s.g, s.off, s.a, s.b, s.r, s.ss, s.rs = p, g, off, a, b, rbuf, ss, rs
        s.sent = []

    def rows(s, ra, rb):
        ia = lax.rem(getattr(s.p, s.a) + ra, 4)
        ib = lax.rem(getattr(s.p, s.b) + rb, 4)
        zz, yy = (ia, ib) if s.a == "z" else (ib, ia)
        return ds((zz * 4 + yy) * 96 + s.off, 48)

    def send(s, ra, rb, axis, d, rid):
        k = rcopy(s.g.at[s.rows(ra, rb)], s.r.at[rid], s.ss.at[len(s.sent)], s.rs.at[rid], s.p.at(axis, d))
        s.sent.append(k)
        k.start()

    def add(s, ra, rb, *rids):
        for i in rids:
            rcopy(s.r.at[i], s.r.at[i], s.ss.at[0], s.rs.at[i], s.p.at(s.a, 1)).wait_recv()
        r = s.rows(ra, rb)
        v = s.g[r].astype(F32)
        for i in rids:
            v = v + s.r[i].astype(F32)
        s.g[r] = v.astype(BF)

    def step(s, i):
        a, b = s.a, s.b
        if i == 0:
            for ra in (0, 1):
                s.send(ra, 2, b, 1, 11 + ra)
            for ra in (2, 3):
                s.send(ra, 2, b, 3, 11 + ra)
            for ra in (2, 3):
                s.send(ra, 1, b, 1, 3 + ra)
            for ra in (0, 1):
                s.send(ra, 3, b, 3, 7 + ra)
        if i == 1:
            for ra in (0, 1):
                s.add(ra, 1, 11 + ra)
                s.send(ra, 1, b, 1, 3 + ra)
            for ra in (2, 3):
                s.add(ra, 3, 11 + ra)
                s.send(ra, 3, b, 3, 7 + ra)
        if i == 2:
            s.add(2, 0, 5, 9)
            s.send(2, 0, a, 1, 2)
            s.add(3, 0, 6, 10)
            s.send(3, 0, a, 3, 1)
        if i == 3:
            s.add(1, 0, 4, 8, 2)
            s.send(1, 0, a, 1, 0)
        if i == 4:
            s.add(0, 0, 3, 7, 0, 1)
            for k in s.sent:
                k.wait_send()


class ReduceW:
    def __init__(s, p, g, rbuf, mine, other, xbuf, xs, ss, rs):
        s.p, s.g, s.mine, s.other, s.xbuf, s.xs = p, g, mine, other, xbuf, xs
        s.oo, s.po = p.xh * 48, (1 - p.xh) * 48
        s.A = ReduceHalf(p, g, s.oo, "y", "z", rbuf.at[0], ss.at[0], rs.at[0])
        s.B = ReduceHalf(p, g, s.po, "z", "y", rbuf.at[1], ss.at[1], rs.at[1])

    def step(s, i):
        p = s.p
        if i < 5:
            s.B.step(i)
        if i == 4:
            src = s.g.at[ds(p.sb * 96 + s.po, 48)]
            s.xk = rcopy(src, s.xbuf, s.xs.at[0], s.xs.at[1], p.at_x(2))
            s.xk.start()
        if i < 5:
            s.A.step(i)
        if i == 4:
            s.mine[...] = s.g[ds(p.sb * 96 + s.oo, 48)]
        if i == 5:
            s.xk.wait_recv()
            s.xk.wait_send()
            s.other[...] = s.xbuf[...]


def lanes(shape):
    return lax.broadcasted_iota(jnp.int32, shape, len(shape) - 1)


def swap(v):
    n = v.shape[1]
    low = lax.rem(lanes(v.shape), 64) < 32
    return jnp.where(low, pltpu.roll(v, n - 32, 1), pltpu.roll(v, 32, 1))


def head_mean(v):
    n = v.shape[1]
    a = lax.broadcasted_iota(jnp.int32, (n, n), 0) // 64
    b = lax.broadcasted_iota(jnp.int32, (n, n), 1) // 64
    m = jnp.where(a == b, 1.0 / 64, 0.0).astype(F32)
    return mm(v, m, NN, HI)


def rms_inv(v):
    return lax.rsqrt(jnp.mean(v * v, axis=-1, keepdims=True) + EPS)


def loop(n, body):
    lax.fori_loop(0, n, lambda i, c: (body(i), c)[1], 0)


def tile(t, n=TILE):
    return pl.ds(pl.multiple_of(t * n, n), n)


def kernel(
    tokens, segf, attn_gain, ffn_gain, gqk, wa_mine, wa_theirs, wf_mine, wf_theirs, out_grad, ctab, stab,
    result, grad_tokens, ga_mine, ga_other, gf_mine, gf_other, gains,
    wa, wf, bo, og, b2, mr, hid, dg, du, fr, ar, fx, axb,
    pa, psib, phalf, pfull,
    q, do, kvw, kvt, acc, dkv, dks, dkr, att, attf, qkraw, mid, dmid,
    segx, segw, stq, lse, dlt, gbuf, gx, gy, gz,
    wsx, wsl, was, war, wfs, wfr, gxs, gxr, rxs, rxr, ras, rar, rfs, rfr, kvs, kvr, sgs, sgr, gns, gnr, free,
):
    p = Pos()
    shard = p.x * 2 + p.c
    ga, dall = wa, dg
    own_rows = ds(shard * 128, 128)
    barrier(p)

    WA = Weights(p, wa_mine, wa_theirs, wa, wsx.at[0], wsl.at[0], was, war)
    WF = Weights(p, wf_mine, wf_theirs, wf, wsx.at[1], wsl.at[1], wfs, wfr)
    WA.exchange()
    tf = tokens[...].astype(F32)
    bo[own_rows] = (tf * rms_inv(tf) * attn_gain[...]).astype(BF)
    GB = GatherX(p, bo, gxs.at[0], gxr.at[0])
    GB.own()
    segx[pl.ds(pl.multiple_of(shard * 8, 8), 8)] = segf[...]
    seg_sent = []
    here = segx.at[pl.ds(pl.multiple_of(shard * 8, 8), 8)]
    peers = [(d, cc) for d in range(4) for cc in range(2) if (d, cc) != (0, 0)]
    for i, (d, cc) in enumerate(peers):
        k = rcopy(here, here, sgs.at[i], sgr.at[i], p.at_x(d, p.c if cc == 0 else 1 - p.c))
        k.start()
        seg_sent.append(k)
    WA.own()
    WF.exchange()
    for i, (d, cc) in enumerate(peers):
        x = lax.rem(p.x + 4 - d, 4)
        c = p.c if cc == 0 else 1 - p.c
        there = segx.at[pl.ds(pl.multiple_of((x * 2 + c) * 8, 8), 8)]
        rcopy(there, there, sgs.at[i], sgr.at[i], p.sib).wait_recv()
    for g in range(8):
        segw[pl.ds(16 + g, 1)] = segx[pl.ds(8 * g, 1)]
    for j in (1, 2):
        k = rcopy(segw.at[pl.ds(16, 8)], segw.at[pl.ds(16 - 8 * j, 8)], sgs.at[6 + j], sgr.at[6 + j], p.at_sb(j))
        k.start()
        seg_sent.append(k)
    og[own_rows] = out_grad[...]
    GB.step(0)
    WA.step(0)
    WA.step(1)
    GB.step(1)
    WA.step(2)
    GO = GatherX(p, og, gxs.at[1], gxr.at[1])
    WA.step(3)
    WF.own()
    for i in (2, 3, 4, 5):
        GB.step(i)
    WA.step(4)
    WA.step(5)
    GO.own()

    for j in (1, 2):
        there = segw.at[pl.ds(16 - 8 * j, 8)]
        rcopy(there, there, sgs.at[6 + j], sgr.at[6 + j], p.sib).wait_recv()
    for k in seg_sent:
        k.wait_send()
    sq = segw[pl.ds(16, 8)]
    s1 = jnp.where(p.sb >= 1, segw[pl.ds(8, 8)], -1.0)
    s2 = jnp.where(p.sb >= 2, segw[pl.ds(0, 8)], -1.0)
    start = jnp.zeros((8, 128), F32)
    for d in range(16):
        fewer = (sq < d).astype(F32) + (s1 < d).astype(F32) + (s2 < d).astype(F32)
        count = jnp.sum(jnp.sum(fewer, axis=1, keepdims=True), axis=0, keepdims=True)
        start = start + jnp.where(sq == d, count, 0.0)
    start = start.astype(jnp.int32)
    for t in range(4):
        for h in range(3):
            for j in range(2):
                stq[pl.ds(t, 1), pl.ds(h * 256 + j * 128, 128)] = start[2 * t + j : 2 * t + j + 1]

    def project(t):
        x = bo[tile(t)]
        qk = mm(x, wa[:, 0:256], NN)
        ov = mm(x, wa[:, 256:512], NN)
        qkraw[tile(t)] = qk
        n = qk * lax.rsqrt(head_mean(qk * qk) + EPS) * gqk[...]
        c1, s1 = ctab[tile(t)], stab[tile(t)]
        c2, s2 = jnp.concatenate([c1, c1], 1), jnp.concatenate([s1, s1], 1)
        r = n * c2 + swap(n) * s2
        a0, a1 = r[:, :128], r[:, 128:]
        low = lanes((TILE, 128)) < 64
        q[0, tile(t)] = jnp.where(low, a0, 0.0).astype(BF)
        q[1, tile(t)] = jnp.where(low, pltpu.roll(a0, 64, 1), 0.0).astype(BF)
        q[2, tile(t)] = jnp.where(low, a1, 0.0).astype(BF)
        kv = jnp.where(low, pltpu.roll(a1, 64, 1), ov[:, 128:])
        kvw[ds(2048 + t * 256, 256)] = kv.astype(BF)
        kvt[8 + t] = kv.T.astype(BF)

    loop(4, project)
    kv_own = kvw.at[pl.ds(2048, 1024)]
    kv_sent = []
    for j in (1, 2):
        k = rcopy(kv_own, kvw.at[pl.ds(2048 - 1024 * j, 1024)], kvs.at[j - 1], kvr.at[j - 1], p.at_sb(j))
        k.start()
        kv_sent.append(k)

    def kv_wait(j):
        there = kvw.at[pl.ds(2048 - 1024 * j, 1024)]
        rcopy(there, there, kvs.at[j - 1], kvr.at[j - 1], p.sib).wait_recv()

        def turn(t):
            u = 8 - 4 * j + t
            kvt[u] = kvw[tile(u)].astype(F32).T.astype(BF)

        loop(4, turn)

    key_at = lax.broadcasted_iota(jnp.int32, (TILE, 3 * TILE), 0)
    scale = 0.125

    def mask_of(t, u, diag):
        ok = key_at >= stq[pl.ds(t, 1)] - u * TILE
        if diag:
            ok = ok & (key_at <= lax.rem(lanes((TILE, 3 * TILE)), TILE))
        return ok

    def forward(t, u, diag):
        k = kvw[tile(u)]
        q3 = q[:, tile(t)].reshape(3 * TILE, 128)
        s = mm(k, q3, NT)
        e = jnp.where(mask_of(t, u, diag), jnp.exp2(s * (scale * LOG2E)), 0.0).astype(BF)
        va = jnp.where(lax.broadcasted_iota(jnp.int32, (128, TILE), 0) < 64, 1.0, kvt[u].astype(F32)).astype(BF)
        new = mm(va, e, NN)
        if diag:
            acc[t] = new
        else:
            acc[t] = acc[t] + new

    loop(4, lambda t: forward(t, t + 8, True))
    GO.step(0)
    WF.step(0)
    loop(3, lambda i: lax.fori_loop(0, i + 1, lambda j, c: (forward(i + 1, 8 + j, False), c)[1], 0))
    GO.step(1)
    kv_wait(1)
    WF.step(1)
    loop(4, lambda t: forward(t, 7, False))
    loop(4, lambda t: forward(t, 6, False))
    WF.step(2)
    loop(4, lambda t: forward(t, 5, False))
    loop(4, lambda t: forward(t, 4, False))
    for i in (2, 3, 4, 5):
        GO.step(i)
    kv_wait(2)
    WF.step(3)
    loop(4, lambda i: lax.fori_loop(0, i + 1, lambda t, c: (forward(t, i, False), c)[1], 0))
    for k in kv_sent:
        k.wait_send()

    def attended(t):
        a = acc[t]
        o = a[64:128] / a[0:64]
        lse[pl.ds(t, 1)] = jnp.log2(a[0:1])
        ot = jnp.concatenate([o[:, 0:256], o[:, 256:512], o[:, 512:768], jnp.zeros((64, 256), F32)], axis=0)
        o2 = ot.T
        attf[tile(t)] = o2
        att[tile(t)] = o2.astype(BF)

    loop(4, attended)

    R1 = ReduceX(p, pa, psib, phalf, pfull, rxs.at[0], rxr.at[0])
    for d in (2, 1, 3, 0):
        x = lax.rem(p.x + d, 4)
        for j in range(3):
            n = pl.ds(j * 512, 512)
            pa[tile(x), n] = mm(att[tile(x)], wa[n, 256:512], NT).astype(BF)
        R1.to_sib(d)
        if d == 1:
            R1.far()
    R1.near()
    WF.step(4)
    m = tokens[...].astype(F32) + R1.final()
    mid[...] = m
    b2[own_rows] = (m * rms_inv(m) * ffn_gain[...]).astype(BF)
    G2 = GatherX(p, b2, gxs.at[2], gxr.at[2])
    G2.own()
    WF.step(5)

    def ffn(d):
        r = tile(lax.rem(p.x + d, 4))
        for lo, n in ((0, 512), (512, HP - 512)):
            gate = mm(b2[r], wf[:, lo : lo + n], NN)
            up = mm(b2[r], wf[:, HP + lo : HP + lo + n], NN)
            dh = mm(og[r], wf[:, 2 * HP + lo : 2 * HP + lo + n], NN)
            sig = jax.nn.sigmoid(gate)
            swish = gate * sig
            hid[r, lo : lo + n] = (swish * up).astype(BF)
            dg[r, lo : lo + n] = (dh * up * sig * (1.0 + gate * (1.0 - sig))).astype(BF)
            du[r, lo : lo + n] = (dh * swish).astype(BF)

    G2.step(2)
    ffn(0)
    G2.step(0)
    G2.step(3)
    ffn(3)
    G2.step(1)
    G2.step(4)
    ffn(1)
    G2.step(5)
    ffn(2)

    R2 = ReduceX(p, pa, psib, phalf, pfull, rxs.at[1], rxr.at[1])
    R3 = ReduceX(p, pa, psib, phalf, pfull, rxs.at[2], rxr.at[2])

    def back_in(d):
        r = tile(lax.rem(p.x + d, 4))
        for j in range(3):
            n = pl.ds(j * 512, 512)
            v = mm(dg[r], wf[n, 0:HP], NT) + mm(du[r], wf[n, HP : 2 * HP], NT)
            pa[r, n] = v.astype(BF)
        R2.to_sib(d)

    def branch(d):
        r = tile(lax.rem(p.x + d, 4))
        for j in range(3):
            n = pl.ds(j * 512, 512)
            pa[r, n] = mm(hid[r], wf[n, 2 * HP :], NT).astype(BF)
        R3.to_sib(d)

    back_in(2)
    back_in(1)
    R2.far()
    back_in(3)
    back_in(0)
    R2.near()

    dn = R2.final()
    m = mid[...]
    r = rms_inv(m)
    n = m * r
    e = dn * ffn_gain[...]
    dm = out_grad[...].astype(F32) + r * (e - n * jnp.mean(e * n, axis=-1, keepdims=True))
    dmid[...] = dm
    gbuf[...] = jnp.zeros_like(gbuf)
    gbuf[pl.ds(1, 1)] = jnp.sum(dn * n, axis=0, keepdims=True)
    mr[own_rows] = dm.astype(BF)
    G3 = GatherX(p, mr, gxs.at[3], gxr.at[3])
    G3.own()

    def grads(cols, left, right):
        def body(i):
            c = pl.ds(pl.multiple_of(i * 256, 256), 256)
            wf[tile(i), cols] = mm(left[:, c], right[...], TN).astype(BF)

        loop(6, body)

    grads(pl.ds(0, HP), b2, dg)
    G3.step(0)
    grads(pl.ds(HP, HP), b2, du)
    G3.step(1)
    G3.step(2)
    branch(2)
    branch(1)
    R3.far()
    branch(3)
    branch(0)
    grads(pl.ds(2 * HP, HP), og, hid)
    RF = ReduceW(p, wf, fr, gf_mine, gf_other, fx, wsx.at[2], rfs, rfr)
    RF.step(0)
    for i in (3, 4, 5):
        G3.step(i)
    R3.near()

    head_row = lax.broadcasted_iota(jnp.int32, (8, 256), 0)
    head_lane = lanes((8, 256)) // 64
    per_head = jnp.where(head_row == head_lane, 1.0, 0.0).astype(F32)

    def d_attended(t):
        d = mm(mr[tile(t)], wa[:, 256:512], NN).astype(BF).astype(F32)
        sums = mm(per_head, d * attf[tile(t)], NT, HI)
        for h in range(3):
            dlt[pl.ds(t, 1), pl.ds(h * 256, 256)] = sums[h : h + 1]
        a0, a1 = d[:, :128], d[:, 128:]
        high = lanes((TILE, 128)) >= 64
        do[0, tile(t)] = jnp.where(high, pltpu.roll(a0, 64, 1), 0.0).astype(BF)
        do[1, tile(t)] = jnp.where(high, a0, 0.0).astype(BF)
        do[2, tile(t)] = jnp.where(high, pltpu.roll(a1, 64, 1), 0.0).astype(BF)
        acc[t] = jnp.zeros((128, 768), F32)

    loop(4, d_attended)
    result[...] = (mid[...] + R3.final()).astype(BF)
    for dev in (p.sib, p.at_x(1), p.at_x(3)):
        pl.semaphore_signal(free, inc=1, device_id=dev, device_id_type=MESH)
    dkv[...] = jnp.zeros_like(dkv)

    def backward(t, u, diag):
        k = kvw[tile(u)]
        q3 = q[:, tile(t)].reshape(3 * TILE, 128)
        do3 = do[:, tile(t)].reshape(3 * TILE, 128)
        s = mm(k, q3, NT)
        pr = jnp.where(mask_of(t, u, diag), jnp.exp2(s * (scale * LOG2E) - lse[pl.ds(t, 1)]), 0.0)
        dp = mm(k, do3, NT)
        dsc = (pr * (dp - dlt[pl.ds(t, 1)])).astype(BF)
        dkv[u] = dkv[u] + mm(dsc, q3, NN) + mm(pr.astype(BF), do3, NN)
        acc[t] = acc[t] + mm(kvt[u], dsc, NN)

    def scaled(v):
        return jnp.where(lanes(v.shape) < 64, v * scale, v)

    dk_sent = []

    def dk_send(j):
        def body(t):
            dks[j - 1, tile(t)] = scaled(dkv[8 - 4 * j + t]).astype(BF)

        loop(4, body)
        k = rcopy(dks.at[j - 1], dkr.at[j - 1], kvs.at[1 + j], kvr.at[1 + j], p.at_sb(-j))
        k.start()
        dk_sent.append(k)

    loop(4, lambda i: lax.fori_loop(0, i + 1, lambda t, c: (backward(t, i, False), c)[1], 0))
    dk_send(2)
    RF.step(1)
    loop(4, lambda t: backward(t, 4, False))
    loop(4, lambda t: backward(t, 5, False))
    RF.step(2)
    loop(4, lambda t: backward(t, 6, False))
    loop(4, lambda t: backward(t, 7, False))
    dk_send(1)
    RF.step(3)
    loop(3, lambda i: lax.fori_loop(0, i + 1, lambda j, c: (backward(i + 1, 8 + j, False), c)[1], 0))
    RF.step(4)
    loop(4, lambda t: backward(t, t + 8, True))
    for j in (1, 2):
        rcopy(dkr.at[j - 1], dkr.at[j - 1], kvs.at[1 + j], kvr.at[1 + j], p.sib).wait_recv()
    for k in dk_sent:
        k.wait_send()

    def unproject(t):
        a = acc[t][0:64]
        at = jnp.concatenate([a[:, 0:256], a[:, 256:512], a[:, 512:768], jnp.zeros((64, 256), F32)], axis=0)
        dq = at.T * scale
        dk = scaled(dkv[8 + t]) + dkr[0, tile(t)].astype(F32) + dkr[1, tile(t)].astype(F32)
        low = lanes((TILE, 128)) < 64
        d = jnp.concatenate([dq[:, :128], jnp.where(low, dq[:, 128:], pltpu.roll(dk, 64, 1))], 1)
        d = d.astype(BF).astype(F32)
        c1, s1 = ctab[tile(t)], stab[tile(t)]
        c2, s2 = jnp.concatenate([c1, c1], 1), jnp.concatenate([s1, s1], 1)
        dn = d * c2 + swap(d * s2)
        raw = qkraw[tile(t)]
        r = lax.rsqrt(head_mean(raw * raw) + EPS)
        n = raw * r
        e = dn * gqk[...]
        dx = r * (e - n * head_mean(e * n))
        gbuf[pl.ds(2, 1), pl.ds(0, 256)] = gbuf[pl.ds(2, 1), pl.ds(0, 256)] + jnp.sum(dn * n, axis=0, keepdims=True)
        dall[tile(t), 0:256] = dx.astype(BF)
        dall[tile(t), 256:384] = jnp.zeros((TILE, 128), BF)
        dall[tile(t), 384:512] = jnp.where(low, 0.0, dk).astype(BF)

    loop(4, unproject)

    pl.semaphore_wait(free, 3)
    R4 = ReduceX(p, pa, psib, phalf, pfull, rxs.at[3], rxr.at[3])
    for d in (2, 1, 3, 0):
        x = lax.rem(p.x + d, 4)
        for j in range(3):
            n = pl.ds(j * 512, 512)
            pa[tile(x), n] = mm(dall[tile(x), 0:512], wa[n, :], NT).astype(BF)
        R4.to_sib(d)
        if d == 1:
            R4.far()

    def attn_grads(i):
        c = pl.ds(pl.multiple_of(i * 256, 256), 256)
        ga[tile(i), 0:256] = mm(bo[:, c], dall[:, 0:256], TN).astype(BF)
        ga[tile(i), 256:512] = (mm(bo[:, c], dall[:, 256:512], TN) + mm(mr[:, c], att[...], TN)).astype(BF)

    loop(6, attn_grads)
    RA = ReduceW(p, ga, ar, ga_mine, ga_other, axb, wsx.at[3], ras, rar)
    RA.step(0)
    R4.near()
    RF.step(5)
    RA.step(1)
    dn = R4.final()
    t = tokens[...].astype(F32)
    r = rms_inv(t)
    n = t * r
    e = dn * attn_gain[...]
    grad_tokens[...] = (dmid[...] + r * (e - n * jnp.mean(e * n, axis=-1, keepdims=True))).astype(BF)
    gbuf[pl.ds(0, 1)] = jnp.sum(dn * n, axis=0, keepdims=True)
    RA.step(2)

    sent = []
    gx[shard] = gbuf[...]
    for i, (d, cc) in enumerate(peers):
        k = rcopy(gbuf, gx.at[shard], gns.at[i], gnr.at[i], p.at_x(d, p.c if cc == 0 else 1 - p.c))
        k.start()
        sent.append(k)
    RA.step(3)
    for i in range(7):
        rcopy(gx.at[i], gx.at[i], gns.at[i], gnr.at[i], p.sib).wait_recv()
    v = gx[0]
    for i in range(1, 8):
        v = v + gx[i]
    gy[p.y] = v
    for d in (1, 2, 3):
        k = rcopy(gy.at[p.y], gy.at[p.y], gns.at[6 + d], gnr.at[6 + d], p.at("y", d))
        k.start()
        sent.append(k)
    RA.step(4)
    for d in (1, 2, 3):
        rcopy(gy.at[0], gy.at[0], gns.at[6 + d], gnr.at[6 + d], p.sib).wait_recv()
    v = (gy[0] + gy[1]) + (gy[2] + gy[3])
    gz[p.z] = v
    for d in (1, 2, 3):
        k = rcopy(gz.at[p.z], gz.at[p.z], gns.at[9 + d], gnr.at[9 + d], p.at("z", d))
        k.start()
        sent.append(k)
    RA.step(5)
    for d in (1, 2, 3):
        rcopy(gz.at[0], gz.at[0], gns.at[9 + d], gnr.at[9 + d], p.sib).wait_recv()
    gains[...] = (gz[0] + gz[1]) + (gz[2] + gz[3])
    for k in sent:
        k.wait_send()


def call_kernel(*args):
    vm = pl.BlockSpec(memory_space=pltpu.VMEM)
    S = jax.ShapeDtypeStruct
    V = pltpu.VMEM
    dma = pltpu.SemaphoreType.DMA
    outs = (
        S((128, D), BF), S((128, D), BF), S((48, CA), BF), S((48, CA), BF),
        S((48, CF), BF), S((48, CF), BF), S((8, D), F32),
    )
    scratch = [
        V((D, CA), BF), V((D, CF), BF), V((ROWS, D), BF), V((ROWS, D), BF), V((ROWS, D), BF), V((ROWS, D), BF),
        V((ROWS, HP), BF), V((ROWS, HP), BF), V((ROWS, HP), BF),
        V((2, 15, 48, CF), BF), V((2, 15, 48, CA), BF), V((48, CF), BF), V((48, CA), BF),
        V((ROWS, D), BF), V((4, 128, D), BF), V((2, 64, D), BF), V((2, 128, D), BF),
        V((3, ROWS, 128), BF), V((3, ROWS, 128), BF), V((3 * ROWS, 128), BF), V((12, 128, TILE), BF),
        V((4, 128, 768), F32), V((12, TILE, 128), F32), V((2, ROWS, 128), BF), V((2, ROWS, 128), BF),
        V((ROWS, 256), BF), V((ROWS, 256), F32), V((ROWS, 256), F32),
        V((128, D), F32), V((128, D), F32),
        V((64, 128), F32), V((24, 128), F32), V((8, 768), jnp.int32), V((8, 768), F32), V((8, 768), F32),
        V((8, D), F32), V((8, 8, D), F32), V((4, 8, D), F32), V((4, 8, D), F32),
        dma((4, 2)), dma((2,)), dma((2, 15)), dma((2, 15)), dma((2, 15)), dma((2, 15)),
        dma((4, 9)), dma((4, 9)), dma((4, 8)), dma((4, 8)),
        dma((2, 15)), dma((2, 15)), dma((2, 15)), dma((2, 15)),
        dma((4,)), dma((4,)), dma((9,)), dma((9,)), dma((13,)), dma((13,)), pltpu.SemaphoreType.REGULAR,
    ]
    return pl.pallas_call(
        kernel,
        out_shape=outs,
        in_specs=[vm] * 5 + [pl.BlockSpec(memory_space=pl.ANY)] * 4 + [vm] * 3,
        out_specs=(vm,) * len(outs),
        scratch_shapes=scratch,
        compiler_params=pltpu.CompilerParams(
            collective_id=0, has_side_effects=True, vmem_limit_bytes=VMEM_LIMIT
        ),
    )(*args)


VMEM_LIMIT = 63 * 2**20


def on_device(
    tokens, segments, attn_gain, w_query, w_key, w_value, query_gain, key_gain, w_out, ffn_gain,
    w_gate, w_up, w_down, out_grad,
):
    xh = lax.axis_index("xh")
    sb = lax.axis_index("z") * 4 + lax.axis_index("y")

    wo, wd = w_out.T, w_down.T

    def attn_half(i):
        cut = lambda w, n: w[:, i * n : (i + 1) * n]
        return jnp.concatenate([cut(w_query, 192), cut(w_key, 64), cut(wo, 192), cut(w_value, 64)], axis=1)

    def ffn_half(i):
        cut = lambda w: jnp.pad(w[:, i * HID : (i + 1) * HID], ((0, 0), (0, HP - HID)))
        return jnp.concatenate([cut(w_gate), cut(w_up), cut(wd)], axis=1)

    def sides(of):
        a, b = of(0), of(1)
        return jnp.where(xh == 0, a, b), jnp.where(xh == 0, b, a)

    wa_mine, wa_theirs = sides(attn_half)
    wf_mine, wf_theirs = sides(ffn_half)
    steps = jnp.arange(32, dtype=F32) * (2.0 / 64)
    freqs = jnp.exp(-jnp.log(THETA) * steps)
    positions = (sb * ROWS + jnp.arange(ROWS, dtype=jnp.int32)).astype(F32)
    angles = positions[:, None] * freqs[None, :]
    cos, sin = jnp.cos(angles), jnp.sin(angles)
    ctab = jnp.concatenate([cos] * 4, axis=1)
    stab = jnp.concatenate([-sin, sin, -sin, sin], axis=1)
    gqk = jnp.concatenate([query_gain] * 3 + [key_gain])[None, :]
    segf = jnp.broadcast_to(segments.astype(F32)[None, :], (8, 128))

    result, grad_tokens, gam, gao, gfm, gfo, gains = call_kernel(
        tokens, segf, attn_gain[None], ffn_gain[None], gqk, wa_mine, wa_theirs, wf_mine, wf_theirs, out_grad, ctab, stab,
    )

    def both(mine, other):
        both = [jnp.where(xh == 0, mine, other), jnp.where(xh == 0, other, mine)]
        return jnp.concatenate(both, axis=1).astype(F32)

    ga = lambda lo, n: both(gam[:, lo : lo + n], gao[:, lo : lo + n])
    gf = lambda i: both(gfm[:, i * HP : i * HP + HID], gfo[:, i * HP : i * HP + HID])
    qg = gains[2, 0:64] + gains[2, 64:128] + gains[2, 128:192]
    return (
        result, grad_tokens, gains[0], ga(0, 192), ga(192, 64), ga(448, 64), qg, gains[2, 192:256],
        ga(256, 192).T, gains[1], gf(0), gf(1), gf(2).T,
    )


def solution(mesh):
    finer = Mesh(mesh.devices.reshape(4, 4, 2, 2, 2), AXES)
    rows, blk, narrow = P(AXES), ("z", "y", "xh"), ("xl", "core")
    cols, turned = P(blk, narrow), P(narrow, blk)
    in_specs = (rows, rows, P(), cols, cols, cols, P(), P(), turned, P(), cols, cols, turned, rows)
    out_specs = (rows, rows, P(), cols, cols, cols, P(), P(), turned, P(), cols, cols, turned)
    return jax.shard_map(
        on_device, mesh=finer, in_specs=in_specs, out_specs=out_specs, check_vma=False
    )
```

```python
from functools import partial

import jax
import jax.numpy as jnp
import numpy as np
from jax import lax
from jax.experimental import pallas as pl
from jax.experimental.pallas import tpu as pltpu
from jax.sharding import Mesh
from jax.sharding import PartitionSpec as P

EPS = 1e-05
THETA = 1000000.0
LOG2E = 1.4426950408889634
MESH = pl.DeviceIdType.MESH
BF = jnp.bfloat16
F32 = jnp.float32
HI = lax.Precision.HIGHEST
AXES = ("z", "y", "xh", "xl", "core")

D = 1536
HP = 896
HQ = 832
CF = 3 * HP
CA = 512
ROWS = 1024
TILE = 256
NT = ((1,), (1,)), ((), ())
NN = ((1,), (0,)), ((), ())
TN = ((0,), (0,)), ((), ())


def mm(a, b, dims, precision=None):
    return lax.dot_general(a, b, dims, precision=precision, preferred_element_type=F32)


class Pos:
    def __init__(s):
        ax = lax.axis_index
        s.z, s.y, s.xh, s.xl, s.c = ax("z"), ax("y"), ax("xh"), ax("xl"), ax("core")
        s.x = s.xh * 2 + s.xl
        s.sb = s.z * 4 + s.y
        s.sib = s.at_x(0, 1 - s.c)

    def at_x(s, d, c=None):
        x = lax.rem(s.x + d, 4)
        return {"xh": x // 2, "xl": lax.rem(x, 2), "core": s.c if c is None else c}

    def at(s, axis, d):
        return {axis: lax.rem(getattr(s, axis) + d, 4)}

    def at_sb(s, d):
        t = lax.rem(s.sb + d + 16, 16)
        return {"z": t // 4, "y": lax.rem(t, 4)}


def barrier(p):
    b = pltpu.get_barrier_semaphore()
    peers = [p.at("y", 1), p.at("y", 2), p.at("y", 3), p.at("z", 1), p.at("z", 2), p.at("z", 3)]
    peers += [p.at_sb(d) for d in (1, 2, -1, -2)]
    peers += [p.at_x(d, cc) for d in (1, 2, 3) for cc in (p.c, 1 - p.c)] + [p.sib]
    for q in peers:
        pl.semaphore_signal(b, inc=1, device_id=q, device_id_type=MESH)
    pl.semaphore_wait(b, len(peers))


def rcopy(src, dst, ss, rs, dev):
    return pltpu.make_async_remote_copy(
        src_ref=src, dst_ref=dst, send_sem=ss, recv_sem=rs, device_id=dev, device_id_type=MESH
    )


def ds(start, n):
    return pl.ds(pl.multiple_of(start, 16), n)


class Half:
    def __init__(s, p, w, off, a, b, ss, rs):
        s.p, s.w, s.off, s.a, s.b, s.ss, s.rs = p, w, off, a, b, ss, rs
        s.sent = []

    def unit(s, ra, rb):
        ia = lax.rem(getattr(s.p, s.a) + ra, 4)
        ib = lax.rem(getattr(s.p, s.b) + rb, 4)
        zz, yy = (ia, ib) if s.a == "z" else (ib, ia)
        return s.w.at[ds((zz * 4 + yy) * 96 + s.off, 48)]

    def send(s, ra, rb, axis, d, rid):
        u = s.unit(ra, rb)
        k = rcopy(u, u, s.ss.at[len(s.sent)], s.rs.at[rid], s.p.at(axis, d))
        s.sent.append(k)
        k.start()

    def got(s, ra, rb, rid):
        u = s.unit(ra, rb)
        rcopy(u, u, s.ss.at[0], s.rs.at[rid], s.p.at(s.a, 1)).wait_recv()

    def own(s):
        s.send(0, 0, s.a, 1, 0)
        s.send(0, 0, s.a, 3, 1)
        s.send(0, 0, s.b, 1, 3)
        s.send(0, 0, s.b, 3, 7)

    def step(s, i):
        if i == 0:
            s.got(3, 0, 0)
            s.send(3, 0, s.a, 1, 2)
            s.send(3, 0, s.b, 1, 6)
            s.send(3, 0, s.b, 3, 10)
            s.got(1, 0, 1)
            s.send(1, 0, s.b, 1, 4)
            s.send(1, 0, s.b, 3, 8)
        if i == 1:
            s.got(0, 3, 3)
            s.send(0, 3, s.b, 1, 11)
            s.got(2, 0, 2)
            s.send(2, 0, s.b, 1, 5)
            s.send(2, 0, s.b, 3, 9)
        if i == 2:
            s.got(3, 1, 10)
            s.send(3, 1, s.b, 3, 14)
            s.got(1, 3, 4)
            s.send(1, 3, s.b, 1, 12)
        if i == 3:
            s.got(2, 1, 9)
            s.send(2, 1, s.b, 3, 13)
        if i == 4:
            s.got(0, 1, 7)
            s.got(1, 1, 8)
            s.got(2, 3, 5)
            s.got(3, 3, 6)
        if i == 5:
            for ra in range(4):
                s.got(ra, 2, 11 + ra)
            for k in s.sent:
                k.wait_send()


class Weights:
    def __init__(s, p, theirs, w, xs, ss, rs):
        s.p, s.theirs, s.w, s.xs = p, theirs, w, xs
        s.oo, s.po = p.xh * 48, (1 - p.xh) * 48
        s.A = Half(p, w, s.oo, "y", "z", ss.at[0], rs.at[0])
        s.B = Half(p, w, s.po, "z", "y", ss.at[1], rs.at[1])

    def exchange(s):
        p = s.p
        dst = s.w.at[ds(p.sb * 96 + s.oo, 48)]
        s.xk = rcopy(s.theirs, dst, s.xs.at[0], s.xs.at[1], p.at_x(2))
        s.xk.start()

    def own(s):
        p = s.p
        s.A.own()
        got = s.w.at[ds(p.sb * 96 + s.po, 48)]
        rcopy(s.theirs, got, s.xs.at[0], s.xs.at[1], p.at_x(2)).wait_recv()
        s.B.own()

    def step(s, i):
        s.A.step(i)
        s.B.step(i)
        if i == 5:
            s.xk.wait_send()


class GatherX:
    def __init__(s, p, buf, ss, rs):
        s.p, s.buf, s.ss, s.rs, s.sent = p, buf, ss, rs, []

    def piece(s, d, c, i):
        x = lax.rem(s.p.x + d, 4)
        return s.buf.at[ds((x * 2 + c) * 128 + i * 64, 64)]

    def send(s, d, i, dev, rid):
        u = s.piece(d, s.p.c, i)
        k = rcopy(u, u, s.ss.at[len(s.sent)], s.rs.at[rid], dev)
        s.sent.append(k)
        k.start()

    def got(s, d, c, i, rid):
        u = s.piece(d, c, i)
        rcopy(u, u, s.ss.at[0], s.rs.at[rid], s.p.sib).wait_recv()

    def own(s):
        p = s.p
        s.send(0, 0, p.at_x(1), 0)
        s.send(0, 1, p.at_x(3), 3)
        s.send(0, 0, p.sib, 6)
        s.send(0, 1, p.sib, 7)
        s.send(0, 1, p.at_x(1), 1)
        s.send(0, 0, p.at_x(3), 2)

    def relay(s):
        p = s.p
        s.got(3, p.c, 0, 0)
        s.send(3, 0, p.at_x(1), 4)
        s.send(3, 0, p.sib, 8)
        s.got(1, p.c, 1, 3)
        s.send(1, 1, p.at_x(3), 5)
        s.send(1, 1, p.sib, 11)

    def rest(s):
        p = s.p
        s.got(3, p.c, 1, 1)
        s.send(3, 1, p.sib, 9)
        s.got(1, p.c, 0, 2)
        s.send(1, 0, p.sib, 10)

    def far(s):
        p = s.p
        s.got(2, p.c, 0, 4)
        s.send(2, 0, p.sib, 12)
        s.got(2, p.c, 1, 5)
        s.send(2, 1, p.sib, 13)

    def sib(s, d):
        base = {0: 6, 3: 8, 1: 10, 2: 12}[d]
        s.got(d, 1 - s.p.c, 0, base)
        s.got(d, 1 - s.p.c, 1, base + 1)

    def end(s):
        for k in s.sent:
            k.wait_send()


class ReduceX:
    def __init__(s, p, buf, sib, half, full, ss, rs):
        s.p, s.buf, s.sib, s.half, s.full, s.ss, s.rs, s.sent = p, buf, sib, half, full, ss, rs, []

    def rows(s, d, c, lo=0, n=128):
        x = lax.rem(s.p.x + d, 4)
        return ds((x * 2 + c) * 128 + lo, n)

    def send(s, src, dst, rid, dev):
        k = rcopy(src, dst, s.ss.at[rid], s.rs.at[rid], dev)
        s.sent.append(k)
        k.start()

    def wait(s, dst, rid):
        rcopy(dst, dst, s.ss.at[rid], s.rs.at[rid], s.p.sib).wait_recv()

    def to_sib(s, d):
        s.send(s.buf.at[s.rows(d, 1 - s.p.c)], s.sib.at[d], d, s.p.sib)

    def add_sib(s, d):
        s.wait(s.sib.at[d], d)
        r = s.rows(d, s.p.c)
        s.buf[r] = (s.buf[r].astype(F32) + s.sib[d].astype(F32)).astype(BF)

    def far(s):
        s.add_sib(2)
        s.send(s.buf.at[s.rows(2, s.p.c, 0, 64)], s.half.at[0], 4, s.p.at_x(1))
        s.send(s.buf.at[s.rows(2, s.p.c, 64, 64)], s.half.at[1], 5, s.p.at_x(3))

    def right(s):
        s.add_sib(1)
        s.send(s.buf.at[s.rows(1, s.p.c, 64, 64)], s.full.at[0, 64:128], 6, s.p.at_x(1))

    def left(s):
        s.add_sib(3)
        s.send(s.buf.at[s.rows(3, s.p.c, 0, 64)], s.full.at[1, 0:64], 7, s.p.at_x(3))

    def near(s):
        s.wait(s.half.at[0], 4)
        r = s.rows(1, s.p.c, 0, 64)
        s.buf[r] = (s.buf[r].astype(F32) + s.half[0].astype(F32)).astype(BF)
        s.send(s.buf.at[r], s.full.at[0, 0:64], 8, s.p.at_x(1))
        s.wait(s.half.at[1], 5)
        r = s.rows(3, s.p.c, 64, 64)
        s.buf[r] = (s.buf[r].astype(F32) + s.half[1].astype(F32)).astype(BF)
        s.send(s.buf.at[r], s.full.at[1, 64:128], 9, s.p.at_x(3))

    def final(s):
        s.wait(s.sib.at[0], 0)
        s.wait(s.full.at[0, 64:128], 6)
        s.wait(s.full.at[1, 0:64], 7)
        s.wait(s.full.at[0, 0:64], 8)
        s.wait(s.full.at[1, 64:128], 9)
        for k in s.sent:
            k.wait_send()
        r = s.rows(0, s.p.c)
        return (s.buf[r].astype(F32) + s.sib[0].astype(F32)) + (
            s.full[0].astype(F32) + s.full[1].astype(F32)
        )


class ReduceHalf:
    def __init__(s, p, unit, a, b, rbuf, ss, rs):
        s.p, s.unit, s.a, s.b, s.r, s.ss, s.rs = p, unit, a, b, rbuf, ss, rs
        s.sent = []

    def at(s, ra, rb):
        ia = lax.rem(getattr(s.p, s.a) + ra, 4)
        ib = lax.rem(getattr(s.p, s.b) + rb, 4)
        zz, yy = (ia, ib) if s.a == "z" else (ib, ia)
        return s.unit(zz * 4 + yy)

    def send(s, ra, rb, axis, d, rid):
        k = rcopy(s.at(ra, rb), s.r.at[rid], s.ss.at[len(s.sent)], s.rs.at[rid], s.p.at(axis, d))
        s.sent.append(k)
        k.start()

    def add(s, ra, rb, *rids):
        for i in rids:
            rcopy(s.r.at[i], s.r.at[i], s.ss.at[0], s.rs.at[i], s.p.at(s.a, 1)).wait_recv()
        u = s.at(ra, rb)
        v = u[...].astype(F32)
        for i in rids:
            v = v + s.r[i].astype(F32)
        u[...] = v.astype(BF)

    def step(s, i):
        a, b = s.a, s.b
        if i == 0:
            for ra in (0, 1):
                s.send(ra, 2, b, 1, 11 + ra)
            for ra in (2, 3):
                s.send(ra, 2, b, 3, 11 + ra)
            for ra in (2, 3):
                s.send(ra, 1, b, 1, 3 + ra)
            for ra in (0, 1):
                s.send(ra, 3, b, 3, 7 + ra)
        if i == 1:
            for ra in (0, 1):
                s.add(ra, 1, 11 + ra)
                s.send(ra, 1, b, 1, 3 + ra)
            for ra in (2, 3):
                s.add(ra, 3, 11 + ra)
                s.send(ra, 3, b, 3, 7 + ra)
        if i == 2:
            s.add(2, 0, 5, 9)
            s.send(2, 0, a, 1, 2)
            s.add(3, 0, 6, 10)
            s.send(3, 0, a, 3, 1)
        if i == 3:
            s.add(1, 0, 4, 8, 2)
            s.send(1, 0, a, 1, 0)
        if i == 4:
            s.add(0, 0, 3, 7, 0, 1)
            for k in s.sent:
                k.wait_send()


class ReduceW:
    def __init__(s, p, unit, rbuf, mine, other, xbuf, xs, ss, rs):
        s.p, s.mine, s.other, s.xbuf, s.xs = p, mine, other, xbuf, xs
        s.own, s.far = lambda u: unit(p.xh, u), lambda u: unit(1 - p.xh, u)
        s.A = ReduceHalf(p, s.own, "y", "z", rbuf.at[0], ss.at[0], rs.at[0])
        s.B = ReduceHalf(p, s.far, "z", "y", rbuf.at[1], ss.at[1], rs.at[1])

    def step(s, i):
        p = s.p
        if i < 5:
            s.B.step(i)
        if i == 4:
            s.xk = rcopy(s.far(p.sb), s.xbuf, s.xs.at[0], s.xs.at[1], p.at_x(2))
            s.xk.start()
        if i < 5:
            s.A.step(i)
        if i == 4:
            s.mine[...] = s.own(p.sb)[...]
        if i == 5:
            s.xk.wait_recv()
            s.xk.wait_send()
            s.other[...] = s.xbuf[...]


def lanes(shape):
    return lax.broadcasted_iota(jnp.int32, shape, len(shape) - 1)


def swap(v):
    n = v.shape[1]
    low = lax.rem(lanes(v.shape), 64) < 32
    return jnp.where(low, pltpu.roll(v, n - 32, 1), pltpu.roll(v, 32, 1))


def head_mean(v):
    n = v.shape[1]
    a = lax.broadcasted_iota(jnp.int32, (n, n), 0) // 64
    b = lax.broadcasted_iota(jnp.int32, (n, n), 1) // 64
    m = jnp.where(a == b, 1.0 / 64, 0.0).astype(F32)
    return mm(v, m, NN, HI)


def rms_inv(v):
    return lax.rsqrt(jnp.mean(v * v, axis=-1, keepdims=True) + EPS)


def loop(n, body):
    lax.fori_loop(0, n, lambda i, c: (body(i), c)[1], 0)


def tile(t, n=TILE):
    return pl.ds(pl.multiple_of(t * n, n), n)


def kernel(
    tokens, segs, attn_gain, ffn_gain, qg, kg, freq, w_query, w_key, w_value, w_out, w_gate, w_up, w_down, out_grad,
    result, grad_tokens, ga_mine, ga_other, gf_mine, gf_other, gains,
    wa, wf, bo, og, b2, mr, hid, dg, du, fr, ar, fx, axb,
    pa, psib, phalf, pfull,
    q, do, kvw, kvt, acc, dkv, dks, dkr, att, qkraw, mid, dmid, ctab, stab,
    segx, segw, stq, lse, dlt, gbuf, gx, gy, gz,
    wsx, was, war, wfs, wfr, gxs, gxr, rxs, rxr, ras, rar, rfs, rfr, kvs, kvr, sgs, sgr, gns, gnr, free,
):
    p = Pos()
    shard = p.x * 2 + p.c
    dall = dg
    own_rows = ds(shard * 128, 128)

    wrow = ds(p.sb * 96 + p.xh * 48, 48)
    low48 = lanes((48, 128)) < 64

    def two_heads(wide, narrow):
        x, k = wide[...].astype(F32), narrow[...].astype(F32)
        far = pltpu.roll(x[:, 128:384], 192, 1)
        first = (x[:, 0:128], jnp.where(low48, x[:, 128:256], pltpu.roll(k, 64, 1)))
        return first, (far[:, 0:128], jnp.where(low48, far[:, 128:], k))

    for base, wide, narrow in ((0, w_query, w_key), (256, w_out, w_value)):
        first, second = two_heads(wide, narrow)
        for j in range(2):
            cols = pl.ds(base + j * 128, 128)
            wa[wrow, cols] = jnp.where(p.xh == 0, first[j], second[j]).astype(BF)
            axb[:, cols] = jnp.where(p.xh == 0, second[j], first[j]).astype(BF)

    def put(dst, rows, half):
        for i, w in enumerate((w_gate, w_up, w_down)):
            if half == 0:
                dst[rows, i * HP : (i + 1) * HP] = w[:, 0:HP]
            else:
                dst[rows, (i + 1) * HP - 128 : (i + 1) * HP] = jnp.zeros((48, 128), BF)
                dst[rows, i * HP : i * HP + HQ] = w[:, HP:]

    for xh in (0, 1):

        @pl.when(p.xh == xh)
        def _(xh=xh):
            put(wf, wrow, xh)
            put(fx, pl.ds(0, 48), 1 - xh)

    tf = tokens[...].astype(F32)
    bo[own_rows] = (tf * rms_inv(tf) * attn_gain[...]).astype(BF)
    og[own_rows] = out_grad[...]
    seg8 = pl.ds(pl.multiple_of(shard * 8, 8), 8)
    segx[seg8] = jnp.broadcast_to(segs[...].astype(F32), (8, 128))
    barrier(p)

    WA = Weights(p, axb, wa, wsx.at[0], was, war)
    WF = Weights(p, fx, wf, wsx.at[1], wfs, wfr)
    WA.exchange()
    GB = GatherX(p, bo, gxs.at[0], gxr.at[0])
    GB.own()
    seg_sent = []
    here = segx.at[seg8]
    peers = [(d, cc) for d in range(4) for cc in range(2) if (d, cc) != (0, 0)]
    for i, (d, cc) in enumerate(peers):
        k = rcopy(here, here, sgs.at[i], sgr.at[i], p.at_x(d, p.c if cc == 0 else 1 - p.c))
        k.start()
        seg_sent.append(k)
    WF.exchange()
    WA.own()
    GO = GatherX(p, og, gxs.at[1], gxr.at[1])

    def trig(t):
        at = lax.broadcasted_iota(jnp.int32, (TILE, 128), 0) + (p.sb * ROWS + t * TILE)
        angle = at.astype(F32) * freq[...]
        sine = jnp.sin(angle)
        ctab[tile(t)] = jnp.cos(angle)
        stab[tile(t)] = jnp.where(lax.rem(lanes((TILE, 128)), 64) < 32, -sine, sine)

    trig(0)
    WA.step(0)
    for i, (d, cc) in enumerate(peers):
        x = lax.rem(p.x + 4 - d, 4)
        c = p.c if cc == 0 else 1 - p.c
        there = segx.at[pl.ds(pl.multiple_of((x * 2 + c) * 8, 8), 8)]
        rcopy(there, there, sgs.at[i], sgr.at[i], p.sib).wait_recv()
    for g in range(8):
        segw[pl.ds(16 + g, 1)] = segx[pl.ds(8 * g, 1)]
    for j in (1, 2):
        k = rcopy(segw.at[pl.ds(16, 8)], segw.at[pl.ds(16 - 8 * j, 8)], sgs.at[6 + j], sgr.at[6 + j], p.at_sb(j))
        k.start()
        seg_sent.append(k)
    WF.own()
    trig(1)
    GB.relay()
    WA.step(1)
    trig(2)
    GB.rest()
    WA.step(2)
    trig(3)
    WA.step(3)
    GB.far()
    WA.step(4)
    for d in range(4):
        GB.sib(d)
    GB.end()
    WA.step(5)
    GO.own()
    WF.step(0)

    for j in (1, 2):
        there = segw.at[pl.ds(16 - 8 * j, 8)]
        rcopy(there, there, sgs.at[6 + j], sgr.at[6 + j], p.sib).wait_recv()
    for k in seg_sent:
        k.wait_send()
    sq = segw[pl.ds(16, 8)]
    s1 = jnp.where(p.sb >= 1, segw[pl.ds(8, 8)], -1.0)
    s2 = jnp.where(p.sb >= 2, segw[pl.ds(0, 8)], -1.0)
    start = jnp.zeros((8, 128), F32)
    for d in range(16):
        fewer = (sq < d).astype(F32) + (s1 < d).astype(F32) + (s2 < d).astype(F32)
        count = jnp.sum(jnp.sum(fewer, axis=1, keepdims=True), axis=0, keepdims=True)
        start = start + jnp.where(sq == d, count, 0.0)
    start = start.astype(jnp.int32)
    for t in range(4):
        for h in range(3):
            for j in range(2):
                stq[pl.ds(t, 1), pl.ds(h * 256 + j * 128, 128)] = start[2 * t + j : 2 * t + j + 1]

    qg2 = jnp.concatenate([qg[...], qg[...]], axis=1)
    gqk = jnp.concatenate([qg2, qg[...], kg[...]], axis=1)

    def project(t):
        x = bo[tile(t)]
        qk = mm(x, wa[:, 0:256], NN)
        ov = mm(x, wa[:, 256:512], NN)
        qkraw[tile(t)] = qk
        n = qk * lax.rsqrt(head_mean(qk * qk) + EPS) * gqk
        c1, s1 = ctab[tile(t)], stab[tile(t)]
        c2, s2 = jnp.concatenate([c1, c1], 1), jnp.concatenate([s1, s1], 1)
        r = n * c2 + swap(n) * s2
        a0, a1 = r[:, :128], r[:, 128:]
        low = lanes((TILE, 128)) < 64
        q[0, tile(t)] = jnp.where(low, a0, 0.0).astype(BF)
        q[1, tile(t)] = jnp.where(low, pltpu.roll(a0, 64, 1), 0.0).astype(BF)
        q[2, tile(t)] = jnp.where(low, a1, 0.0).astype(BF)
        kv = jnp.where(low, pltpu.roll(a1, 64, 1), ov[:, 128:])
        kvw[ds(2048 + t * 256, 256)] = kv.astype(BF)
        kvt[8 + t] = kv.T.astype(BF)

    loop(4, project)
    kv_own = kvw.at[pl.ds(2048, 1024)]
    kv_sent = []
    for j in (1, 2):
        k = rcopy(kv_own, kvw.at[pl.ds(2048 - 1024 * j, 1024)], kvs.at[j - 1], kvr.at[j - 1], p.at_sb(j))
        k.start()
        kv_sent.append(k)

    def kv_wait(j):
        there = kvw.at[pl.ds(2048 - 1024 * j, 1024)]
        rcopy(there, there, kvs.at[j - 1], kvr.at[j - 1], p.sib).wait_recv()

        def turn(t):
            u = 8 - 4 * j + t
            kvt[u] = kvw[tile(u)].astype(F32).T.astype(BF)

        loop(4, turn)

    key_at = lax.broadcasted_iota(jnp.int32, (TILE, 3 * TILE), 0)
    scale = 0.125

    def mask_of(t, u, diag):
        ok = key_at >= stq[pl.ds(t, 1)] - u * TILE
        if diag:
            ok = ok & (key_at <= lax.rem(lanes((TILE, 3 * TILE)), TILE))
        return ok

    def forward(t, u, diag):
        k = kvw[tile(u)]
        q3 = q[:, tile(t)].reshape(3 * TILE, 128)
        s = mm(k, q3, NT)
        e = jnp.where(mask_of(t, u, diag), jnp.exp2(s * (scale * LOG2E)), 0.0).astype(BF)
        va = jnp.where(lax.broadcasted_iota(jnp.int32, (128, TILE), 0) < 64, 1.0, kvt[u].astype(F32)).astype(BF)
        new = mm(va, e, NN)
        if diag:
            acc[t] = new
        else:
            acc[t] = acc[t] + new

    loop(4, lambda t: forward(t, t + 8, True))
    GO.relay()
    loop(3, lambda i: lax.fori_loop(0, i + 1, lambda j, c: (forward(i + 1, 8 + j, False), c)[1], 0))
    WF.step(1)
    GO.rest()
    kv_wait(1)
    kv_wait(2)
    for k in kv_sent:
        k.wait_send()

    def attended(t):
        a = acc[t]
        o = a[64:128] / a[0:64]
        lse[pl.ds(t, 1)] = jnp.log2(a[0:1])
        ot = jnp.concatenate([o[:, 0:256], o[:, 256:512], o[:, 512:768], jnp.zeros((64, 256), F32)], axis=0)
        o2 = ot.T
        att[tile(t)] = o2.astype(BF)

    R1 = ReduceX(p, pa, psib, phalf, pfull, rxs.at[0], rxr.at[0])

    def finish(d):
        x = lax.rem(p.x + d, 4)
        lax.fori_loop(x, 8, lambda u, c: (forward(x, u, False), c)[1], 0)
        attended(x)
        for j in range(3):
            n = pl.ds(j * 512, 512)
            pa[tile(x), n] = mm(att[tile(x)], wa[n, 256:512], NT).astype(BF)
        R1.to_sib(d)

    finish(2)
    GO.far()
    WF.step(2)
    finish(1)
    R1.far()
    WF.step(3)
    finish(3)
    R1.right()
    R1.left()
    finish(0)
    R1.near()
    for d in range(4):
        GO.sib(d)
    GO.end()
    WF.step(4)
    m = tokens[...].astype(F32) + R1.final()
    mid[...] = m
    b2[own_rows] = (m * rms_inv(m) * ffn_gain[...]).astype(BF)
    G2 = GatherX(p, b2, gxs.at[2], gxr.at[2])
    G2.own()
    WF.step(5)

    def ffn(d):
        r = tile(lax.rem(p.x + d, 4))
        for lo, n in ((0, 512), (512, HP - 512)):
            gate = mm(b2[r], wf[:, lo : lo + n], NN)
            up = mm(b2[r], wf[:, HP + lo : HP + lo + n], NN)
            dh = mm(og[r], wf[:, 2 * HP + lo : 2 * HP + lo + n], NN)
            sig = jax.nn.sigmoid(gate)
            swish = gate * sig
            hid[r, lo : lo + n] = (swish * up).astype(BF)
            dg[r, lo : lo + n] = (dh * up * sig * (1.0 + gate * (1.0 - sig))).astype(BF)
            du[r, lo : lo + n] = (dh * swish).astype(BF)

    G2.sib(0)
    ffn(0)
    G2.relay()
    G2.rest()
    G2.sib(3)
    ffn(3)
    G2.far()
    G2.sib(1)
    ffn(1)
    G2.sib(2)
    G2.end()
    ffn(2)

    R2 = ReduceX(p, pa, psib, phalf, pfull, rxs.at[1], rxr.at[1])
    R3 = ReduceX(p, pa, psib, phalf, pfull, rxs.at[2], rxr.at[2])

    def back_in(d):
        r = tile(lax.rem(p.x + d, 4))
        for j in range(3):
            n = pl.ds(j * 512, 512)
            v = mm(dg[r], wf[n, 0:HP], NT) + mm(du[r], wf[n, HP : 2 * HP], NT)
            pa[r, n] = v.astype(BF)
        R2.to_sib(d)

    def branch(d):
        r = tile(lax.rem(p.x + d, 4))
        for j in range(3):
            n = pl.ds(j * 512, 512)
            pa[r, n] = mm(hid[r], wf[n, 2 * HP :], NT).astype(BF)
        R3.to_sib(d)

    def grads(cols, left, right, lo=0, hi=6):
        def body(i, carry):
            c = pl.ds(pl.multiple_of(i * 256, 256), 256)
            wf[tile(i), cols] = mm(left[:, c], right[...], TN).astype(BF)
            return carry

        lax.fori_loop(lo, hi, body, 0)

    back_in(2)
    back_in(1)
    R2.far()
    back_in(3)
    R2.right()
    R2.left()
    back_in(0)
    grads(pl.ds(0, HP), b2, dg, 0, 2)
    R2.near()
    grads(pl.ds(0, HP), b2, dg, 2, 6)

    dn = R2.final()
    m = mid[...]
    r = rms_inv(m)
    n = m * r
    e = dn * ffn_gain[...]
    dm = out_grad[...].astype(F32) + r * (e - n * jnp.mean(e * n, axis=-1, keepdims=True))
    dmid[...] = dm
    gbuf[...] = jnp.zeros_like(gbuf)
    gbuf[pl.ds(1, 1)] = jnp.sum(dn * n, axis=0, keepdims=True)
    mr[own_rows] = dm.astype(BF)
    G3 = GatherX(p, mr, gxs.at[3], gxr.at[3])
    G3.own()

    grads(pl.ds(HP, HP), b2, du)
    G3.relay()
    G3.rest()
    G3.sib(0)
    branch(2)
    branch(1)
    R3.far()
    branch(3)
    R3.right()
    R3.left()
    branch(0)
    G3.far()
    grads(pl.ds(2 * HP, HP), og, hid, 0, 3)
    R3.near()
    grads(pl.ds(2 * HP, HP), og, hid, 3, 6)
    RF = ReduceW(
        p, lambda h, u: wf.at[ds(u * 96 + h * 48, 48)], fr, gf_mine, gf_other, fx, wsx.at[2], rfs, rfr
    )
    RF.step(0)
    for d in (3, 1, 2):
        G3.sib(d)
    G3.end()

    head_row = lax.broadcasted_iota(jnp.int32, (8, 256), 0)
    head_lane = lanes((8, 256)) // 64
    per_head = jnp.where(head_row == head_lane, 1.0, 0.0).astype(F32)

    def d_attended(t):
        d = mm(mr[tile(t)], wa[:, 256:512], NN).astype(BF).astype(F32)
        sums = mm(per_head, d * att[tile(t)].astype(F32), NT, HI)
        for h in range(3):
            dlt[pl.ds(t, 1), pl.ds(h * 256, 256)] = sums[h : h + 1]
        a0, a1 = d[:, :128], d[:, 128:]
        high = lanes((TILE, 128)) >= 64
        do[0, tile(t)] = jnp.where(high, pltpu.roll(a0, 64, 1), 0.0).astype(BF)
        do[1, tile(t)] = jnp.where(high, a0, 0.0).astype(BF)
        do[2, tile(t)] = jnp.where(high, pltpu.roll(a1, 64, 1), 0.0).astype(BF)
        acc[t] = jnp.zeros((128, 768), F32)

    loop(4, d_attended)
    result[...] = (mid[...] + R3.final()).astype(BF)
    for dev in (p.sib, p.at_x(1), p.at_x(3)):
        pl.semaphore_signal(free, inc=1, device_id=dev, device_id_type=MESH)
    dkv[...] = jnp.zeros_like(dkv)

    def backward(t, u, diag):
        k = kvw[tile(u)]
        q3 = q[:, tile(t)].reshape(3 * TILE, 128)
        do3 = do[:, tile(t)].reshape(3 * TILE, 128)
        s = mm(k, q3, NT)
        pr = jnp.where(mask_of(t, u, diag), jnp.exp2(s * (scale * LOG2E) - lse[pl.ds(t, 1)]), 0.0)
        dp = mm(k, do3, NT)
        dsc = (pr * (dp - dlt[pl.ds(t, 1)])).astype(BF)
        dkv[u] = dkv[u] + mm(dsc, q3, NN) + mm(pr.astype(BF), do3, NN)
        acc[t] = acc[t] + mm(kvt[u], dsc, NN)

    def scaled(v):
        return jnp.where(lanes(v.shape) < 64, v * scale, v)

    dk_sent = []

    def dk_send(j):
        def body(t):
            dks[j - 1, tile(t)] = scaled(dkv[8 - 4 * j + t]).astype(BF)

        loop(4, body)
        k = rcopy(dks.at[j - 1], dkr.at[j - 1], kvs.at[1 + j], kvr.at[1 + j], p.at_sb(-j))
        k.start()
        dk_sent.append(k)

    loop(4, lambda i: lax.fori_loop(0, i + 1, lambda t, c: (backward(t, i, False), c)[1], 0))
    dk_send(2)
    RF.step(1)
    loop(4, lambda t: backward(t, 4, False))
    loop(4, lambda t: backward(t, 5, False))
    RF.step(2)
    loop(4, lambda t: backward(t, 6, False))
    loop(4, lambda t: backward(t, 7, False))
    dk_send(1)
    RF.step(3)
    loop(3, lambda i: lax.fori_loop(0, i + 1, lambda j, c: (backward(i + 1, 8 + j, False), c)[1], 0))
    RF.step(4)
    loop(4, lambda t: backward(t, t + 8, True))
    RF.step(5)
    for j in (1, 2):
        rcopy(dkr.at[j - 1], dkr.at[j - 1], kvs.at[1 + j], kvr.at[1 + j], p.sib).wait_recv()
    for k in dk_sent:
        k.wait_send()

    def unproject(t):
        a = acc[t][0:64]
        at = jnp.concatenate([a[:, 0:256], a[:, 256:512], a[:, 512:768], jnp.zeros((64, 256), F32)], axis=0)
        dq = at.T * scale
        dk = scaled(dkv[8 + t]) + dkr[0, tile(t)].astype(F32) + dkr[1, tile(t)].astype(F32)
        low = lanes((TILE, 128)) < 64
        d = jnp.concatenate([dq[:, :128], jnp.where(low, dq[:, 128:], pltpu.roll(dk, 64, 1))], 1)
        d = d.astype(BF).astype(F32)
        c1, s1 = ctab[tile(t)], stab[tile(t)]
        c2, s2 = jnp.concatenate([c1, c1], 1), jnp.concatenate([s1, s1], 1)
        dn = d * c2 + swap(d * s2)
        raw = qkraw[tile(t)]
        r = lax.rsqrt(head_mean(raw * raw) + EPS)
        n = raw * r
        e = dn * gqk
        dx = r * (e - n * head_mean(e * n))
        gbuf[pl.ds(2, 1), pl.ds(0, 256)] = gbuf[pl.ds(2, 1), pl.ds(0, 256)] + jnp.sum(dn * n, axis=0, keepdims=True)
        dall[tile(t), 0:256] = dx.astype(BF)
        dall[tile(t), 256:384] = jnp.zeros((TILE, 128), BF)
        dall[tile(t), 384:512] = jnp.where(low, 0.0, dk).astype(BF)

    loop(4, unproject)

    def attn_grads(i):
        c = pl.ds(pl.multiple_of(i * 384, 128), 384)
        for lo in (0, 256):
            v = mm(bo[:, c], dall[:, lo : lo + 256], TN)
            if lo:
                v = v + mm(mr[:, c], att[...], TN)
            v = v.astype(BF)
            for j in range(8):
                fr[j % 2, i * 4 + j // 2, :, lo : lo + 256] = v[j * 48 : j * 48 + 48]

    loop(4, attn_grads)
    RA = ReduceW(p, lambda h, u: fr.at[h, u, :, 0:CA], ar, ga_mine, ga_other, axb, wsx.at[3], ras, rar)
    RA.step(0)

    pl.semaphore_wait(free, 3)
    R4 = ReduceX(p, pa, psib, phalf, pfull, rxs.at[3], rxr.at[3])
    total = [jnp.zeros((1, 512), F32)] * 3
    for d in (2, 1, 3, 0):
        x = lax.rem(p.x + d, 4)
        for j in range(3):
            n = pl.ds(j * 512, 512)
            v = mm(dall[tile(x), 0:512], wa[n, :], NT)
            pa[tile(x), n] = v.astype(BF)
            total[j] = total[j] + jnp.sum(v * bo[tile(x), n].astype(F32), axis=0, keepdims=True)
        R4.to_sib(d)
        if d == 1:
            R4.far()
        if d == 3:
            R4.right()
            R4.left()
    gbuf[pl.ds(0, 1)] = jnp.concatenate(total, axis=1) / attn_gain[...]
    RA.step(1)
    R4.near()

    sent = []
    gx[shard] = gbuf[...]
    for i, (d, cc) in enumerate(peers):
        k = rcopy(gbuf, gx.at[shard], gns.at[i], gnr.at[i], p.at_x(d, p.c if cc == 0 else 1 - p.c))
        k.start()
        sent.append(k)
    RA.step(2)
    for i in range(7):
        rcopy(gx.at[i], gx.at[i], gns.at[i], gnr.at[i], p.sib).wait_recv()
    v = gx[0]
    for i in range(1, 8):
        v = v + gx[i]
    gy[p.y] = v
    for d in (1, 2, 3):
        k = rcopy(gy.at[p.y], gy.at[p.y], gns.at[6 + d], gnr.at[6 + d], p.at("y", d))
        k.start()
        sent.append(k)
    dn = R4.final()
    t = tokens[...].astype(F32)
    r = rms_inv(t)
    n = t * r
    e = dn * attn_gain[...]
    grad_tokens[...] = (dmid[...] + r * (e - n * jnp.mean(e * n, axis=-1, keepdims=True))).astype(BF)
    RA.step(3)
    for d in (1, 2, 3):
        rcopy(gy.at[0], gy.at[0], gns.at[6 + d], gnr.at[6 + d], p.sib).wait_recv()
    v = (gy[0] + gy[1]) + (gy[2] + gy[3])
    gz[p.z] = v
    for d in (1, 2, 3):
        k = rcopy(gz.at[p.z], gz.at[p.z], gns.at[9 + d], gnr.at[9 + d], p.at("z", d))
        k.start()
        sent.append(k)
    RA.step(4)
    for d in (1, 2, 3):
        rcopy(gz.at[0], gz.at[0], gns.at[9 + d], gnr.at[9 + d], p.sib).wait_recv()
    gains[...] = (gz[0] + gz[1]) + (gz[2] + gz[3])
    for k in sent:
        k.wait_send()
    RA.step(5)


VMEM_LIMIT = 63 * 2**20
VM = pl.BlockSpec(memory_space=pltpu.VMEM)


def call_kernel(*args):
    S = jax.ShapeDtypeStruct
    V = pltpu.VMEM
    dma = pltpu.SemaphoreType.DMA
    outs = (
        S((128, D), BF), S((128, D), BF), S((48, CA), BF), S((48, CA), BF),
        S((48, CF), BF), S((48, CF), BF), S((8, D), F32),
    )
    scratch = [
        V((D, CA), BF), V((D, CF), BF), V((ROWS, D), BF), V((ROWS, D), BF), V((ROWS, D), BF), V((ROWS, D), BF),
        V((ROWS, HP), BF), V((ROWS, HP), BF), V((ROWS, HP), BF),
        V((2, 16, 48, CF), BF), V((2, 15, 48, CA), BF), V((48, CF), BF), V((48, CA), BF),
        V((ROWS, D), BF), V((4, 128, D), BF), V((2, 64, D), BF), V((2, 128, D), BF),
        V((3, ROWS, 128), BF), V((3, ROWS, 128), BF), V((3 * ROWS, 128), BF), V((12, 128, TILE), BF),
        V((4, 128, 768), F32), V((12, TILE, 128), F32), V((2, ROWS, 128), BF), V((2, ROWS, 128), BF),
        V((ROWS, 256), BF), V((ROWS, 256), F32),
        V((128, D), F32), V((128, D), F32), V((ROWS, 128), F32), V((ROWS, 128), F32),
        V((64, 128), F32), V((24, 128), F32), V((8, 768), jnp.int32), V((8, 768), F32), V((8, 768), F32),
        V((8, D), F32), V((8, 8, D), F32), V((4, 8, D), F32), V((4, 8, D), F32),
        dma((4, 2)), dma((2, 15)), dma((2, 15)), dma((2, 15)), dma((2, 15)),
        dma((4, 14)), dma((4, 14)), dma((4, 10)), dma((4, 10)),
        dma((2, 15)), dma((2, 15)), dma((2, 15)), dma((2, 15)),
        dma((4,)), dma((4,)), dma((9,)), dma((9,)), dma((13,)), dma((13,)), pltpu.SemaphoreType.REGULAR,
    ]
    return pl.pallas_call(
        kernel,
        out_shape=outs,
        in_specs=[VM] * len(args),
        out_specs=(VM,) * len(outs),
        scratch_shapes=scratch,
        compiler_params=pltpu.CompilerParams(
            collective_id=0, has_side_effects=True, vmem_limit_bytes=VMEM_LIMIT
        ),
    )(*args)


def last_kernel(
    res, gtok, ga_mine, ga_other, gf_mine, gf_other, gains,
    result, grad_tokens, g_attn, g_query, g_key, g_value, g_qg, g_kg, g_out, g_ffn, g_gate, g_up, g_down,
):
    xh = lax.axis_index("xh")
    result[...] = res[...]
    grad_tokens[...] = gtok[...]
    g_attn[...] = gains[0:1]
    g_ffn[...] = gains[1:2]
    a0, a1 = gains[2:3, 0:128], gains[2:3, 128:256]
    g_qg[...] = a0[:, 0:64] + pltpu.roll(a0, 64, 1)[:, 0:64] + a1[:, 0:64]
    g_kg[...] = pltpu.roll(a1, 64, 1)[:, 0:64]
    low = lanes((48, 128)) < 64
    for base, wide, narrow in ((0, g_query, g_key), (256, g_out, g_value)):
        m = [ga_mine[:, base + j * 128 : base + j * 128 + 128].astype(F32) for j in range(2)]
        o = [ga_other[:, base + j * 128 : base + j * 128 + 128].astype(F32) for j in range(2)]
        h0 = [jnp.where(xh == 0, a, b) for a, b in zip(m, o)]
        h1 = [jnp.where(xh == 0, b, a) for a, b in zip(m, o)]
        turned = [pltpu.roll(v, 64, 1) for v in h1]
        wide[:, 0:128] = h0[0]
        wide[:, 128:256] = jnp.where(low, h0[1], turned[0])
        wide[:, 256:384] = jnp.where(low, turned[0], turned[1])
        narrow[...] = jnp.where(low, pltpu.roll(h0[1], 64, 1), h1[1])
    for at in (0, 1):

        @pl.when(xh == at)
        def _(at=at):
            first, second = (gf_mine, gf_other) if at == 0 else (gf_other, gf_mine)
            for i, out in enumerate((g_gate, g_up, g_down)):
                out[:, 0:HP] = first[:, i * HP : (i + 1) * HP].astype(F32)
                out[:, HP:] = second[:, i * HP : i * HP + HQ].astype(F32)


def call_last(*args):
    S = jax.ShapeDtypeStruct
    outs = (
        S((128, D), BF), S((128, D), BF), S((1, D), F32), S((48, 384), F32), S((48, 128), F32), S((48, 128), F32),
        S((1, 64), F32), S((1, 64), F32), S((48, 384), F32), S((1, D), F32),
        S((48, HP + HQ), F32), S((48, HP + HQ), F32), S((48, HP + HQ), F32),
    )
    return pl.pallas_call(
        last_kernel,
        out_shape=outs,
        in_specs=[VM] * len(args),
        out_specs=(VM,) * len(outs),
        compiler_params=pltpu.CompilerParams(vmem_limit_bytes=32 * 2**20),
    )(*args)


def on_device(
    tokens, segments, attn_gain, w_query, w_key, w_value, query_gain, key_gain, w_out, ffn_gain,
    w_gate, w_up, w_down, out_grad,
):
    steps = np.arange(32, dtype=np.float32) * np.float32(2.0 / 64)
    freqs = np.exp(-np.log(np.float32(THETA)) * steps).astype(np.float32)
    freq = jnp.asarray(np.tile(freqs, 4)[None, :])
    parts = call_kernel(
        tokens, segments[None], attn_gain[None], ffn_gain[None], query_gain[None], key_gain[None], freq,
        w_query, w_key, w_value, w_out.T, w_gate, w_up, w_down.T, out_grad,
    )
    out = list(call_last(*parts))
    for i in (2, 6, 7, 9):
        out[i] = out[i][0]
    for i in (8, 12):
        out[i] = out[i].T
    return tuple(out)


def solution(mesh):
    finer = Mesh(mesh.devices.reshape(4, 4, 2, 2, 2), AXES)
    rows, blk, narrow = P(AXES), ("z", "y", "xh"), ("xl", "core")
    cols, turned = P(blk, narrow), P(narrow, blk)
    in_specs = (rows, rows, P(), cols, cols, cols, P(), P(), turned, P(), cols, cols, turned, rows)
    out_specs = (rows, rows, P(), cols, cols, cols, P(), P(), turned, P(), cols, cols, turned)
    return jax.shard_map(
        on_device, mesh=finer, in_specs=in_specs, out_specs=out_specs, check_vma=False
    )
```

```python
from functools import partial

import jax
import jax.numpy as jnp
import numpy as np
from jax import lax
from jax.experimental import pallas as pl
from jax.experimental.pallas import tpu as pltpu
from jax.sharding import Mesh
from jax.sharding import PartitionSpec as P

EPS = 1e-05
THETA = 1000000.0
LOG2E = 1.4426950408889634
MESH = pl.DeviceIdType.MESH
BF = jnp.bfloat16
F32 = jnp.float32
HI = lax.Precision.HIGHEST
AXES = ("z", "y", "xh", "xl", "core")

D = 1536
HP = 896
HQ = 832
CF = 3 * HP
CA = 512
ROWS = 1024
TILE = 256
NT = ((1,), (1,)), ((), ())
NN = ((1,), (0,)), ((), ())
TN = ((0,), (0,)), ((), ())


def mm(a, b, dims, precision=None):
    return lax.dot_general(a, b, dims, precision=precision, preferred_element_type=F32)


class Pos:
    def __init__(s):
        ax = lax.axis_index
        s.z, s.y, s.xh, s.xl, s.c = ax("z"), ax("y"), ax("xh"), ax("xl"), ax("core")
        s.x = s.xh * 2 + s.xl
        s.sb = s.z * 4 + s.y
        s.sib = s.at_x(0, 1 - s.c)

    def at_x(s, d, c=None):
        x = lax.rem(s.x + d, 4)
        return {"xh": x // 2, "xl": lax.rem(x, 2), "core": s.c if c is None else c}

    def at(s, axis, d):
        return {axis: lax.rem(getattr(s, axis) + d, 4)}

    def at_sb(s, d):
        t = lax.rem(s.sb + d + 16, 16)
        return {"z": t // 4, "y": lax.rem(t, 4)}


def barrier(p):
    b = pltpu.get_barrier_semaphore()
    peers = [p.at("y", 1), p.at("y", 2), p.at("y", 3), p.at("z", 1), p.at("z", 2), p.at("z", 3)]
    peers += [p.at_sb(d) for d in (1, 2, -1, -2)]
    peers += [p.at_x(d, cc) for d in (1, 2, 3) for cc in (p.c, 1 - p.c)] + [p.sib]
    for q in peers:
        pl.semaphore_signal(b, inc=1, device_id=q, device_id_type=MESH)
    pl.semaphore_wait(b, len(peers))


def rcopy(src, dst, ss, rs, dev):
    return pltpu.make_async_remote_copy(
        src_ref=src, dst_ref=dst, send_sem=ss, recv_sem=rs, device_id=dev, device_id_type=MESH
    )


def ds(start, n):
    return pl.ds(pl.multiple_of(start, 16), n)


class Half:
    def __init__(s, p, w, off, a, b, ss, rs, direct):
        s.p, s.w, s.off, s.a, s.b, s.ss, s.rs, s.direct = p, w, off, a, b, ss, rs, direct
        s.sent = []

    def unit(s, ra, rb):
        ia = lax.rem(getattr(s.p, s.a) + ra, 4)
        ib = lax.rem(getattr(s.p, s.b) + rb, 4)
        zz, yy = (ia, ib) if s.a == "z" else (ib, ia)
        return s.w.at[ds((zz * 4 + yy) * 96 + s.off, 48)]

    def send(s, ra, rb, axis, d, rid):
        u = s.unit(ra, rb)
        k = rcopy(u, u, s.ss.at[len(s.sent)], s.rs.at[rid], s.p.at(axis, d))
        s.sent.append(k)
        k.start()

    def got(s, ra, rb, rid):
        u = s.unit(ra, rb)
        rcopy(u, u, s.ss.at[0], s.rs.at[rid], s.p.at(s.a, 1)).wait_recv()

    def over_b(s, ra):
        s.send(ra, 0, s.b, 1, 3 + ra)
        s.send(ra, 0, s.b, 3, 7 + ra)
        if s.direct:
            s.send(ra, 0, s.b, 2, 11 + ra)

    def own(s):
        s.send(0, 0, s.a, 1, 0)
        s.send(0, 0, s.a, 3, 1)
        s.send(0, 0, s.a, 2, 2)
        s.over_b(0)

    def spread(s, *ids):
        for ra in ids:
            s.got(ra, 0, {3: 0, 1: 1, 2: 2}[ra])
            s.over_b(ra)

    def relay(s, *ids):
        for ra in ids:
            rb, rid, d = (3, 3 + ra, 1) if ra < 2 else (1, 7 + ra, 3)
            s.got(ra, rb, rid)
            s.send(ra, rb, s.b, d, 11 + ra)

    def end(s):
        for ra in range(4):
            if s.direct or ra < 2:
                s.got(ra, 1, 7 + ra)
            if s.direct or ra >= 2:
                s.got(ra, 3, 3 + ra)
            s.got(ra, 2, 11 + ra)
        for k in s.sent:
            k.wait_send()


class Weights:
    def __init__(s, p, theirs, w, xs, ss, rs, direct):
        s.p, s.theirs, s.w, s.xs = p, theirs, w, xs
        s.oo, s.po = p.xh * 48, (1 - p.xh) * 48
        s.A = Half(p, w, s.oo, "y", "z", ss.at[0], rs.at[0], direct)
        s.B = Half(p, w, s.po, "z", "y", ss.at[1], rs.at[1], direct)

    def exchange(s):
        p = s.p
        dst = s.w.at[ds(p.sb * 96 + s.oo, 48)]
        s.xk = rcopy(s.theirs, dst, s.xs.at[0], s.xs.at[1], p.at_x(2))
        s.xk.start()

    def first(s):
        s.A.own()

    def second(s):
        p = s.p
        got = s.w.at[ds(p.sb * 96 + s.po, 48)]
        rcopy(s.theirs, got, s.xs.at[0], s.xs.at[1], p.at_x(2)).wait_recv()
        s.B.own()

    def spread(s, *ids):
        s.A.spread(*ids)
        s.B.spread(*ids)

    def relay(s, *ids):
        s.A.relay(*ids)
        s.B.relay(*ids)

    def end(s):
        s.A.end()
        s.B.end()
        s.xk.wait_send()


class GatherX:
    def __init__(s, p, buf, ss, rs):
        s.p, s.buf, s.ss, s.rs, s.sent = p, buf, ss, rs, []

    def piece(s, d, c, i):
        x = lax.rem(s.p.x + d, 4)
        return s.buf.at[ds((x * 2 + c) * 128 + i * 64, 64)]

    def send(s, d, i, dev, rid):
        u = s.piece(d, s.p.c, i)
        k = rcopy(u, u, s.ss.at[len(s.sent)], s.rs.at[rid], dev)
        s.sent.append(k)
        k.start()

    def got(s, d, c, i, rid):
        u = s.piece(d, c, i)
        rcopy(u, u, s.ss.at[0], s.rs.at[rid], s.p.sib).wait_recv()

    def own(s):
        p = s.p
        s.send(0, 0, p.at_x(1), 0)
        s.send(0, 1, p.at_x(3), 3)
        s.send(0, 0, p.sib, 6)
        s.send(0, 1, p.sib, 7)
        s.send(0, 1, p.at_x(1), 1)
        s.send(0, 0, p.at_x(3), 2)

    def relay(s):
        p = s.p
        s.got(3, p.c, 0, 0)
        s.send(3, 0, p.at_x(1), 4)
        s.send(3, 0, p.sib, 8)
        s.got(1, p.c, 1, 3)
        s.send(1, 1, p.at_x(3), 5)
        s.send(1, 1, p.sib, 11)

    def rest(s):
        p = s.p
        s.got(3, p.c, 1, 1)
        s.send(3, 1, p.sib, 9)
        s.got(1, p.c, 0, 2)
        s.send(1, 0, p.sib, 10)

    def far(s):
        p = s.p
        s.got(2, p.c, 0, 4)
        s.send(2, 0, p.sib, 12)
        s.got(2, p.c, 1, 5)
        s.send(2, 1, p.sib, 13)

    def sib(s, d):
        base = {0: 6, 3: 8, 1: 10, 2: 12}[d]
        s.got(d, 1 - s.p.c, 0, base)
        s.got(d, 1 - s.p.c, 1, base + 1)

    def end(s):
        for k in s.sent:
            k.wait_send()


class ReduceX:
    def __init__(s, p, buf, sib, half, full, ss, rs):
        s.p, s.buf, s.sib, s.half, s.full, s.ss, s.rs, s.sent = p, buf, sib, half, full, ss, rs, []

    def rows(s, d, c, lo=0, n=128):
        x = lax.rem(s.p.x + d, 4)
        return ds((x * 2 + c) * 128 + lo, n)

    def send(s, src, dst, rid, dev):
        k = rcopy(src, dst, s.ss.at[rid], s.rs.at[rid], dev)
        s.sent.append(k)
        k.start()

    def wait(s, dst, rid):
        rcopy(dst, dst, s.ss.at[rid], s.rs.at[rid], s.p.sib).wait_recv()

    def to_sib(s, d):
        s.send(s.buf.at[s.rows(d, 1 - s.p.c)], s.sib.at[d], d, s.p.sib)

    def add_sib(s, d):
        s.wait(s.sib.at[d], d)
        r = s.rows(d, s.p.c)
        s.buf[r] = (s.buf[r].astype(F32) + s.sib[d].astype(F32)).astype(BF)

    def far(s):
        s.add_sib(2)
        s.send(s.buf.at[s.rows(2, s.p.c, 0, 64)], s.half.at[0], 4, s.p.at_x(1))
        s.send(s.buf.at[s.rows(2, s.p.c, 64, 64)], s.half.at[1], 5, s.p.at_x(3))

    def right(s):
        s.add_sib(1)
        s.send(s.buf.at[s.rows(1, s.p.c, 64, 64)], s.full.at[0, 64:128], 6, s.p.at_x(1))

    def left(s):
        s.add_sib(3)
        s.send(s.buf.at[s.rows(3, s.p.c, 0, 64)], s.full.at[1, 0:64], 7, s.p.at_x(3))

    def near(s):
        s.wait(s.half.at[0], 4)
        r = s.rows(1, s.p.c, 0, 64)
        s.buf[r] = (s.buf[r].astype(F32) + s.half[0].astype(F32)).astype(BF)
        s.send(s.buf.at[r], s.full.at[0, 0:64], 8, s.p.at_x(1))
        s.wait(s.half.at[1], 5)
        r = s.rows(3, s.p.c, 64, 64)
        s.buf[r] = (s.buf[r].astype(F32) + s.half[1].astype(F32)).astype(BF)
        s.send(s.buf.at[r], s.full.at[1, 64:128], 9, s.p.at_x(3))

    def final(s):
        s.wait(s.sib.at[0], 0)
        s.wait(s.full.at[0, 64:128], 6)
        s.wait(s.full.at[1, 0:64], 7)
        s.wait(s.full.at[0, 0:64], 8)
        s.wait(s.full.at[1, 64:128], 9)
        for k in s.sent:
            k.wait_send()
        r = s.rows(0, s.p.c)
        return (s.buf[r].astype(F32) + s.sib[0].astype(F32)) + (
            s.full[0].astype(F32) + s.full[1].astype(F32)
        )


class ReduceHalf:
    def __init__(s, p, unit, a, b, rbuf, ss, rs, direct):
        s.p, s.unit, s.a, s.b, s.r, s.ss, s.rs, s.direct = p, unit, a, b, rbuf, ss, rs, direct
        s.sent = []

    def at(s, ra, rb):
        ia = lax.rem(getattr(s.p, s.a) + ra, 4)
        ib = lax.rem(getattr(s.p, s.b) + rb, 4)
        zz, yy = (ia, ib) if s.a == "z" else (ib, ia)
        return s.unit(zz * 4 + yy)

    def send(s, ra, rb, axis, d, rid):
        k = rcopy(s.at(ra, rb), s.r.at[rid], s.ss.at[len(s.sent)], s.rs.at[rid], s.p.at(axis, d))
        s.sent.append(k)
        k.start()

    def add(s, ra, rb, *rids):
        for i in rids:
            rcopy(s.r.at[i], s.r.at[i], s.ss.at[0], s.rs.at[i], s.p.at(s.a, 1)).wait_recv()
        u = s.at(ra, rb)
        v = u[...].astype(F32)
        for i in rids:
            v = v + s.r[i].astype(F32)
        u[...] = v.astype(BF)

    def begin(s):
        if s.direct:
            for rb in (2, 1, 3):
                for ra in range(4):
                    s.send(ra, rb, s.b, rb, (rb - 1) * 4 + ra)
            return
        for ra in range(4):
            s.send(ra, 2, s.b, 1 if ra < 2 else 3, 8 + ra)
        for ra in range(4):
            rb = 3 if ra < 2 else 1
            s.send(ra, rb, s.b, rb, (4 if rb == 3 else 0) + ra)

    def pass_on(s):
        for ra in range(4):
            rb = 1 if ra < 2 else 3
            s.add(ra, rb, 8 + ra)
            s.send(ra, rb, s.b, rb, (4 if rb == 3 else 0) + ra)

    def over_a(s):
        for ra in (2, 1, 3):
            s.add(ra, 0, ra, 4 + ra, *([8 + ra] if s.direct else []))
            s.send(ra, 0, s.a, ra, 11 + ra)

    def last(s):
        s.add(0, 0, 0, 4, *([8] if s.direct else []), 12, 13, 14)
        for k in s.sent:
            k.wait_send()


class ReduceW:
    def __init__(s, p, unit, rbuf, mine, other, xbuf, xs, ss, rs, direct):
        s.p, s.mine, s.other, s.xbuf, s.xs = p, mine, other, xbuf, xs
        s.own, s.far = lambda u: unit(p.xh, u), lambda u: unit(1 - p.xh, u)
        s.A = ReduceHalf(p, s.own, "y", "z", rbuf.at[0], ss.at[0], rs.at[0], direct)
        s.B = ReduceHalf(p, s.far, "z", "y", rbuf.at[1], ss.at[1], rs.at[1], direct)

    def begin(s):
        s.A.begin()
        s.B.begin()

    def pass_on(s):
        s.A.pass_on()
        s.B.pass_on()

    def over_a(s):
        s.A.over_a()
        s.B.over_a()

    def last(s):
        s.B.last()
        s.xk = rcopy(s.far(s.p.sb), s.xbuf, s.xs.at[0], s.xs.at[1], s.p.at_x(2))
        s.xk.start()
        s.A.last()
        s.mine[...] = s.own(s.p.sb)[...]

    def end(s):
        s.xk.wait_recv()
        s.xk.wait_send()
        s.other[...] = s.xbuf[...]


def lanes(shape):
    return lax.broadcasted_iota(jnp.int32, shape, len(shape) - 1)


def swap(v):
    n = v.shape[1]
    low = lax.rem(lanes(v.shape), 64) < 32
    return jnp.where(low, pltpu.roll(v, n - 32, 1), pltpu.roll(v, 32, 1))


def head_mean(v):
    n = v.shape[1]
    a = lax.broadcasted_iota(jnp.int32, (n, n), 0) // 64
    b = lax.broadcasted_iota(jnp.int32, (n, n), 1) // 64
    m = jnp.where(a == b, 1.0 / 64, 0.0).astype(F32)
    return mm(v, m, NN, HI)


def rms_inv(v):
    return lax.rsqrt(jnp.mean(v * v, axis=-1, keepdims=True) + EPS)


def loop(n, body):
    lax.fori_loop(0, n, lambda i, c: (body(i), c)[1], 0)


def tile(t, n=TILE):
    return pl.ds(pl.multiple_of(t * n, n), n)


def kernel(
    tokens, segs, attn_gain, ffn_gain, qg, kg, freq, w_query, w_key, w_value, w_out, w_gate, w_up, w_down, out_grad,
    result, grad_tokens, ga_mine, ga_other, gf_mine, gf_other, gains,
    wa, wf, bo, og, b2, mr, hid, dg, du, fr, ar, fx, axb,
    pa, psib, phalf, pfull,
    q, do, kvw, kvt, acc, dkv, dks, dkr, att, qkraw, mid, dmid, ctab, stab,
    segx, segw, stq, lse, dlt, gbuf, gx, gy, gz,
    wsx, was, war, wfs, wfr, gxs, gxr, rxs, rxr, ras, rar, rfs, rfr, kvs, kvr, sgs, sgr, gns, gnr, free,
):
    p = Pos()
    shard = p.x * 2 + p.c
    dall = dg
    own_rows = ds(shard * 128, 128)

    wrow = ds(p.sb * 96 + p.xh * 48, 48)
    low48 = lanes((48, 128)) < 64

    def two_heads(wide, narrow):
        x, k = wide[...].astype(F32), narrow[...].astype(F32)
        far = pltpu.roll(x[:, 128:384], 192, 1)
        first = (x[:, 0:128], jnp.where(low48, x[:, 128:256], pltpu.roll(k, 64, 1)))
        return first, (far[:, 0:128], jnp.where(low48, far[:, 128:], k))

    for base, wide, narrow in ((0, w_query, w_key), (256, w_out, w_value)):
        first, second = two_heads(wide, narrow)
        for j in range(2):
            cols = pl.ds(base + j * 128, 128)
            wa[wrow, cols] = jnp.where(p.xh == 0, first[j], second[j]).astype(BF)
            axb[:, cols] = jnp.where(p.xh == 0, second[j], first[j]).astype(BF)

    def put(dst, rows, half):
        for i, w in enumerate((w_gate, w_up, w_down)):
            if half == 0:
                dst[rows, i * HP : (i + 1) * HP] = w[:, 0:HP]
            else:
                dst[rows, (i + 1) * HP - 128 : (i + 1) * HP] = jnp.zeros((48, 128), BF)
                dst[rows, i * HP : i * HP + HQ] = w[:, HP:]

    for xh in (0, 1):

        @pl.when(p.xh == xh)
        def _(xh=xh):
            put(wf, wrow, xh)
            put(fx, pl.ds(0, 48), 1 - xh)

    tf = tokens[...].astype(F32)
    bo[own_rows] = (tf * rms_inv(tf) * attn_gain[...]).astype(BF)
    og[own_rows] = out_grad[...]
    seg8 = pl.ds(pl.multiple_of(shard * 8, 8), 8)
    segx[seg8] = jnp.broadcast_to(segs[...].astype(F32), (8, 128))
    barrier(p)

    WA = Weights(p, axb, wa, wsx.at[0], was, war, True)
    WF = Weights(p, fx, wf, wsx.at[1], wfs, wfr, False)
    WA.exchange()
    GB = GatherX(p, bo, gxs.at[0], gxr.at[0])
    GB.own()
    seg_sent = []
    here = segx.at[seg8]
    peers = [(d, cc) for d in range(4) for cc in range(2) if (d, cc) != (0, 0)]
    for i, (d, cc) in enumerate(peers):
        k = rcopy(here, here, sgs.at[i], sgr.at[i], p.at_x(d, p.c if cc == 0 else 1 - p.c))
        k.start()
        seg_sent.append(k)
    WA.first()
    WF.exchange()
    WF.first()
    GO = GatherX(p, og, gxs.at[1], gxr.at[1])

    def trig(t):
        at = lax.broadcasted_iota(jnp.int32, (TILE, 128), 0) + (p.sb * ROWS + t * TILE)
        angle = at.astype(F32) * freq[...]
        sine = jnp.sin(angle)
        ctab[tile(t)] = jnp.cos(angle)
        stab[tile(t)] = jnp.where(lax.rem(lanes((TILE, 128)), 64) < 32, -sine, sine)

    trig(0)
    WA.second()
    WF.second()
    GB.relay()
    trig(1)
    WA.spread(3, 1, 2)
    GB.rest()
    for i, (d, cc) in enumerate(peers):
        x = lax.rem(p.x + 4 - d, 4)
        c = p.c if cc == 0 else 1 - p.c
        there = segx.at[pl.ds(pl.multiple_of((x * 2 + c) * 8, 8), 8)]
        rcopy(there, there, sgs.at[i], sgr.at[i], p.sib).wait_recv()
    for g in range(8):
        segw[pl.ds(16 + g, 1)] = segx[pl.ds(8 * g, 1)]
    for j in (1, 2):
        k = rcopy(segw.at[pl.ds(16, 8)], segw.at[pl.ds(16 - 8 * j, 8)], sgs.at[6 + j], sgr.at[6 + j], p.at_sb(j))
        k.start()
        seg_sent.append(k)
    trig(2)
    WF.spread(3)
    trig(3)
    GB.far()
    for d in range(4):
        GB.sib(d)
    GB.end()
    WA.end()
    GO.own()
    WF.spread(1)

    for j in (1, 2):
        there = segw.at[pl.ds(16 - 8 * j, 8)]
        rcopy(there, there, sgs.at[6 + j], sgr.at[6 + j], p.sib).wait_recv()
    for k in seg_sent:
        k.wait_send()
    sq = segw[pl.ds(16, 8)]
    s1 = jnp.where(p.sb >= 1, segw[pl.ds(8, 8)], -1.0)
    s2 = jnp.where(p.sb >= 2, segw[pl.ds(0, 8)], -1.0)
    start = jnp.zeros((8, 128), F32)
    for d in range(16):
        fewer = (sq < d).astype(F32) + (s1 < d).astype(F32) + (s2 < d).astype(F32)
        count = jnp.sum(jnp.sum(fewer, axis=1, keepdims=True), axis=0, keepdims=True)
        start = start + jnp.where(sq == d, count, 0.0)
    start = start.astype(jnp.int32)
    for t in range(4):
        for h in range(3):
            for j in range(2):
                stq[pl.ds(t, 1), pl.ds(h * 256 + j * 128, 128)] = start[2 * t + j : 2 * t + j + 1]

    qg2 = jnp.concatenate([qg[...], qg[...]], axis=1)
    gqk = jnp.concatenate([qg2, qg[...], kg[...]], axis=1)

    def project(t):
        x = bo[tile(t)]
        qk = mm(x, wa[:, 0:256], NN)
        ov = mm(x, wa[:, 256:512], NN)
        qkraw[tile(t)] = qk
        n = qk * lax.rsqrt(head_mean(qk * qk) + EPS) * gqk
        c1, s1 = ctab[tile(t)], stab[tile(t)]
        c2, s2 = jnp.concatenate([c1, c1], 1), jnp.concatenate([s1, s1], 1)
        r = n * c2 + swap(n) * s2
        a0, a1 = r[:, :128], r[:, 128:]
        low = lanes((TILE, 128)) < 64
        q[0, tile(t)] = jnp.where(low, a0, 0.0).astype(BF)
        q[1, tile(t)] = jnp.where(low, pltpu.roll(a0, 64, 1), 0.0).astype(BF)
        q[2, tile(t)] = jnp.where(low, a1, 0.0).astype(BF)
        kv = jnp.where(low, pltpu.roll(a1, 64, 1), ov[:, 128:])
        kvw[ds(2048 + t * 256, 256)] = kv.astype(BF)
        kvt[8 + t] = kv.T.astype(BF)

    loop(4, project)
    kv_own = kvw.at[pl.ds(2048, 1024)]
    kv_sent = []
    for j in (1, 2):
        k = rcopy(kv_own, kvw.at[pl.ds(2048 - 1024 * j, 1024)], kvs.at[j - 1], kvr.at[j - 1], p.at_sb(j))
        k.start()
        kv_sent.append(k)

    def kv_wait(j):
        there = kvw.at[pl.ds(2048 - 1024 * j, 1024)]
        rcopy(there, there, kvs.at[j - 1], kvr.at[j - 1], p.sib).wait_recv()

        def turn(t):
            u = 8 - 4 * j + t
            kvt[u] = kvw[tile(u)].astype(F32).T.astype(BF)

        loop(4, turn)

    key_at = lax.broadcasted_iota(jnp.int32, (TILE, 3 * TILE), 0)
    scale = 0.125

    def mask_of(t, u, diag):
        ok = key_at >= stq[pl.ds(t, 1)] - u * TILE
        if diag:
            ok = ok & (key_at <= lax.rem(lanes((TILE, 3 * TILE)), TILE))
        return ok

    def forward(t, u, diag):
        k = kvw[tile(u)]
        q3 = q[:, tile(t)].reshape(3 * TILE, 128)
        s = mm(k, q3, NT)
        e = jnp.where(mask_of(t, u, diag), jnp.exp2(s * (scale * LOG2E)), 0.0).astype(BF)
        va = jnp.where(lax.broadcasted_iota(jnp.int32, (128, TILE), 0) < 64, 1.0, kvt[u].astype(F32)).astype(BF)
        new = mm(va, e, NN)
        if diag:
            acc[t] = new
        else:
            acc[t] = acc[t] + new

    loop(4, lambda t: forward(t, t + 8, True))
    GO.relay()
    loop(3, lambda i: lax.fori_loop(0, i + 1, lambda j, c: (forward(i + 1, 8 + j, False), c)[1], 0))
    GO.rest()
    kv_wait(1)
    WF.spread(2)
    WF.relay(0)
    loop(4, lambda t: forward(t, 7, False))
    loop(4, lambda t: forward(t, 6, False))
    loop(4, lambda t: forward(t, 5, False))
    loop(4, lambda t: forward(t, 4, False))
    kv_wait(2)
    WF.relay(3, 1, 2)
    for k in kv_sent:
        k.wait_send()

    def attended(t):
        a = acc[t]
        o = a[64:128] / a[0:64]
        lse[pl.ds(t, 1)] = jnp.log2(a[0:1])
        ot = jnp.concatenate([o[:, 0:256], o[:, 256:512], o[:, 512:768], jnp.zeros((64, 256), F32)], axis=0)
        o2 = ot.T
        att[tile(t)] = o2.astype(BF)

    R1 = ReduceX(p, pa, psib, phalf, pfull, rxs.at[0], rxr.at[0])

    def finish(d):
        x = lax.rem(p.x + d, 4)
        lax.fori_loop(x, 4, lambda u, c: (forward(x, u, False), c)[1], 0)
        attended(x)
        for j in range(3):
            n = pl.ds(j * 512, 512)
            pa[tile(x), n] = mm(att[tile(x)], wa[n, 256:512], NT).astype(BF)
        R1.to_sib(d)

    finish(2)
    GO.far()
    finish(1)
    R1.far()
    finish(3)
    R1.right()
    R1.left()
    finish(0)
    R1.near()
    for d in range(4):
        GO.sib(d)
    GO.end()
    m = tokens[...].astype(F32) + R1.final()
    mid[...] = m
    b2[own_rows] = (m * rms_inv(m) * ffn_gain[...]).astype(BF)
    G2 = GatherX(p, b2, gxs.at[2], gxr.at[2])
    G2.own()
    WF.end()

    def ffn(d):
        r = tile(lax.rem(p.x + d, 4))
        for lo, n in ((0, 512), (512, HP - 512)):
            gate = mm(b2[r], wf[:, lo : lo + n], NN)
            up = mm(b2[r], wf[:, HP + lo : HP + lo + n], NN)
            dh = mm(og[r], wf[:, 2 * HP + lo : 2 * HP + lo + n], NN)
            sig = jax.nn.sigmoid(gate)
            swish = gate * sig
            hid[r, lo : lo + n] = (swish * up).astype(BF)
            dg[r, lo : lo + n] = (dh * up * sig * (1.0 + gate * (1.0 - sig))).astype(BF)
            du[r, lo : lo + n] = (dh * swish).astype(BF)

    G2.sib(0)
    ffn(0)
    G2.relay()
    G2.rest()
    G2.sib(3)
    ffn(3)
    G2.far()
    G2.sib(1)
    ffn(1)
    G2.sib(2)
    G2.end()
    ffn(2)

    R2 = ReduceX(p, pa, psib, phalf, pfull, rxs.at[1], rxr.at[1])
    R3 = ReduceX(p, pa, psib, phalf, pfull, rxs.at[2], rxr.at[2])

    def back_in(d):
        r = tile(lax.rem(p.x + d, 4))
        for j in range(3):
            n = pl.ds(j * 512, 512)
            v = mm(dg[r], wf[n, 0:HP], NT) + mm(du[r], wf[n, HP : 2 * HP], NT)
            pa[r, n] = v.astype(BF)
        R2.to_sib(d)

    def branch(d):
        r = tile(lax.rem(p.x + d, 4))
        for j in range(3):
            n = pl.ds(j * 512, 512)
            pa[r, n] = mm(hid[r], wf[n, 2 * HP :], NT).astype(BF)
        R3.to_sib(d)

    def grads(cols, left, right, lo=0, hi=6):
        def body(i, carry):
            c = pl.ds(pl.multiple_of(i * 256, 256), 256)
            wf[tile(i), cols] = mm(left[:, c], right[...], TN).astype(BF)
            return carry

        lax.fori_loop(lo, hi, body, 0)

    back_in(2)
    back_in(1)
    R2.far()
    back_in(3)
    R2.right()
    R2.left()
    back_in(0)
    def reduce_ffn(g):
        cols = pl.ds(g * HP, HP)
        unit = lambda h, u: wf.at[ds(u * 96 + h * 48, 48), cols]
        return ReduceW(
            p, unit, fr.at[g], gf_mine.at[:, cols], gf_other.at[:, cols], fx.at[:, cols], wsx.at[2 + g], rfs.at[g], rfr.at[g], False
        )

    RF0, RF1, RF2 = reduce_ffn(0), reduce_ffn(1), reduce_ffn(2)
    grads(pl.ds(0, HP), b2, dg, 0, 2)
    R2.near()
    grads(pl.ds(0, HP), b2, dg, 2, 6)
    RF0.begin()

    dn = R2.final()
    m = mid[...]
    r = rms_inv(m)
    n = m * r
    e = dn * ffn_gain[...]
    dm = out_grad[...].astype(F32) + r * (e - n * jnp.mean(e * n, axis=-1, keepdims=True))
    dmid[...] = dm
    gbuf[...] = jnp.zeros_like(gbuf)
    gbuf[pl.ds(1, 1)] = jnp.sum(dn * n, axis=0, keepdims=True)
    mr[own_rows] = dm.astype(BF)
    G3 = GatherX(p, mr, gxs.at[3], gxr.at[3])
    G3.own()

    grads(pl.ds(HP, HP), b2, du, 0, 3)
    G3.relay()
    grads(pl.ds(HP, HP), b2, du, 3, 6)
    RF1.begin()
    G3.rest()
    RF0.pass_on()
    G3.sib(0)
    for d in (2, 1, 3, 0):
        branch(d)
    G3.far()
    grads(pl.ds(2 * HP, HP), og, hid)
    RF2.begin()
    RF1.pass_on()
    for d in (3, 1, 2):
        G3.sib(d)
    G3.end()
    R3.far()
    RF0.over_a()

    head_row = lax.broadcasted_iota(jnp.int32, (8, 256), 0)
    head_lane = lanes((8, 256)) // 64
    per_head = jnp.where(head_row == head_lane, 1.0, 0.0).astype(F32)

    def d_attended(t):
        d = mm(mr[tile(t)], wa[:, 256:512], NN).astype(BF).astype(F32)
        sums = mm(per_head, d * att[tile(t)].astype(F32), NT, HI)
        for h in range(3):
            dlt[pl.ds(t, 1), pl.ds(h * 256, 256)] = sums[h : h + 1]
        a0, a1 = d[:, :128], d[:, 128:]
        high = lanes((TILE, 128)) >= 64
        do[0, tile(t)] = jnp.where(high, pltpu.roll(a0, 64, 1), 0.0).astype(BF)
        do[1, tile(t)] = jnp.where(high, a0, 0.0).astype(BF)
        do[2, tile(t)] = jnp.where(high, pltpu.roll(a1, 64, 1), 0.0).astype(BF)
        acc[t] = jnp.zeros((128, 768), F32)

    loop(4, d_attended)
    R3.right()
    R3.left()
    dkv[...] = jnp.zeros_like(dkv)
    RF1.over_a()
    RF2.pass_on()

    def backward(t, u, diag):
        k = kvw[tile(u)]
        q3 = q[:, tile(t)].reshape(3 * TILE, 128)
        do3 = do[:, tile(t)].reshape(3 * TILE, 128)
        s = mm(k, q3, NT)
        pr = jnp.where(mask_of(t, u, diag), jnp.exp2(s * (scale * LOG2E) - lse[pl.ds(t, 1)]), 0.0)
        dp = mm(k, do3, NT)
        dsc = (pr * (dp - dlt[pl.ds(t, 1)])).astype(BF)
        dkv[u] = dkv[u] + mm(dsc, q3, NN) + mm(pr.astype(BF), do3, NN)
        acc[t] = acc[t] + mm(kvt[u], dsc, NN)

    def scaled(v):
        return jnp.where(lanes(v.shape) < 64, v * scale, v)

    dk_sent = []

    def dk_send(j):
        def body(t):
            dks[j - 1, tile(t)] = scaled(dkv[8 - 4 * j + t]).astype(BF)

        loop(4, body)
        k = rcopy(dks.at[j - 1], dkr.at[j - 1], kvs.at[1 + j], kvr.at[1 + j], p.at_sb(-j))
        k.start()
        dk_sent.append(k)

    loop(4, lambda i: lax.fori_loop(0, i + 1, lambda t, c: (backward(t, i, False), c)[1], 0))
    dk_send(2)
    R3.near()
    RF0.last()
    loop(4, lambda t: backward(t, 4, False))
    loop(4, lambda t: backward(t, 5, False))
    RF2.over_a()
    RF1.last()
    loop(4, lambda t: backward(t, 6, False))
    loop(4, lambda t: backward(t, 7, False))
    dk_send(1)
    result[...] = (mid[...] + R3.final()).astype(BF)
    for dev in (p.sib, p.at_x(1), p.at_x(3)):
        pl.semaphore_signal(free, inc=1, device_id=dev, device_id_type=MESH)
    loop(3, lambda i: lax.fori_loop(0, i + 1, lambda j, c: (backward(i + 1, 8 + j, False), c)[1], 0))
    RF2.last()
    RF0.end()
    RF1.end()
    loop(4, lambda t: backward(t, t + 8, True))
    RF2.end()
    for j in (1, 2):
        rcopy(dkr.at[j - 1], dkr.at[j - 1], kvs.at[1 + j], kvr.at[1 + j], p.sib).wait_recv()
    for k in dk_sent:
        k.wait_send()

    def unproject(t):
        a = acc[t][0:64]
        at = jnp.concatenate([a[:, 0:256], a[:, 256:512], a[:, 512:768], jnp.zeros((64, 256), F32)], axis=0)
        dq = at.T * scale
        dk = scaled(dkv[8 + t]) + dkr[0, tile(t)].astype(F32) + dkr[1, tile(t)].astype(F32)
        low = lanes((TILE, 128)) < 64
        d = jnp.concatenate([dq[:, :128], jnp.where(low, dq[:, 128:], pltpu.roll(dk, 64, 1))], 1)
        d = d.astype(BF).astype(F32)
        c1, s1 = ctab[tile(t)], stab[tile(t)]
        c2, s2 = jnp.concatenate([c1, c1], 1), jnp.concatenate([s1, s1], 1)
        dn = d * c2 + swap(d * s2)
        raw = qkraw[tile(t)]
        r = lax.rsqrt(head_mean(raw * raw) + EPS)
        n = raw * r
        e = dn * gqk
        dx = r * (e - n * head_mean(e * n))
        gbuf[pl.ds(2, 1), pl.ds(0, 256)] = gbuf[pl.ds(2, 1), pl.ds(0, 256)] + jnp.sum(dn * n, axis=0, keepdims=True)
        dall[tile(t), 0:256] = dx.astype(BF)
        dall[tile(t), 256:384] = jnp.zeros((TILE, 128), BF)
        dall[tile(t), 384:512] = jnp.where(low, 0.0, dk).astype(BF)

    loop(4, unproject)

    def attn_grads(i):
        c = pl.ds(pl.multiple_of(i * 384, 128), 384)
        for lo in (0, 256):
            v = mm(bo[:, c], dall[:, lo : lo + 256], TN)
            if lo:
                v = v + mm(mr[:, c], att[...], TN)
            v = v.astype(BF)
            for j in range(8):
                fr[0, j % 2, i * 4 + j // 2, :, lo : lo + 256] = v[j * 48 : j * 48 + 48]

    loop(4, attn_grads)
    RA = ReduceW(p, lambda h, u: fr.at[0, h, u, :, 0:CA], ar, ga_mine, ga_other, axb, wsx.at[5], ras, rar, True)
    RA.begin()

    pl.semaphore_wait(free, 3)
    R4 = ReduceX(p, pa, psib, phalf, pfull, rxs.at[3], rxr.at[3])
    total = [jnp.zeros((1, 512), F32)] * 3
    for d in (2, 1, 3, 0):
        x = lax.rem(p.x + d, 4)
        for j in range(3):
            n = pl.ds(j * 512, 512)
            v = mm(dall[tile(x), 0:512], wa[n, :], NT)
            pa[tile(x), n] = v.astype(BF)
            total[j] = total[j] + jnp.sum(v * bo[tile(x), n].astype(F32), axis=0, keepdims=True)
        R4.to_sib(d)
        if d == 1:
            R4.far()
        if d == 3:
            R4.right()
            R4.left()
    gbuf[pl.ds(0, 1)] = jnp.concatenate(total, axis=1) / attn_gain[...]
    sent = []
    gx[shard] = gbuf[...]
    for i, (d, cc) in enumerate(peers):
        k = rcopy(gbuf, gx.at[shard], gns.at[i], gnr.at[i], p.at_x(d, p.c if cc == 0 else 1 - p.c))
        k.start()
        sent.append(k)
    R4.near()
    RA.over_a()
    for i in range(7):
        rcopy(gx.at[i], gx.at[i], gns.at[i], gnr.at[i], p.sib).wait_recv()
    v = gx[0]
    for i in range(1, 8):
        v = v + gx[i]
    gy[p.y] = v
    for d in (1, 2, 3):
        k = rcopy(gy.at[p.y], gy.at[p.y], gns.at[6 + d], gnr.at[6 + d], p.at("y", d))
        k.start()
        sent.append(k)
    dn = R4.final()
    t = tokens[...].astype(F32)
    r = rms_inv(t)
    n = t * r
    e = dn * attn_gain[...]
    grad_tokens[...] = (dmid[...] + r * (e - n * jnp.mean(e * n, axis=-1, keepdims=True))).astype(BF)
    RA.last()
    for d in (1, 2, 3):
        rcopy(gy.at[0], gy.at[0], gns.at[6 + d], gnr.at[6 + d], p.sib).wait_recv()
    v = (gy[0] + gy[1]) + (gy[2] + gy[3])
    gz[p.z] = v
    for d in (1, 2, 3):
        k = rcopy(gz.at[p.z], gz.at[p.z], gns.at[9 + d], gnr.at[9 + d], p.at("z", d))
        k.start()
        sent.append(k)
    for d in (1, 2, 3):
        rcopy(gz.at[0], gz.at[0], gns.at[9 + d], gnr.at[9 + d], p.sib).wait_recv()
    gains[...] = (gz[0] + gz[1]) + (gz[2] + gz[3])
    for k in sent:
        k.wait_send()
    RA.end()


VMEM_LIMIT = 63 * 2**20
VM = pl.BlockSpec(memory_space=pltpu.VMEM)


def call_kernel(*args):
    S = jax.ShapeDtypeStruct
    V = pltpu.VMEM
    dma = pltpu.SemaphoreType.DMA
    outs = (
        S((128, D), BF), S((128, D), BF), S((48, CA), BF), S((48, CA), BF),
        S((48, CF), BF), S((48, CF), BF), S((8, D), F32),
    )
    scratch = [
        V((D, CA), BF), V((D, CF), BF), V((ROWS, D), BF), V((ROWS, D), BF), V((ROWS, D), BF), V((ROWS, D), BF),
        V((ROWS, HP), BF), V((ROWS, HP), BF), V((ROWS, HP), BF),
        V((3, 2, 16, 48, HP), BF), V((2, 15, 48, CA), BF), V((48, CF), BF), V((48, CA), BF),
        V((ROWS, D), BF), V((4, 128, D), BF), V((2, 64, D), BF), V((2, 128, D), BF),
        V((3, ROWS, 128), BF), V((3, ROWS, 128), BF), V((3 * ROWS, 128), BF), V((12, 128, TILE), BF),
        V((4, 128, 768), F32), V((12, TILE, 128), F32), V((2, ROWS, 128), BF), V((2, ROWS, 128), BF),
        V((ROWS, 256), BF), V((ROWS, 256), F32),
        V((128, D), F32), V((128, D), F32), V((ROWS, 128), F32), V((ROWS, 128), F32),
        V((64, 128), F32), V((24, 128), F32), V((8, 768), jnp.int32), V((8, 768), F32), V((8, 768), F32),
        V((8, D), F32), V((8, 8, D), F32), V((4, 8, D), F32), V((4, 8, D), F32),
        dma((6, 2)), dma((2, 15)), dma((2, 15)), dma((2, 15)), dma((2, 15)),
        dma((4, 14)), dma((4, 14)), dma((4, 10)), dma((4, 10)),
        dma((2, 15)), dma((2, 15)), dma((3, 2, 15)), dma((3, 2, 15)),
        dma((4,)), dma((4,)), dma((9,)), dma((9,)), dma((13,)), dma((13,)), pltpu.SemaphoreType.REGULAR,
    ]
    return pl.pallas_call(
        kernel,
        out_shape=outs,
        in_specs=[VM] * len(args),
        out_specs=(VM,) * len(outs),
        scratch_shapes=scratch,
        compiler_params=pltpu.CompilerParams(
            collective_id=0, has_side_effects=True, vmem_limit_bytes=VMEM_LIMIT
        ),
    )(*args)


def last_kernel(
    res, gtok, ga_mine, ga_other, gf_mine, gf_other, gains,
    result, grad_tokens, g_attn, g_query, g_key, g_value, g_qg, g_kg, g_out, g_ffn, g_gate, g_up, g_down,
):
    xh = lax.axis_index("xh")
    result[...] = res[...]
    grad_tokens[...] = gtok[...]
    g_attn[...] = gains[0:1]
    g_ffn[...] = gains[1:2]
    a0, a1 = gains[2:3, 0:128], gains[2:3, 128:256]
    g_qg[...] = a0[:, 0:64] + pltpu.roll(a0, 64, 1)[:, 0:64] + a1[:, 0:64]
    g_kg[...] = pltpu.roll(a1, 64, 1)[:, 0:64]
    low = lanes((48, 128)) < 64
    for base, wide, narrow in ((0, g_query, g_key), (256, g_out, g_value)):
        m = [ga_mine[:, base + j * 128 : base + j * 128 + 128].astype(F32) for j in range(2)]
        o = [ga_other[:, base + j * 128 : base + j * 128 + 128].astype(F32) for j in range(2)]
        h0 = [jnp.where(xh == 0, a, b) for a, b in zip(m, o)]
        h1 = [jnp.where(xh == 0, b, a) for a, b in zip(m, o)]
        turned = [pltpu.roll(v, 64, 1) for v in h1]
        wide[:, 0:128] = h0[0]
        wide[:, 128:256] = jnp.where(low, h0[1], turned[0])
        wide[:, 256:384] = jnp.where(low, turned[0], turned[1])
        narrow[...] = jnp.where(low, pltpu.roll(h0[1], 64, 1), h1[1])
    for at in (0, 1):

        @pl.when(xh == at)
        def _(at=at):
            first, second = (gf_mine, gf_other) if at == 0 else (gf_other, gf_mine)
            for i, out in enumerate((g_gate, g_up, g_down)):
                out[:, 0:HP] = first[:, i * HP : (i + 1) * HP].astype(F32)
                out[:, HP:] = second[:, i * HP : i * HP + HQ].astype(F32)


def call_last(*args):
    S = jax.ShapeDtypeStruct
    outs = (
        S((128, D), BF), S((128, D), BF), S((1, D), F32), S((48, 384), F32), S((48, 128), F32), S((48, 128), F32),
        S((1, 64), F32), S((1, 64), F32), S((48, 384), F32), S((1, D), F32),
        S((48, HP + HQ), F32), S((48, HP + HQ), F32), S((48, HP + HQ), F32),
    )
    return pl.pallas_call(
        last_kernel,
        out_shape=outs,
        in_specs=[VM] * len(args),
        out_specs=(VM,) * len(outs),
        compiler_params=pltpu.CompilerParams(vmem_limit_bytes=VMEM_LIMIT),
    )(*args)


def on_device(
    tokens, segments, attn_gain, w_query, w_key, w_value, query_gain, key_gain, w_out, ffn_gain,
    w_gate, w_up, w_down, out_grad,
):
    steps = np.arange(32, dtype=np.float32) * np.float32(2.0 / 64)
    freqs = np.exp(-np.log(np.float32(THETA)) * steps).astype(np.float32)
    freq = jnp.asarray(np.tile(freqs, 4)[None, :])
    parts = call_kernel(
        tokens, segments[None], attn_gain[None], ffn_gain[None], query_gain[None], key_gain[None], freq,
        w_query, w_key, w_value, w_out.T, w_gate, w_up, w_down.T, out_grad,
    )
    out = list(call_last(*parts))
    for i in (2, 6, 7, 9):
        out[i] = out[i][0]
    for i in (8, 12):
        out[i] = out[i].T
    return tuple(out)


def solution(mesh):
    finer = Mesh(mesh.devices.reshape(4, 4, 2, 2, 2), AXES)
    rows, blk, narrow = P(AXES), ("z", "y", "xh"), ("xl", "core")
    cols, turned = P(blk, narrow), P(narrow, blk)
    in_specs = (rows, rows, P(), cols, cols, cols, P(), P(), turned, P(), cols, cols, turned, rows)
    out_specs = (rows, rows, P(), cols, cols, cols, P(), P(), turned, P(), cols, cols, turned)
    return jax.shard_map(
        on_device, mesh=finer, in_specs=in_specs, out_specs=out_specs, check_vma=False
    )
```

```python
from functools import partial

import jax
import jax.numpy as jnp
import numpy as np
from jax import lax
from jax.experimental import pallas as pl
from jax.experimental.pallas import tpu as pltpu
from jax.sharding import Mesh
from jax.sharding import PartitionSpec as P

EPS = 1e-05
THETA = 1000000.0
LOG2E = 1.4426950408889634
MESH = pl.DeviceIdType.MESH
BF = jnp.bfloat16
F32 = jnp.float32
HI = lax.Precision.HIGHEST
AXES = ("z", "y", "xh", "xl", "core")

D = 1536
HP = 896
HQ = 832
CF = 3 * HP
CA = 512
ROWS = 1024
TILE = 256
NT = ((1,), (1,)), ((), ())
NN = ((1,), (0,)), ((), ())
TN = ((0,), (0,)), ((), ())


def mm(a, b, dims, precision=None):
    return lax.dot_general(a, b, dims, precision=precision, preferred_element_type=F32)


class Pos:
    def __init__(s):
        ax = lax.axis_index
        s.z, s.y, s.xh, s.xl, s.c = ax("z"), ax("y"), ax("xh"), ax("xl"), ax("core")
        s.x = s.xh * 2 + s.xl
        s.sb = s.z * 4 + s.y
        s.sib = s.at_x(0, 1 - s.c)

    def at_x(s, d, c=None):
        x = lax.rem(s.x + d, 4)
        return {"xh": x // 2, "xl": lax.rem(x, 2), "core": s.c if c is None else c}

    def at(s, axis, d):
        return {axis: lax.rem(getattr(s, axis) + d, 4)}

    def at_sb(s, d):
        t = lax.rem(s.sb + d + 16, 16)
        return {"z": t // 4, "y": lax.rem(t, 4)}


def barrier(p):
    b = pltpu.get_barrier_semaphore()
    peers = [p.at("y", 1), p.at("y", 2), p.at("y", 3), p.at("z", 1), p.at("z", 2), p.at("z", 3)]
    peers += [p.at_sb(d) for d in (1, 2, -1, -2)]
    peers += [p.at_x(d, cc) for d in (1, 2, 3) for cc in (p.c, 1 - p.c)] + [p.sib]
    for q in peers:
        pl.semaphore_signal(b, inc=1, device_id=q, device_id_type=MESH)
    pl.semaphore_wait(b, len(peers))


def rcopy(src, dst, ss, rs, dev):
    return pltpu.make_async_remote_copy(
        src_ref=src, dst_ref=dst, send_sem=ss, recv_sem=rs, device_id=dev, device_id_type=MESH
    )


def ds(start, n):
    return pl.ds(pl.multiple_of(start, 16), n)


class Half:
    def __init__(s, p, w, cols, off, a, b, ss, rs, direct):
        s.p, s.w, s.cols, s.off, s.a, s.b, s.ss, s.rs, s.direct = p, w, cols, off, a, b, ss, rs, direct
        s.sent = []

    def unit(s, ra, rb):
        ia = lax.rem(getattr(s.p, s.a) + ra, 4)
        ib = lax.rem(getattr(s.p, s.b) + rb, 4)
        zz, yy = (ia, ib) if s.a == "z" else (ib, ia)
        return s.w.at[ds((zz * 4 + yy) * 96 + s.off, 48), s.cols]

    def send(s, ra, rb, axis, d, rid):
        u = s.unit(ra, rb)
        k = rcopy(u, u, s.ss.at[len(s.sent)], s.rs.at[rid], s.p.at(axis, d))
        s.sent.append(k)
        k.start()

    def got(s, ra, rb, rid):
        u = s.unit(ra, rb)
        rcopy(u, u, s.ss.at[0], s.rs.at[rid], s.p.at(s.a, 1)).wait_recv()

    def over_b(s, ra):
        s.send(ra, 0, s.b, 1, 3 + ra)
        s.send(ra, 0, s.b, 3, 7 + ra)
        if s.direct:
            s.send(ra, 0, s.b, 2, 11 + ra)

    def own(s):
        s.send(0, 0, s.a, 1, 0)
        s.send(0, 0, s.a, 3, 1)
        s.send(0, 0, s.a, 2, 2)
        s.over_b(0)

    def spread(s, *ids):
        for ra in ids:
            s.got(ra, 0, {3: 0, 1: 1, 2: 2}[ra])
            s.over_b(ra)

    def relay(s, *ids):
        for ra in ids:
            rb, rid, d = (3, 3 + ra, 1) if ra < 2 else (1, 7 + ra, 3)
            s.got(ra, rb, rid)
            s.send(ra, rb, s.b, d, 11 + ra)

    def end(s):
        for ra in range(4):
            if s.direct or ra < 2:
                s.got(ra, 1, 7 + ra)
            if s.direct or ra >= 2:
                s.got(ra, 3, 3 + ra)
            s.got(ra, 2, 11 + ra)
        for k in s.sent:
            k.wait_send()


class Weights:
    def __init__(s, p, theirs, w, cols, xs, ss, rs, direct):
        s.p, s.theirs, s.w, s.cols, s.xs = p, theirs.at[:, cols], w, cols, xs
        s.oo, s.po = p.xh * 48, (1 - p.xh) * 48
        s.A = Half(p, w, cols, s.oo, "y", "z", ss.at[0], rs.at[0], direct)
        s.B = Half(p, w, cols, s.po, "z", "y", ss.at[1], rs.at[1], direct)

    def exchange(s):
        p = s.p
        dst = s.w.at[ds(p.sb * 96 + s.oo, 48), s.cols]
        s.xk = rcopy(s.theirs, dst, s.xs.at[0], s.xs.at[1], p.at_x(2))
        s.xk.start()

    def first(s):
        s.A.own()

    def second(s):
        p = s.p
        got = s.w.at[ds(p.sb * 96 + s.po, 48), s.cols]
        rcopy(s.theirs, got, s.xs.at[0], s.xs.at[1], p.at_x(2)).wait_recv()
        s.B.own()

    def spread(s, *ids):
        s.A.spread(*ids)
        s.B.spread(*ids)

    def relay(s, *ids):
        s.A.relay(*ids)
        s.B.relay(*ids)

    def end(s):
        s.A.end()
        s.B.end()
        s.xk.wait_send()


class GatherX:
    def __init__(s, p, buf, ss, rs):
        s.p, s.buf, s.ss, s.rs, s.sent = p, buf, ss, rs, []

    def piece(s, d, c, i):
        x = lax.rem(s.p.x + d, 4)
        return s.buf.at[ds((x * 2 + c) * 128 + i * 64, 64)]

    def send(s, d, i, dev, rid):
        u = s.piece(d, s.p.c, i)
        k = rcopy(u, u, s.ss.at[len(s.sent)], s.rs.at[rid], dev)
        s.sent.append(k)
        k.start()

    def got(s, d, c, i, rid):
        u = s.piece(d, c, i)
        rcopy(u, u, s.ss.at[0], s.rs.at[rid], s.p.sib).wait_recv()

    def own(s):
        p = s.p
        s.send(0, 0, p.at_x(1), 0)
        s.send(0, 1, p.at_x(3), 3)
        s.send(0, 0, p.sib, 6)
        s.send(0, 1, p.sib, 7)
        s.send(0, 1, p.at_x(1), 1)
        s.send(0, 0, p.at_x(3), 2)

    def relay(s):
        p = s.p
        s.got(3, p.c, 0, 0)
        s.send(3, 0, p.at_x(1), 4)
        s.send(3, 0, p.sib, 8)
        s.got(1, p.c, 1, 3)
        s.send(1, 1, p.at_x(3), 5)
        s.send(1, 1, p.sib, 11)

    def rest(s):
        p = s.p
        s.got(3, p.c, 1, 1)
        s.send(3, 1, p.sib, 9)
        s.got(1, p.c, 0, 2)
        s.send(1, 0, p.sib, 10)

    def far(s):
        p = s.p
        s.got(2, p.c, 0, 4)
        s.send(2, 0, p.sib, 12)
        s.got(2, p.c, 1, 5)
        s.send(2, 1, p.sib, 13)

    def sib(s, d):
        base = {0: 6, 3: 8, 1: 10, 2: 12}[d]
        s.got(d, 1 - s.p.c, 0, base)
        s.got(d, 1 - s.p.c, 1, base + 1)

    def end(s):
        for k in s.sent:
            k.wait_send()


class ReduceX:
    def __init__(s, p, buf, sib, half, full, ss, rs):
        s.p, s.buf, s.sib, s.half, s.full, s.ss, s.rs, s.sent = p, buf, sib, half, full, ss, rs, []

    def rows(s, d, c, lo=0, n=128):
        x = lax.rem(s.p.x + d, 4)
        return ds((x * 2 + c) * 128 + lo, n)

    def send(s, src, dst, rid, dev):
        k = rcopy(src, dst, s.ss.at[rid], s.rs.at[rid], dev)
        s.sent.append(k)
        k.start()

    def wait(s, dst, rid):
        rcopy(dst, dst, s.ss.at[rid], s.rs.at[rid], s.p.sib).wait_recv()

    def to_sib(s, d):
        s.send(s.buf.at[s.rows(d, 1 - s.p.c)], s.sib.at[d], d, s.p.sib)

    def add_sib(s, d):
        s.wait(s.sib.at[d], d)
        r = s.rows(d, s.p.c)
        s.buf[r] = (s.buf[r].astype(F32) + s.sib[d].astype(F32)).astype(BF)

    def far(s):
        s.add_sib(2)
        s.send(s.buf.at[s.rows(2, s.p.c, 0, 64)], s.half.at[0], 4, s.p.at_x(1))
        s.send(s.buf.at[s.rows(2, s.p.c, 64, 64)], s.half.at[1], 5, s.p.at_x(3))

    def right(s):
        s.add_sib(1)
        s.send(s.buf.at[s.rows(1, s.p.c, 64, 64)], s.full.at[0, 64:128], 6, s.p.at_x(1))

    def left(s):
        s.add_sib(3)
        s.send(s.buf.at[s.rows(3, s.p.c, 0, 64)], s.full.at[1, 0:64], 7, s.p.at_x(3))

    def near(s):
        s.wait(s.half.at[0], 4)
        r = s.rows(1, s.p.c, 0, 64)
        s.buf[r] = (s.buf[r].astype(F32) + s.half[0].astype(F32)).astype(BF)
        s.send(s.buf.at[r], s.full.at[0, 0:64], 8, s.p.at_x(1))
        s.wait(s.half.at[1], 5)
        r = s.rows(3, s.p.c, 64, 64)
        s.buf[r] = (s.buf[r].astype(F32) + s.half[1].astype(F32)).astype(BF)
        s.send(s.buf.at[r], s.full.at[1, 64:128], 9, s.p.at_x(3))

    def final(s):
        s.wait(s.sib.at[0], 0)
        s.wait(s.full.at[0, 64:128], 6)
        s.wait(s.full.at[1, 0:64], 7)
        s.wait(s.full.at[0, 0:64], 8)
        s.wait(s.full.at[1, 64:128], 9)
        for k in s.sent:
            k.wait_send()
        r = s.rows(0, s.p.c)
        return (s.buf[r].astype(F32) + s.sib[0].astype(F32)) + (
            s.full[0].astype(F32) + s.full[1].astype(F32)
        )


class ReduceHalf:
    def __init__(s, p, unit, a, b, rbuf, ss, rs, direct):
        s.p, s.unit, s.a, s.b, s.r, s.ss, s.rs, s.direct = p, unit, a, b, rbuf, ss, rs, direct
        s.sent = []

    def at(s, ra, rb):
        ia = lax.rem(getattr(s.p, s.a) + ra, 4)
        ib = lax.rem(getattr(s.p, s.b) + rb, 4)
        zz, yy = (ia, ib) if s.a == "z" else (ib, ia)
        return s.unit(zz * 4 + yy)

    def send(s, ra, rb, axis, d, rid):
        k = rcopy(s.at(ra, rb), s.r.at[rid], s.ss.at[len(s.sent)], s.rs.at[rid], s.p.at(axis, d))
        s.sent.append(k)
        k.start()

    def add(s, ra, rb, *rids):
        for i in rids:
            rcopy(s.r.at[i], s.r.at[i], s.ss.at[0], s.rs.at[i], s.p.at(s.a, 1)).wait_recv()
        u = s.at(ra, rb)
        v = u[...].astype(F32)
        for i in rids:
            v = v + s.r[i].astype(F32)
        u[...] = v.astype(BF)

    def begin(s):
        if s.direct:
            for rb in (2, 1, 3):
                for ra in range(4):
                    s.send(ra, rb, s.b, rb, (rb - 1) * 4 + ra)
            return
        for ra in range(4):
            s.send(ra, 2, s.b, 1 if ra < 2 else 3, 8 + ra)
        for ra in range(4):
            rb = 3 if ra < 2 else 1
            s.send(ra, rb, s.b, rb, (4 if rb == 3 else 0) + ra)

    def pass_on(s):
        for ra in range(4):
            rb = 1 if ra < 2 else 3
            s.add(ra, rb, 8 + ra)
            s.send(ra, rb, s.b, rb, (4 if rb == 3 else 0) + ra)

    def over_a(s):
        for ra in (2, 1, 3):
            s.add(ra, 0, ra, 4 + ra, *([8 + ra] if s.direct else []))
            s.send(ra, 0, s.a, ra, 11 + ra)

    def last(s):
        s.add(0, 0, 0, 4, *([8] if s.direct else []), 12, 13, 14)
        for k in s.sent:
            k.wait_send()


class ReduceW:
    def __init__(s, p, unit, rbuf, mine, other, xbuf, xs, ss, rs, direct):
        s.p, s.mine, s.other, s.xbuf, s.xs = p, mine, other, xbuf, xs
        s.own, s.far = lambda u: unit(p.xh, u), lambda u: unit(1 - p.xh, u)
        s.A = ReduceHalf(p, s.own, "y", "z", rbuf.at[0], ss.at[0], rs.at[0], direct)
        s.B = ReduceHalf(p, s.far, "z", "y", rbuf.at[1], ss.at[1], rs.at[1], direct)

    def begin(s):
        s.A.begin()
        s.B.begin()

    def pass_on(s):
        s.A.pass_on()
        s.B.pass_on()

    def over_a(s):
        s.A.over_a()
        s.B.over_a()

    def last(s):
        s.B.last()
        s.xk = rcopy(s.far(s.p.sb), s.xbuf, s.xs.at[0], s.xs.at[1], s.p.at_x(2))
        s.xk.start()
        s.A.last()
        s.mine[...] = s.own(s.p.sb)[...]

    def end(s):
        s.xk.wait_recv()
        s.xk.wait_send()
        s.other[...] = s.xbuf[...]


def lanes(shape):
    return lax.broadcasted_iota(jnp.int32, shape, len(shape) - 1)


def swap(v):
    n = v.shape[1]
    low = lax.rem(lanes(v.shape), 64) < 32
    return jnp.where(low, pltpu.roll(v, n - 32, 1), pltpu.roll(v, 32, 1))


def head_mean(v):
    n = v.shape[1]
    a = lax.broadcasted_iota(jnp.int32, (n, n), 0) // 64
    b = lax.broadcasted_iota(jnp.int32, (n, n), 1) // 64
    m = jnp.where(a == b, 1.0 / 64, 0.0).astype(F32)
    return mm(v, m, NN, HI)


def rms_inv(v):
    return lax.rsqrt(jnp.mean(v * v, axis=-1, keepdims=True) + EPS)


def loop(n, body):
    lax.fori_loop(0, n, lambda i, c: (body(i), c)[1], 0)


def tile(t, n=TILE):
    return pl.ds(pl.multiple_of(t * n, n), n)


def kernel(
    tokens, segs, attn_gain, ffn_gain, qg, kg, freq, w_query, w_key, w_value, w_out, w_gate, w_up, w_down, out_grad,
    result, grad_tokens, ga_mine, ga_other, gf_mine, gf_other, gains,
    wa, wf, bo, og, b2, mr, hid, dg, du, fr, ar, fx, axb,
    pa, psib, phalf, pfull,
    q, do, kvw, kvt, acc, dkv, dks, dkr, att, qkraw, mid, dmid, ctab, stab,
    segx, segw, stq, lse, dlt, gbuf, gx, gy, gz,
    wsx, was, war, wfs, wfr, gxs, gxr, rxs, rxr, ras, rar, rfs, rfr, kvs, kvr, sgs, sgr, gns, gnr, free,
):
    p = Pos()
    shard = p.x * 2 + p.c
    dall = dg
    own_rows = ds(shard * 128, 128)

    wrow = ds(p.sb * 96 + p.xh * 48, 48)
    low48 = lanes((48, 128)) < 64

    def two_heads(wide, narrow):
        x, k = wide[...].astype(F32), narrow[...].astype(F32)
        far = pltpu.roll(x[:, 128:384], 192, 1)
        first = (x[:, 0:128], jnp.where(low48, x[:, 128:256], pltpu.roll(k, 64, 1)))
        return first, (far[:, 0:128], jnp.where(low48, far[:, 128:], k))

    for base, wide, narrow in ((0, w_query, w_key), (256, w_out, w_value)):
        first, second = two_heads(wide, narrow)
        for j in range(2):
            cols = pl.ds(base + j * 128, 128)
            wa[wrow, cols] = jnp.where(p.xh == 0, first[j], second[j]).astype(BF)
            axb[:, cols] = jnp.where(p.xh == 0, second[j], first[j]).astype(BF)

    def put(dst, rows, half):
        for i, w in enumerate((w_gate, w_up, w_down)):
            if half == 0:
                dst[rows, i * HP : (i + 1) * HP] = w[:, 0:HP]
            else:
                dst[rows, (i + 1) * HP - 128 : (i + 1) * HP] = jnp.zeros((48, 128), BF)
                dst[rows, i * HP : i * HP + HQ] = w[:, HP:]

    for xh in (0, 1):

        @pl.when(p.xh == xh)
        def _(xh=xh):
            put(wf, wrow, xh)
            put(fx, pl.ds(0, 48), 1 - xh)

    tf = tokens[...].astype(F32)
    bo[own_rows] = (tf * rms_inv(tf) * attn_gain[...]).astype(BF)
    og[own_rows] = out_grad[...]
    seg8 = pl.ds(pl.multiple_of(shard * 8, 8), 8)
    segx[seg8] = jnp.broadcast_to(segs[...].astype(F32), (8, 128))
    barrier(p)

    WA = Weights(p, axb, wa, pl.ds(0, CA), wsx.at[0], was, war, True)
    WF = Weights(p, fx, wf, pl.ds(0, 2 * HP), wsx.at[1], wfs.at[0], wfr.at[0], False)
    WD = Weights(p, fx, wf, pl.ds(2 * HP, HP), wsx.at[6], wfs.at[1], wfr.at[1], False)
    WA.exchange()
    GB = GatherX(p, bo, gxs.at[0], gxr.at[0])
    GB.own()
    seg_sent = []
    here = segx.at[seg8]
    peers = [(d, cc) for d in range(4) for cc in range(2) if (d, cc) != (0, 0)]
    for i, (d, cc) in enumerate(peers):
        k = rcopy(here, here, sgs.at[i], sgr.at[i], p.at_x(d, p.c if cc == 0 else 1 - p.c))
        k.start()
        seg_sent.append(k)
    WA.first()
    WF.exchange()
    WD.exchange()
    WF.first()
    GO = GatherX(p, og, gxs.at[1], gxr.at[1])

    def trig(t):
        at = lax.broadcasted_iota(jnp.int32, (TILE, 128), 0) + (p.sb * ROWS + t * TILE)
        angle = at.astype(F32) * freq[...]
        sine = jnp.sin(angle)
        ctab[tile(t)] = jnp.cos(angle)
        stab[tile(t)] = jnp.where(lax.rem(lanes((TILE, 128)), 64) < 32, -sine, sine)

    trig(0)
    WA.second()
    WF.second()
    GB.relay()
    trig(1)
    WA.spread(3, 1, 2)
    GB.rest()
    for i, (d, cc) in enumerate(peers):
        x = lax.rem(p.x + 4 - d, 4)
        c = p.c if cc == 0 else 1 - p.c
        there = segx.at[pl.ds(pl.multiple_of((x * 2 + c) * 8, 8), 8)]
        rcopy(there, there, sgs.at[i], sgr.at[i], p.sib).wait_recv()
    for g in range(8):
        segw[pl.ds(16 + g, 1)] = segx[pl.ds(8 * g, 1)]
    for j in (1, 2):
        k = rcopy(segw.at[pl.ds(16, 8)], segw.at[pl.ds(16 - 8 * j, 8)], sgs.at[6 + j], sgr.at[6 + j], p.at_sb(j))
        k.start()
        seg_sent.append(k)
    trig(2)
    WF.spread(3)
    trig(3)
    GB.far()
    for d in range(4):
        GB.sib(d)
    GB.end()
    WA.end()
    GO.own()
    WF.spread(1)

    for j in (1, 2):
        there = segw.at[pl.ds(16 - 8 * j, 8)]
        rcopy(there, there, sgs.at[6 + j], sgr.at[6 + j], p.sib).wait_recv()
    for k in seg_sent:
        k.wait_send()
    sq = segw[pl.ds(16, 8)]
    s1 = jnp.where(p.sb >= 1, segw[pl.ds(8, 8)], -1.0)
    s2 = jnp.where(p.sb >= 2, segw[pl.ds(0, 8)], -1.0)
    start = jnp.zeros((8, 128), F32)
    for d in range(16):
        fewer = (sq < d).astype(F32) + (s1 < d).astype(F32) + (s2 < d).astype(F32)
        count = jnp.sum(jnp.sum(fewer, axis=1, keepdims=True), axis=0, keepdims=True)
        start = start + jnp.where(sq == d, count, 0.0)
    start = start.astype(jnp.int32)
    for t in range(4):
        for h in range(3):
            for j in range(2):
                stq[pl.ds(t, 1), pl.ds(h * 256 + j * 128, 128)] = start[2 * t + j : 2 * t + j + 1]

    qg2 = jnp.concatenate([qg[...], qg[...]], axis=1)
    gqk = jnp.concatenate([qg2, qg[...], kg[...]], axis=1)

    def project(t):
        x = bo[tile(t)]
        qk = mm(x, wa[:, 0:256], NN)
        ov = mm(x, wa[:, 256:512], NN)
        qkraw[tile(t)] = qk
        n = qk * lax.rsqrt(head_mean(qk * qk) + EPS) * gqk
        c1, s1 = ctab[tile(t)], stab[tile(t)]
        c2, s2 = jnp.concatenate([c1, c1], 1), jnp.concatenate([s1, s1], 1)
        r = n * c2 + swap(n) * s2
        a0, a1 = r[:, :128], r[:, 128:]
        low = lanes((TILE, 128)) < 64
        q[0, tile(t)] = jnp.where(low, a0, 0.0).astype(BF)
        q[1, tile(t)] = jnp.where(low, pltpu.roll(a0, 64, 1), 0.0).astype(BF)
        q[2, tile(t)] = jnp.where(low, a1, 0.0).astype(BF)
        kv = jnp.where(low, pltpu.roll(a1, 64, 1), ov[:, 128:])
        kvw[ds(2048 + t * 256, 256)] = kv.astype(BF)
        kvt[8 + t] = kv.T.astype(BF)

    loop(4, project)
    kv_own = kvw.at[pl.ds(2048, 1024)]
    kv_sent = []
    for j in (1, 2):
        k = rcopy(kv_own, kvw.at[pl.ds(2048 - 1024 * j, 1024)], kvs.at[j - 1], kvr.at[j - 1], p.at_sb(j))
        k.start()
        kv_sent.append(k)

    def kv_wait(j):
        there = kvw.at[pl.ds(2048 - 1024 * j, 1024)]
        rcopy(there, there, kvs.at[j - 1], kvr.at[j - 1], p.sib).wait_recv()

        def turn(t):
            u = 8 - 4 * j + t
            kvt[u] = kvw[tile(u)].astype(F32).T.astype(BF)

        loop(4, turn)

    key_at = lax.broadcasted_iota(jnp.int32, (TILE, 3 * TILE), 0)
    scale = 0.125

    def mask_of(t, u, diag):
        ok = key_at >= stq[pl.ds(t, 1)] - u * TILE
        if diag:
            ok = ok & (key_at <= lax.rem(lanes((TILE, 3 * TILE)), TILE))
        return ok

    def forward(t, u, diag):
        k = kvw[tile(u)]
        q3 = q[:, tile(t)].reshape(3 * TILE, 128)
        s = mm(k, q3, NT)
        e = jnp.where(mask_of(t, u, diag), jnp.exp2(s * (scale * LOG2E)), 0.0).astype(BF)
        va = jnp.where(lax.broadcasted_iota(jnp.int32, (128, TILE), 0) < 64, 1.0, kvt[u].astype(F32)).astype(BF)
        new = mm(va, e, NN)
        if diag:
            acc[t] = new
        else:
            acc[t] = acc[t] + new

    loop(4, lambda t: forward(t, t + 8, True))
    GO.relay()
    loop(3, lambda i: lax.fori_loop(0, i + 1, lambda j, c: (forward(i + 1, 8 + j, False), c)[1], 0))
    GO.rest()
    kv_wait(1)
    WF.spread(2)
    WF.relay(0)
    WD.first()
    WD.second()
    loop(4, lambda t: forward(t, 7, False))
    loop(4, lambda t: forward(t, 6, False))
    loop(4, lambda t: forward(t, 5, False))
    loop(4, lambda t: forward(t, 4, False))
    kv_wait(2)
    WF.relay(3, 1, 2)
    for k in kv_sent:
        k.wait_send()

    def attended(t):
        a = acc[t]
        o = a[64:128] / a[0:64]
        lse[pl.ds(t, 1)] = jnp.log2(a[0:1])
        ot = jnp.concatenate([o[:, 0:256], o[:, 256:512], o[:, 512:768], jnp.zeros((64, 256), F32)], axis=0)
        o2 = ot.T
        att[tile(t)] = o2.astype(BF)

    R1 = ReduceX(p, pa, psib, phalf, pfull, rxs.at[0], rxr.at[0])

    def finish(d):
        x = lax.rem(p.x + d, 4)
        lax.fori_loop(x, 4, lambda u, c: (forward(x, u, False), c)[1], 0)
        attended(x)
        for j in range(3):
            n = pl.ds(j * 512, 512)
            pa[tile(x), n] = mm(att[tile(x)], wa[n, 256:512], NT).astype(BF)
        R1.to_sib(d)

    finish(2)
    GO.far()
    finish(1)
    WD.spread(3, 1, 2)
    R1.far()
    finish(3)
    R1.right()
    R1.left()
    finish(0)
    R1.near()
    WD.relay(0)
    for d in range(4):
        GO.sib(d)
    GO.end()
    m = tokens[...].astype(F32) + R1.final()
    mid[...] = m
    b2[own_rows] = (m * rms_inv(m) * ffn_gain[...]).astype(BF)
    G2 = GatherX(p, b2, gxs.at[2], gxr.at[2])
    G2.own()
    WF.end()

    def ffn_up(d):
        r = tile(lax.rem(p.x + d, 4))
        for lo, n in ((0, 512), (512, HP - 512)):
            gate = mm(b2[r], wf[:, lo : lo + n], NN)
            up = mm(b2[r], wf[:, HP + lo : HP + lo + n], NN)
            sig = jax.nn.sigmoid(gate)
            swish = gate * sig
            hid[r, lo : lo + n] = (swish * up).astype(BF)
            dg[r, lo : lo + n] = (up * sig * (1.0 + gate * (1.0 - sig))).astype(BF)
            du[r, lo : lo + n] = swish.astype(BF)

    def ffn_down(d):
        r = tile(lax.rem(p.x + d, 4))
        for lo, n in ((0, 512), (512, HP - 512)):
            dh = mm(og[r], wf[:, 2 * HP + lo : 2 * HP + lo + n], NN)
            dg[r, lo : lo + n] = (dh * dg[r, lo : lo + n].astype(F32)).astype(BF)
            du[r, lo : lo + n] = (dh * du[r, lo : lo + n].astype(F32)).astype(BF)

    G2.sib(0)
    ffn_up(0)
    G2.relay()
    G2.rest()
    WD.relay(3, 1, 2)
    G2.sib(3)
    ffn_up(3)
    G2.far()
    G2.sib(1)
    ffn_up(1)
    G2.sib(2)
    G2.end()
    ffn_up(2)
    WD.end()

    R2 = ReduceX(p, pa, psib, phalf, pfull, rxs.at[1], rxr.at[1])
    R3 = ReduceX(p, pa, psib, phalf, pfull, rxs.at[2], rxr.at[2])

    def back_in(d):
        ffn_down(d)
        r = tile(lax.rem(p.x + d, 4))
        for j in range(3):
            n = pl.ds(j * 512, 512)
            v = mm(dg[r], wf[n, 0:HP], NT) + mm(du[r], wf[n, HP : 2 * HP], NT)
            pa[r, n] = v.astype(BF)
        R2.to_sib(d)

    def branch(d):
        r = tile(lax.rem(p.x + d, 4))
        for j in range(3):
            n = pl.ds(j * 512, 512)
            pa[r, n] = mm(hid[r], wf[n, 2 * HP :], NT).astype(BF)
        R3.to_sib(d)

    def grads(cols, left, right, lo=0, hi=6):
        def body(i, carry):
            c = pl.ds(pl.multiple_of(i * 256, 256), 256)
            wf[tile(i), cols] = mm(left[:, c], right[...], TN).astype(BF)
            return carry

        lax.fori_loop(lo, hi, body, 0)

    back_in(2)
    back_in(1)
    R2.far()
    back_in(3)
    R2.right()
    R2.left()
    back_in(0)
    def reduce_ffn(g):
        cols = pl.ds(g * HP, HP)
        unit = lambda h, u: wf.at[ds(u * 96 + h * 48, 48), cols]
        return ReduceW(
            p, unit, fr.at[g], gf_mine.at[:, cols], gf_other.at[:, cols], fx.at[:, cols], wsx.at[2 + g], rfs.at[g], rfr.at[g], False
        )

    RF0, RF1, RF2 = reduce_ffn(0), reduce_ffn(1), reduce_ffn(2)
    grads(pl.ds(0, HP), b2, dg, 0, 2)
    R2.near()
    grads(pl.ds(0, HP), b2, dg, 2, 6)
    RF0.begin()

    dn = R2.final()
    m = mid[...]
    r = rms_inv(m)
    n = m * r
    e = dn * ffn_gain[...]
    dm = out_grad[...].astype(F32) + r * (e - n * jnp.mean(e * n, axis=-1, keepdims=True))
    dmid[...] = dm
    gbuf[...] = jnp.zeros_like(gbuf)
    by_col = jnp.sum(dn * n, axis=0, keepdims=True)
    for i in range(12):
        gbuf[pl.ds(12 + i, 1)] = by_col[:, i * 128 : i * 128 + 128]
    mr[own_rows] = dm.astype(BF)
    G3 = GatherX(p, mr, gxs.at[3], gxr.at[3])
    G3.own()

    grads(pl.ds(HP, HP), b2, du, 0, 3)
    G3.relay()
    grads(pl.ds(HP, HP), b2, du, 3, 6)
    RF1.begin()
    G3.rest()
    RF0.pass_on()
    G3.sib(0)
    for d in (2, 1, 3, 0):
        branch(d)
    G3.far()
    grads(pl.ds(2 * HP, HP), og, hid)
    RF2.begin()
    RF1.pass_on()
    for d in (3, 1, 2):
        G3.sib(d)
    G3.end()
    R3.far()
    RF0.over_a()

    head_row = lax.broadcasted_iota(jnp.int32, (8, 256), 0)
    head_lane = lanes((8, 256)) // 64
    per_head = jnp.where(head_row == head_lane, 1.0, 0.0).astype(F32)

    def d_attended(t):
        d = mm(mr[tile(t)], wa[:, 256:512], NN).astype(BF).astype(F32)
        sums = mm(per_head, d * att[tile(t)].astype(F32), NT, HI)
        for h in range(3):
            dlt[pl.ds(t, 1), pl.ds(h * 256, 256)] = sums[h : h + 1]
        a0, a1 = d[:, :128], d[:, 128:]
        high = lanes((TILE, 128)) >= 64
        do[0, tile(t)] = jnp.where(high, pltpu.roll(a0, 64, 1), 0.0).astype(BF)
        do[1, tile(t)] = jnp.where(high, a0, 0.0).astype(BF)
        do[2, tile(t)] = jnp.where(high, pltpu.roll(a1, 64, 1), 0.0).astype(BF)
        acc[t] = jnp.zeros((128, 768), F32)

    loop(4, d_attended)
    R3.right()
    R3.left()
    dkv[...] = jnp.zeros_like(dkv)
    RF1.over_a()
    RF2.pass_on()

    def backward(t, u, diag):
        k = kvw[tile(u)]
        q3 = q[:, tile(t)].reshape(3 * TILE, 128)
        do3 = do[:, tile(t)].reshape(3 * TILE, 128)
        s = mm(k, q3, NT)
        pr = jnp.where(mask_of(t, u, diag), jnp.exp2(s * (scale * LOG2E) - lse[pl.ds(t, 1)]), 0.0)
        dp = mm(k, do3, NT)
        dsc = (pr * (dp - dlt[pl.ds(t, 1)])).astype(BF)
        dkv[u] = dkv[u] + mm(dsc, q3, NN) + mm(pr.astype(BF), do3, NN)
        acc[t] = acc[t] + mm(kvt[u], dsc, NN)

    def scaled(v):
        return jnp.where(lanes(v.shape) < 64, v * scale, v)

    dk_sent = []

    def dk_send(j):
        def body(t):
            dks[j - 1, tile(t)] = scaled(dkv[8 - 4 * j + t]).astype(BF)

        loop(4, body)
        k = rcopy(dks.at[j - 1], dkr.at[j - 1], kvs.at[1 + j], kvr.at[1 + j], p.at_sb(-j))
        k.start()
        dk_sent.append(k)

    loop(4, lambda i: lax.fori_loop(0, i + 1, lambda t, c: (backward(t, i, False), c)[1], 0))
    dk_send(2)
    R3.near()
    RF0.last()
    loop(4, lambda t: backward(t, 4, False))
    loop(4, lambda t: backward(t, 5, False))
    RF2.over_a()
    RF1.last()
    loop(4, lambda t: backward(t, 6, False))
    loop(4, lambda t: backward(t, 7, False))
    dk_send(1)
    result[...] = (mid[...] + R3.final()).astype(BF)
    for dev in (p.sib, p.at_x(1), p.at_x(3)):
        pl.semaphore_signal(free, inc=1, device_id=dev, device_id_type=MESH)
    loop(3, lambda i: lax.fori_loop(0, i + 1, lambda j, c: (backward(i + 1, 8 + j, False), c)[1], 0))
    RF2.last()
    RF0.end()
    RF1.end()
    loop(4, lambda t: backward(t, t + 8, True))
    RF2.end()
    for j in (1, 2):
        rcopy(dkr.at[j - 1], dkr.at[j - 1], kvs.at[1 + j], kvr.at[1 + j], p.sib).wait_recv()
    for k in dk_sent:
        k.wait_send()

    def unproject(t):
        a = acc[t][0:64]
        at = jnp.concatenate([a[:, 0:256], a[:, 256:512], a[:, 512:768], jnp.zeros((64, 256), F32)], axis=0)
        dq = at.T * scale
        dk = scaled(dkv[8 + t]) + dkr[0, tile(t)].astype(F32) + dkr[1, tile(t)].astype(F32)
        low = lanes((TILE, 128)) < 64
        d = jnp.concatenate([dq[:, :128], jnp.where(low, dq[:, 128:], pltpu.roll(dk, 64, 1))], 1)
        d = d.astype(BF).astype(F32)
        c1, s1 = ctab[tile(t)], stab[tile(t)]
        c2, s2 = jnp.concatenate([c1, c1], 1), jnp.concatenate([s1, s1], 1)
        dn = d * c2 + swap(d * s2)
        raw = qkraw[tile(t)]
        r = lax.rsqrt(head_mean(raw * raw) + EPS)
        n = raw * r
        e = dn * gqk
        dx = r * (e - n * head_mean(e * n))
        by_lane = jnp.sum(dn * n, axis=0, keepdims=True)
        for j in range(2):
            gbuf[pl.ds(24 + j, 1)] = gbuf[pl.ds(24 + j, 1)] + by_lane[:, j * 128 : j * 128 + 128]
        dall[tile(t), 0:256] = dx.astype(BF)
        dall[tile(t), 256:384] = jnp.zeros((TILE, 128), BF)
        dall[tile(t), 384:512] = jnp.where(low, 0.0, dk).astype(BF)

    def attn_grads(i):
        c = pl.ds(pl.multiple_of(i * 384, 128), 384)
        for lo in (0, 256):
            v = mm(bo[:, c], dall[:, lo : lo + 256], TN)
            if lo:
                v = v + mm(mr[:, c], att[...], TN)
            v = v.astype(BF)
            for j in range(8):
                fr[0, j % 2, i * 4 + j // 2, :, lo : lo + 256] = v[j * 48 : j * 48 + 48]

    pl.semaphore_wait(free, 3)
    R4 = ReduceX(p, pa, psib, phalf, pfull, rxs.at[3], rxr.at[3])
    total = [jnp.zeros((1, 512), F32)] * 3
    for d in (2, 1, 3, 0):
        x = lax.rem(p.x + d, 4)
        unproject(x)
        for j in range(3):
            n = pl.ds(j * 512, 512)
            v = mm(dall[tile(x), 0:512], wa[n, :], NT)
            pa[tile(x), n] = v.astype(BF)
            total[j] = total[j] + jnp.sum(v * bo[tile(x), n].astype(F32), axis=0, keepdims=True)
        R4.to_sib(d)
        if d == 1:
            R4.far()
        if d == 3:
            R4.right()
            R4.left()
    for i in range(12):
        part = total[i // 4][:, i % 4 * 128 : i % 4 * 128 + 128]
        gbuf[pl.ds(i, 1)] = part / attn_gain[:, i * 128 : i * 128 + 128]
    sent = []
    gx[shard] = gbuf[...]
    for i, (d, cc) in enumerate(peers):
        k = rcopy(gbuf, gx.at[shard], gns.at[i], gnr.at[i], p.at_x(d, p.c if cc == 0 else 1 - p.c))
        k.start()
        sent.append(k)
    R4.near()
    loop(4, attn_grads)
    RA = ReduceW(p, lambda h, u: fr.at[0, h, u, :, 0:CA], ar, ga_mine, ga_other, axb, wsx.at[5], ras, rar, True)
    RA.begin()
    for i in range(7):
        rcopy(gx.at[i], gx.at[i], gns.at[i], gnr.at[i], p.sib).wait_recv()
    v = gx[0]
    for i in range(1, 8):
        v = v + gx[i]
    gy[p.y] = v
    for d in (1, 2, 3):
        k = rcopy(gy.at[p.y], gy.at[p.y], gns.at[6 + d], gnr.at[6 + d], p.at("y", d))
        k.start()
        sent.append(k)
    dn = R4.final()
    t = tokens[...].astype(F32)
    r = rms_inv(t)
    n = t * r
    e = dn * attn_gain[...]
    grad_tokens[...] = (dmid[...] + r * (e - n * jnp.mean(e * n, axis=-1, keepdims=True))).astype(BF)
    RA.over_a()
    for d in (1, 2, 3):
        rcopy(gy.at[0], gy.at[0], gns.at[6 + d], gnr.at[6 + d], p.sib).wait_recv()
    v = (gy[0] + gy[1]) + (gy[2] + gy[3])
    gz[p.z] = v
    for d in (1, 2, 3):
        k = rcopy(gz.at[p.z], gz.at[p.z], gns.at[9 + d], gnr.at[9 + d], p.at("z", d))
        k.start()
        sent.append(k)
    RA.last()
    for d in (1, 2, 3):
        rcopy(gz.at[0], gz.at[0], gns.at[9 + d], gnr.at[9 + d], p.sib).wait_recv()
    gains[...] = (gz[0] + gz[1]) + (gz[2] + gz[3])
    for k in sent:
        k.wait_send()
    RA.end()


VMEM_LIMIT = 63 * 2**20
VM = pl.BlockSpec(memory_space=pltpu.VMEM)


def call_kernel(*args):
    S = jax.ShapeDtypeStruct
    V = pltpu.VMEM
    dma = pltpu.SemaphoreType.DMA
    outs = (
        S((128, D), BF), S((128, D), BF), S((48, CA), BF), S((48, CA), BF),
        S((48, CF), BF), S((48, CF), BF), S((32, 128), F32),
    )
    scratch = [
        V((D, CA), BF), V((D, CF), BF), V((ROWS, D), BF), V((ROWS, D), BF), V((ROWS, D), BF), V((ROWS, D), BF),
        V((ROWS, HP), BF), V((ROWS, HP), BF), V((ROWS, HP), BF),
        V((3, 2, 16, 48, HP), BF), V((2, 15, 48, CA), BF), V((48, CF), BF), V((48, CA), BF),
        V((ROWS, D), BF), V((4, 128, D), BF), V((2, 64, D), BF), V((2, 128, D), BF),
        V((3, ROWS, 128), BF), V((3, ROWS, 128), BF), V((3 * ROWS, 128), BF), V((12, 128, TILE), BF),
        V((4, 128, 768), F32), V((12, TILE, 128), F32), V((2, ROWS, 128), BF), V((2, ROWS, 128), BF),
        V((ROWS, 256), BF), V((ROWS, 256), F32),
        V((128, D), F32), V((128, D), F32), V((ROWS, 128), F32), V((ROWS, 128), F32),
        V((64, 128), F32), V((24, 128), F32), V((8, 768), jnp.int32), V((8, 768), F32), V((8, 768), F32),
        V((32, 128), F32), V((8, 32, 128), F32), V((4, 32, 128), F32), V((4, 32, 128), F32),
        dma((7, 2)), dma((2, 15)), dma((2, 15)), dma((2, 2, 15)), dma((2, 2, 15)),
        dma((4, 14)), dma((4, 14)), dma((4, 10)), dma((4, 10)),
        dma((2, 15)), dma((2, 15)), dma((3, 2, 15)), dma((3, 2, 15)),
        dma((4,)), dma((4,)), dma((9,)), dma((9,)), dma((13,)), dma((13,)), pltpu.SemaphoreType.REGULAR,
    ]
    return pl.pallas_call(
        kernel,
        out_shape=outs,
        in_specs=[VM] * len(args),
        out_specs=(VM,) * len(outs),
        scratch_shapes=scratch,
        compiler_params=pltpu.CompilerParams(
            collective_id=0, has_side_effects=True, vmem_limit_bytes=VMEM_LIMIT
        ),
    )(*args)


def last_kernel(
    res, gtok, ga_mine, ga_other, gf_mine, gf_other, gains,
    result, grad_tokens, g_attn, g_query, g_key, g_value, g_qg, g_kg, g_out, g_ffn, g_gate, g_up, g_down,
):
    xh = lax.axis_index("xh")
    result[...] = res[...]
    grad_tokens[...] = gtok[...]
    for i in range(12):
        g_attn[:, i * 128 : i * 128 + 128] = gains[i : i + 1]
        g_ffn[:, i * 128 : i * 128 + 128] = gains[12 + i : 13 + i]
    a0, a1 = gains[24:25], gains[25:26]
    g_qg[...] = a0[:, 0:64] + pltpu.roll(a0, 64, 1)[:, 0:64] + a1[:, 0:64]
    g_kg[...] = pltpu.roll(a1, 64, 1)[:, 0:64]
    low = lanes((48, 128)) < 64
    for base, wide, narrow in ((0, g_query, g_key), (256, g_out, g_value)):
        m = [ga_mine[:, base + j * 128 : base + j * 128 + 128].astype(F32) for j in range(2)]
        o = [ga_other[:, base + j * 128 : base + j * 128 + 128].astype(F32) for j in range(2)]
        h0 = [jnp.where(xh == 0, a, b) for a, b in zip(m, o)]
        h1 = [jnp.where(xh == 0, b, a) for a, b in zip(m, o)]
        turned = [pltpu.roll(v, 64, 1) for v in h1]
        wide[:, 0:128] = h0[0]
        wide[:, 128:256] = jnp.where(low, h0[1], turned[0])
        wide[:, 256:384] = jnp.where(low, turned[0], turned[1])
        narrow[...] = jnp.where(low, pltpu.roll(h0[1], 64, 1), h1[1])
    for at in (0, 1):

        @pl.when(xh == at)
        def _(at=at):
            first, second = (gf_mine, gf_other) if at == 0 else (gf_other, gf_mine)
            for i, out in enumerate((g_gate, g_up, g_down)):
                out[:, 0:HP] = first[:, i * HP : (i + 1) * HP].astype(F32)
                out[:, HP:] = second[:, i * HP : i * HP + HQ].astype(F32)


def call_last(*args):
    S = jax.ShapeDtypeStruct
    outs = (
        S((128, D), BF), S((128, D), BF), S((1, D), F32), S((48, 384), F32), S((48, 128), F32), S((48, 128), F32),
        S((1, 64), F32), S((1, 64), F32), S((48, 384), F32), S((1, D), F32),
        S((48, HP + HQ), F32), S((48, HP + HQ), F32), S((48, HP + HQ), F32),
    )
    return pl.pallas_call(
        last_kernel,
        out_shape=outs,
        in_specs=[VM] * len(args),
        out_specs=(VM,) * len(outs),
        compiler_params=pltpu.CompilerParams(vmem_limit_bytes=VMEM_LIMIT),
    )(*args)


def on_device(
    tokens, segments, attn_gain, w_query, w_key, w_value, query_gain, key_gain, w_out, ffn_gain,
    w_gate, w_up, w_down, out_grad,
):
    steps = np.arange(32, dtype=np.float32) * np.float32(2.0 / 64)
    freqs = np.exp(-np.log(np.float32(THETA)) * steps).astype(np.float32)
    freq = jnp.asarray(np.tile(freqs, 4)[None, :])
    parts = call_kernel(
        tokens, segments[None], attn_gain[None], ffn_gain[None], query_gain[None], key_gain[None], freq,
        w_query, w_key, w_value, w_out.T, w_gate, w_up, w_down.T, out_grad,
    )
    out = list(call_last(*parts))
    for i in (2, 6, 7, 9):
        out[i] = out[i][0]
    for i in (8, 12):
        out[i] = out[i].T
    return tuple(out)


def solution(mesh):
    finer = Mesh(mesh.devices.reshape(4, 4, 2, 2, 2), AXES)
    rows, blk, narrow = P(AXES), ("z", "y", "xh"), ("xl", "core")
    cols, turned = P(blk, narrow), P(narrow, blk)
    in_specs = (rows, rows, P(), cols, cols, cols, P(), P(), turned, P(), cols, cols, turned, rows)
    out_specs = (rows, rows, P(), cols, cols, cols, P(), P(), turned, P(), cols, cols, turned)
    return jax.shard_map(
        on_device, mesh=finer, in_specs=in_specs, out_specs=out_specs, check_vma=False
    )
```

```python
from functools import partial

import jax
import jax.numpy as jnp
import numpy as np
from jax import lax
from jax.experimental import pallas as pl
from jax.experimental.pallas import tpu as pltpu
from jax.sharding import Mesh
from jax.sharding import PartitionSpec as P

EPS = 1e-05
THETA = 1000000.0
LOG2E = 1.4426950408889634
MESH = pl.DeviceIdType.MESH
BF = jnp.bfloat16
F32 = jnp.float32
HI = lax.Precision.HIGHEST
AXES = ("z", "y", "xh", "xl", "core")

D = 1536
HP = 896
HQ = 832
CF = 3 * HP
CA = 512
ROWS = 1024
TILE = 256
NT = ((1,), (1,)), ((), ())
NN = ((1,), (0,)), ((), ())
TN = ((0,), (0,)), ((), ())


def mm(a, b, dims, precision=None):
    return lax.dot_general(a, b, dims, precision=precision, preferred_element_type=F32)


class Pos:
    def __init__(s):
        ax = lax.axis_index
        s.z, s.y, s.xh, s.xl, s.c = ax("z"), ax("y"), ax("xh"), ax("xl"), ax("core")
        s.x = s.xh * 2 + s.xl
        s.sb = s.z * 4 + s.y
        s.sib = s.at_x(0, 1 - s.c)

    def at_x(s, d, c=None):
        x = lax.rem(s.x + d, 4)
        return {"xh": x // 2, "xl": lax.rem(x, 2), "core": s.c if c is None else c}

    def at(s, axis, d):
        return {axis: lax.rem(getattr(s, axis) + d, 4)}

    def at_sb(s, d):
        t = lax.rem(s.sb + d + 16, 16)
        return {"z": t // 4, "y": lax.rem(t, 4)}


def barrier(p):
    b = pltpu.get_barrier_semaphore()
    peers = [p.at("y", 1), p.at("y", 2), p.at("y", 3), p.at("z", 1), p.at("z", 2), p.at("z", 3)]
    peers += [p.at_sb(d) for d in (1, 2, -1, -2)]
    peers += [p.at_x(d, cc) for d in (1, 2, 3) for cc in (p.c, 1 - p.c)] + [p.sib]
    for q in peers:
        pl.semaphore_signal(b, inc=1, device_id=q, device_id_type=MESH)
    return lambda: pl.semaphore_wait(b, len(peers))


def rcopy(src, dst, ss, rs, dev):
    return pltpu.make_async_remote_copy(
        src_ref=src, dst_ref=dst, send_sem=ss, recv_sem=rs, device_id=dev, device_id_type=MESH
    )


def ds(start, n):
    return pl.ds(pl.multiple_of(start, 16), n)


class Half:
    def __init__(s, p, w, cols, off, a, b, ss, rs, direct):
        s.p, s.w, s.cols, s.off, s.a, s.b, s.ss, s.rs, s.direct = p, w, cols, off, a, b, ss, rs, direct
        s.sent = []

    def unit(s, ra, rb):
        ia = lax.rem(getattr(s.p, s.a) + ra, 4)
        ib = lax.rem(getattr(s.p, s.b) + rb, 4)
        zz, yy = (ia, ib) if s.a == "z" else (ib, ia)
        return s.w.at[ds((zz * 4 + yy) * 96 + s.off, 48), s.cols]

    def send(s, ra, rb, axis, d, rid):
        u = s.unit(ra, rb)
        k = rcopy(u, u, s.ss.at[len(s.sent)], s.rs.at[rid], s.p.at(axis, d))
        s.sent.append(k)
        k.start()

    def got(s, ra, rb, rid):
        u = s.unit(ra, rb)
        rcopy(u, u, s.ss.at[0], s.rs.at[rid], s.p.at(s.a, 1)).wait_recv()

    def over_b(s, ra):
        s.send(ra, 0, s.b, 1, 3 + ra)
        s.send(ra, 0, s.b, 3, 7 + ra)
        if s.direct:
            s.send(ra, 0, s.b, 2, 11 + ra)

    def own(s):
        s.send(0, 0, s.a, 1, 0)
        s.send(0, 0, s.a, 3, 1)
        s.send(0, 0, s.a, 2, 2)
        s.over_b(0)

    def spread(s, *ids):
        for ra in ids:
            s.got(ra, 0, {3: 0, 1: 1, 2: 2}[ra])
            s.over_b(ra)

    def relay(s, *ids):
        for ra in ids:
            rb, rid, d = (3, 3 + ra, 1) if ra < 2 else (1, 7 + ra, 3)
            s.got(ra, rb, rid)
            s.send(ra, rb, s.b, d, 11 + ra)

    def end(s):
        for ra in range(4):
            if s.direct or ra < 2:
                s.got(ra, 1, 7 + ra)
            if s.direct or ra >= 2:
                s.got(ra, 3, 3 + ra)
            s.got(ra, 2, 11 + ra)
        for k in s.sent:
            k.wait_send()


class Weights:
    def __init__(s, p, theirs, w, cols, xs, ss, rs, direct):
        s.p, s.theirs, s.w, s.cols, s.xs = p, theirs.at[:, cols], w, cols, xs
        s.oo, s.po = p.xh * 48, (1 - p.xh) * 48
        s.A = Half(p, w, cols, s.oo, "y", "z", ss.at[0], rs.at[0], direct)
        s.B = Half(p, w, cols, s.po, "z", "y", ss.at[1], rs.at[1], direct)

    def exchange(s):
        p = s.p
        dst = s.w.at[ds(p.sb * 96 + s.oo, 48), s.cols]
        s.xk = rcopy(s.theirs, dst, s.xs.at[0], s.xs.at[1], p.at_x(2))
        s.xk.start()

    def first(s):
        s.A.own()

    def second(s):
        p = s.p
        got = s.w.at[ds(p.sb * 96 + s.po, 48), s.cols]
        rcopy(s.theirs, got, s.xs.at[0], s.xs.at[1], p.at_x(2)).wait_recv()
        s.B.own()

    def spread(s, *ids):
        s.A.spread(*ids)
        s.B.spread(*ids)

    def relay(s, *ids):
        s.A.relay(*ids)
        s.B.relay(*ids)

    def end(s):
        s.A.end()
        s.B.end()
        s.xk.wait_send()


class GatherX:
    def __init__(s, p, buf, ss, rs):
        s.p, s.buf, s.ss, s.rs, s.sent = p, buf, ss, rs, []

    def piece(s, d, c, i):
        x = lax.rem(s.p.x + d, 4)
        return s.buf.at[ds((x * 2 + c) * 128 + i * 64, 64)]

    def send(s, d, i, dev, rid):
        u = s.piece(d, s.p.c, i)
        k = rcopy(u, u, s.ss.at[len(s.sent)], s.rs.at[rid], dev)
        s.sent.append(k)
        k.start()

    def got(s, d, c, i, rid):
        u = s.piece(d, c, i)
        rcopy(u, u, s.ss.at[0], s.rs.at[rid], s.p.sib).wait_recv()

    def own(s):
        p = s.p
        s.send(0, 0, p.at_x(1), 0)
        s.send(0, 1, p.at_x(3), 3)
        s.send(0, 0, p.sib, 6)
        s.send(0, 1, p.sib, 7)
        s.send(0, 1, p.at_x(1), 1)
        s.send(0, 0, p.at_x(3), 2)

    def relay(s):
        p = s.p
        s.got(3, p.c, 0, 0)
        s.send(3, 0, p.at_x(1), 4)
        s.send(3, 0, p.sib, 8)
        s.got(1, p.c, 1, 3)
        s.send(1, 1, p.at_x(3), 5)
        s.send(1, 1, p.sib, 11)

    def rest(s):
        p = s.p
        s.got(3, p.c, 1, 1)
        s.send(3, 1, p.sib, 9)
        s.got(1, p.c, 0, 2)
        s.send(1, 0, p.sib, 10)

    def far(s):
        p = s.p
        s.got(2, p.c, 0, 4)
        s.send(2, 0, p.sib, 12)
        s.got(2, p.c, 1, 5)
        s.send(2, 1, p.sib, 13)

    def sib(s, d):
        base = {0: 6, 3: 8, 1: 10, 2: 12}[d]
        s.got(d, 1 - s.p.c, 0, base)
        s.got(d, 1 - s.p.c, 1, base + 1)

    def end(s):
        for k in s.sent:
            k.wait_send()


class ReduceX:
    def __init__(s, p, buf, sib, half, full, ss, rs):
        s.p, s.buf, s.sib, s.half, s.full, s.ss, s.rs, s.sent = p, buf, sib, half, full, ss, rs, []

    def rows(s, d, c, lo=0, n=128):
        x = lax.rem(s.p.x + d, 4)
        return ds((x * 2 + c) * 128 + lo, n)

    def send(s, src, dst, rid, dev):
        k = rcopy(src, dst, s.ss.at[rid], s.rs.at[rid], dev)
        s.sent.append(k)
        k.start()

    def wait(s, dst, rid):
        rcopy(dst, dst, s.ss.at[rid], s.rs.at[rid], s.p.sib).wait_recv()

    def to_sib(s, d):
        s.send(s.buf.at[s.rows(d, 1 - s.p.c)], s.sib.at[d], d, s.p.sib)

    def add_sib(s, d):
        s.wait(s.sib.at[d], d)
        r = s.rows(d, s.p.c)
        s.buf[r] = (s.buf[r].astype(F32) + s.sib[d].astype(F32)).astype(BF)

    def far(s):
        s.add_sib(2)
        s.send(s.buf.at[s.rows(2, s.p.c, 0, 64)], s.half.at[0], 4, s.p.at_x(1))
        s.send(s.buf.at[s.rows(2, s.p.c, 64, 64)], s.half.at[1], 5, s.p.at_x(3))

    def right(s):
        s.add_sib(1)
        s.send(s.buf.at[s.rows(1, s.p.c, 64, 64)], s.full.at[0, 64:128], 6, s.p.at_x(1))

    def left(s):
        s.add_sib(3)
        s.send(s.buf.at[s.rows(3, s.p.c, 0, 64)], s.full.at[1, 0:64], 7, s.p.at_x(3))

    def near(s):
        s.wait(s.half.at[0], 4)
        r = s.rows(1, s.p.c, 0, 64)
        s.buf[r] = (s.buf[r].astype(F32) + s.half[0].astype(F32)).astype(BF)
        s.send(s.buf.at[r], s.full.at[0, 0:64], 8, s.p.at_x(1))
        s.wait(s.half.at[1], 5)
        r = s.rows(3, s.p.c, 64, 64)
        s.buf[r] = (s.buf[r].astype(F32) + s.half[1].astype(F32)).astype(BF)
        s.send(s.buf.at[r], s.full.at[1, 64:128], 9, s.p.at_x(3))

    def final(s):
        s.wait(s.sib.at[0], 0)
        s.wait(s.full.at[0, 64:128], 6)
        s.wait(s.full.at[1, 0:64], 7)
        s.wait(s.full.at[0, 0:64], 8)
        s.wait(s.full.at[1, 64:128], 9)
        for k in s.sent:
            k.wait_send()
        r = s.rows(0, s.p.c)
        return (s.buf[r].astype(F32) + s.sib[0].astype(F32)) + (
            s.full[0].astype(F32) + s.full[1].astype(F32)
        )


class ReduceHalf:
    def __init__(s, p, unit, a, b, rbuf, ss, rs, direct):
        s.p, s.unit, s.a, s.b, s.r, s.ss, s.rs, s.direct = p, unit, a, b, rbuf, ss, rs, direct
        s.sent = []

    def at(s, ra, rb):
        ia = lax.rem(getattr(s.p, s.a) + ra, 4)
        ib = lax.rem(getattr(s.p, s.b) + rb, 4)
        zz, yy = (ia, ib) if s.a == "z" else (ib, ia)
        return s.unit(zz * 4 + yy)

    def send(s, ra, rb, axis, d, rid):
        k = rcopy(s.at(ra, rb), s.r.at[rid], s.ss.at[len(s.sent)], s.rs.at[rid], s.p.at(axis, d))
        s.sent.append(k)
        k.start()

    def add(s, ra, rb, *rids):
        for i in rids:
            rcopy(s.r.at[i], s.r.at[i], s.ss.at[0], s.rs.at[i], s.p.at(s.a, 1)).wait_recv()
        u = s.at(ra, rb)
        v = u[...].astype(F32)
        for i in rids:
            v = v + s.r[i].astype(F32)
        u[...] = v.astype(BF)

    def begin(s):
        if s.direct:
            for rb in (2, 1, 3):
                for ra in range(4):
                    s.send(ra, rb, s.b, rb, (rb - 1) * 4 + ra)
            return
        for ra in range(4):
            s.send(ra, 2, s.b, 1 if ra < 2 else 3, 8 + ra)
        for ra in range(4):
            rb = 3 if ra < 2 else 1
            s.send(ra, rb, s.b, rb, (4 if rb == 3 else 0) + ra)

    def pass_on(s):
        for ra in range(4):
            rb = 1 if ra < 2 else 3
            s.add(ra, rb, 8 + ra)
            s.send(ra, rb, s.b, rb, (4 if rb == 3 else 0) + ra)

    def over_a(s):
        for ra in (2, 1, 3):
            s.add(ra, 0, ra, 4 + ra, *([8 + ra] if s.direct else []))
            s.send(ra, 0, s.a, ra, 11 + ra)

    def last(s):
        s.add(0, 0, 0, 4, *([8] if s.direct else []), 12, 13, 14)
        for k in s.sent:
            k.wait_send()


class ReduceW:
    def __init__(s, p, unit, rbuf, mine, other, xbuf, xs, ss, rs, direct):
        s.p, s.mine, s.other, s.xbuf, s.xs = p, mine, other, xbuf, xs
        s.own, s.far = lambda u: unit(p.xh, u), lambda u: unit(1 - p.xh, u)
        s.A = ReduceHalf(p, s.own, "y", "z", rbuf.at[0], ss.at[0], rs.at[0], direct)
        s.B = ReduceHalf(p, s.far, "z", "y", rbuf.at[1], ss.at[1], rs.at[1], direct)

    def begin(s):
        s.A.begin()
        s.B.begin()

    def pass_on(s):
        s.A.pass_on()
        s.B.pass_on()

    def over_a(s):
        s.A.over_a()
        s.B.over_a()

    def last(s):
        s.B.last()
        s.xk = rcopy(s.far(s.p.sb), s.xbuf, s.xs.at[0], s.xs.at[1], s.p.at_x(2))
        s.xk.start()
        s.A.last()
        s.mine[...] = s.own(s.p.sb)[...]

    def end(s):
        s.xk.wait_recv()
        s.xk.wait_send()
        s.other[...] = s.xbuf[...]


def lanes(shape):
    return lax.broadcasted_iota(jnp.int32, shape, len(shape) - 1)


def swap(v):
    n = v.shape[1]
    low = lax.rem(lanes(v.shape), 64) < 32
    return jnp.where(low, pltpu.roll(v, n - 32, 1), pltpu.roll(v, 32, 1))


def head_mean(v):
    n = v.shape[1]
    a = lax.broadcasted_iota(jnp.int32, (n, n), 0) // 64
    b = lax.broadcasted_iota(jnp.int32, (n, n), 1) // 64
    m = jnp.where(a == b, 1.0 / 64, 0.0).astype(F32)
    return mm(v, m, NN, HI)


def rms_inv(v):
    return lax.rsqrt(jnp.mean(v * v, axis=-1, keepdims=True) + EPS)


def loop(n, body):
    lax.fori_loop(0, n, lambda i, c: (body(i), c)[1], 0)


def tile(t, n=TILE):
    return pl.ds(pl.multiple_of(t * n, n), n)


def kernel(
    tokens, segs, gain_rows, qg, kg, freq, w_query, w_key, w_value, w_out, w_gate, w_up, w_down, out_grad,
    result, grad_tokens, ga_mine, ga_other, gf_mine, gf_other, gains,
    wa, wf, bo, og, b2, mr, hid, dg, du, fr, ar, fx, axb,
    pa, psib, phalf, pfull,
    q, do, kvw, kvt, acc, dkv, dks, dkr, att, qkraw, mid, dmid, ctab, stab,
    segx, segw, stq, lse, dlt, gbuf, gx, gy, gz,
    wsx, was, war, wfs, wfr, gxs, gxr, rxs, rxr, ras, rar, rfs, rfr, kvs, kvr, sgs, sgr, gns, gnr, free,
):
    p = Pos()
    all_here = barrier(p)
    attn_gain, ffn_gain = gain_rows.at[0:1], gain_rows.at[1:2]
    shard = p.x * 2 + p.c
    dall = dg
    own_rows = ds(shard * 128, 128)

    wrow = ds(p.sb * 96 + p.xh * 48, 48)
    low48 = lanes((48, 128)) < 64

    def two_heads(wide, narrow):
        x, k = wide[...].astype(F32), narrow[...].astype(F32)
        far = pltpu.roll(x[:, 128:384], 192, 1)
        first = (x[:, 0:128], jnp.where(low48, x[:, 128:256], pltpu.roll(k, 64, 1)))
        return first, (far[:, 0:128], jnp.where(low48, far[:, 128:], k))

    for base, wide, narrow in ((0, w_query, w_key), (256, w_out, w_value)):
        first, second = two_heads(wide, narrow)
        for j in range(2):
            cols = pl.ds(base + j * 128, 128)
            wa[wrow, cols] = jnp.where(p.xh == 0, first[j], second[j]).astype(BF)
            axb[:, cols] = jnp.where(p.xh == 0, second[j], first[j]).astype(BF)

    def put(dst, rows, half):
        for i, w in enumerate((w_gate, w_up, w_down)):
            if half == 0:
                dst[rows, i * HP : (i + 1) * HP] = w[:, 0:HP]
            else:
                dst[rows, (i + 1) * HP - 128 : (i + 1) * HP] = jnp.zeros((48, 128), BF)
                dst[rows, i * HP : i * HP + HQ] = w[:, HP:]

    for xh in (0, 1):

        @pl.when(p.xh == xh)
        def _(xh=xh):
            put(wf, wrow, xh)
            put(fx, pl.ds(0, 48), 1 - xh)

    tf = tokens[...].astype(F32)
    bo[own_rows] = (tf * rms_inv(tf) * attn_gain[...]).astype(BF)
    og[own_rows] = out_grad[...]
    seg8 = pl.ds(pl.multiple_of(shard * 8, 8), 8)
    segx[seg8] = jnp.broadcast_to(segs[...].astype(F32), (8, 128))
    all_here()

    WA = Weights(p, axb, wa, pl.ds(0, CA), wsx.at[0], was, war, True)
    WF = Weights(p, fx, wf, pl.ds(0, 2 * HP), wsx.at[1], wfs.at[0], wfr.at[0], False)
    WD = Weights(p, fx, wf, pl.ds(2 * HP, HP), wsx.at[6], wfs.at[1], wfr.at[1], False)
    WA.exchange()
    GB = GatherX(p, bo, gxs.at[0], gxr.at[0])
    GB.own()
    seg_sent = []
    here = segx.at[seg8]
    peers = [(d, cc) for d in range(4) for cc in range(2) if (d, cc) != (0, 0)]
    for i, (d, cc) in enumerate(peers):
        k = rcopy(here, here, sgs.at[i], sgr.at[i], p.at_x(d, p.c if cc == 0 else 1 - p.c))
        k.start()
        seg_sent.append(k)
    WA.first()
    WF.exchange()
    WD.exchange()
    WF.first()
    GO = GatherX(p, og, gxs.at[1], gxr.at[1])

    def trig(t):
        at = lax.broadcasted_iota(jnp.int32, (TILE, 128), 0) + (p.sb * ROWS + t * TILE)
        angle = at.astype(F32) * freq[...]
        sine = jnp.sin(angle)
        ctab[tile(t)] = jnp.cos(angle)
        stab[tile(t)] = jnp.where(lax.rem(lanes((TILE, 128)), 64) < 32, -sine, sine)

    trig(0)
    WA.second()
    WF.second()
    GB.relay()
    trig(1)
    WA.spread(3, 1, 2)
    GB.rest()
    for i, (d, cc) in enumerate(peers):
        x = lax.rem(p.x + 4 - d, 4)
        c = p.c if cc == 0 else 1 - p.c
        there = segx.at[pl.ds(pl.multiple_of((x * 2 + c) * 8, 8), 8)]
        rcopy(there, there, sgs.at[i], sgr.at[i], p.sib).wait_recv()
    for g in range(8):
        segw[pl.ds(16 + g, 1)] = segx[pl.ds(8 * g, 1)]
    for j in (1, 2):
        k = rcopy(segw.at[pl.ds(16, 8)], segw.at[pl.ds(16 - 8 * j, 8)], sgs.at[6 + j], sgr.at[6 + j], p.at_sb(j))
        k.start()
        seg_sent.append(k)
    trig(2)
    WF.spread(3)
    trig(3)
    GB.far()
    for d in range(4):
        GB.sib(d)
    GB.end()
    WA.end()
    GO.own()
    WF.spread(1)

    for j in (1, 2):
        there = segw.at[pl.ds(16 - 8 * j, 8)]
        rcopy(there, there, sgs.at[6 + j], sgr.at[6 + j], p.sib).wait_recv()
    for k in seg_sent:
        k.wait_send()
    sq = segw[pl.ds(16, 8)]
    s1 = jnp.where(p.sb >= 1, segw[pl.ds(8, 8)], -1.0)
    s2 = jnp.where(p.sb >= 2, segw[pl.ds(0, 8)], -1.0)
    start = jnp.zeros((8, 128), F32)
    for d in range(16):
        fewer = (sq < d).astype(F32) + (s1 < d).astype(F32) + (s2 < d).astype(F32)
        count = jnp.sum(jnp.sum(fewer, axis=1, keepdims=True), axis=0, keepdims=True)
        start = start + jnp.where(sq == d, count, 0.0)
    start = start.astype(jnp.int32)
    for t in range(4):
        for h in range(3):
            for j in range(2):
                stq[pl.ds(t, 1), pl.ds(h * 256 + j * 128, 128)] = start[2 * t + j : 2 * t + j + 1]

    qg2 = jnp.concatenate([qg[...], qg[...]], axis=1)
    gqk = jnp.concatenate([qg2, qg[...], kg[...]], axis=1)

    def project(t):
        x = bo[tile(t)]
        qk = mm(x, wa[:, 0:256], NN)
        ov = mm(x, wa[:, 256:512], NN)
        qkraw[tile(t)] = qk
        n = qk * lax.rsqrt(head_mean(qk * qk) + EPS) * gqk
        c1, s1 = ctab[tile(t)], stab[tile(t)]
        c2, s2 = jnp.concatenate([c1, c1], 1), jnp.concatenate([s1, s1], 1)
        r = n * c2 + swap(n) * s2
        a0, a1 = r[:, :128], r[:, 128:]
        low = lanes((TILE, 128)) < 64
        q[0, tile(t)] = jnp.where(low, a0, 0.0).astype(BF)
        q[1, tile(t)] = jnp.where(low, pltpu.roll(a0, 64, 1), 0.0).astype(BF)
        q[2, tile(t)] = jnp.where(low, a1, 0.0).astype(BF)
        kv = jnp.where(low, pltpu.roll(a1, 64, 1), ov[:, 128:])
        kvw[ds(2048 + t * 256, 256)] = kv.astype(BF)
        kvt[8 + t] = kv.T.astype(BF)

    loop(4, project)
    kv_own = kvw.at[pl.ds(2048, 1024)]
    kv_sent = []
    for j in (1, 2):
        k = rcopy(kv_own, kvw.at[pl.ds(2048 - 1024 * j, 1024)], kvs.at[j - 1], kvr.at[j - 1], p.at_sb(j))
        k.start()
        kv_sent.append(k)

    def kv_wait(j):
        there = kvw.at[pl.ds(2048 - 1024 * j, 1024)]
        rcopy(there, there, kvs.at[j - 1], kvr.at[j - 1], p.sib).wait_recv()

        def turn(t):
            u = 8 - 4 * j + t
            kvt[u] = kvw[tile(u)].astype(F32).T.astype(BF)

        loop(4, turn)

    WD.first()
    WD.second()
    key_at = lax.broadcasted_iota(jnp.int32, (TILE, 3 * TILE), 0)
    scale = 0.125

    def mask_of(t, u, diag):
        ok = key_at >= stq[pl.ds(t, 1)] - u * TILE
        if diag:
            ok = ok & (key_at <= lax.rem(lanes((TILE, 3 * TILE)), TILE))
        return ok

    def forward(t, u, diag):
        k = kvw[tile(u)]
        q3 = q[:, tile(t)].reshape(3 * TILE, 128)
        s = mm(k, q3, NT)
        e = jnp.where(mask_of(t, u, diag), jnp.exp2(s * (scale * LOG2E)), 0.0).astype(BF)
        va = jnp.where(lax.broadcasted_iota(jnp.int32, (128, TILE), 0) < 64, 1.0, kvt[u].astype(F32)).astype(BF)
        new = mm(va, e, NN)
        if diag:
            acc[t] = new
        else:
            acc[t] = acc[t] + new

    loop(4, lambda t: forward(t, t + 8, True))
    GO.relay()
    loop(3, lambda i: lax.fori_loop(0, i + 1, lambda j, c: (forward(i + 1, 8 + j, False), c)[1], 0))
    GO.rest()
    kv_wait(1)
    WF.spread(2)
    WF.relay(0)
    loop(4, lambda t: forward(t, 7, False))
    loop(4, lambda t: forward(t, 6, False))
    loop(4, lambda t: forward(t, 5, False))
    loop(4, lambda t: forward(t, 4, False))
    kv_wait(2)
    WF.relay(3, 1, 2)
    for k in kv_sent:
        k.wait_send()

    def attended(t):
        a = acc[t]
        o = a[64:128] / a[0:64]
        lse[pl.ds(t, 1)] = jnp.log2(a[0:1])
        ot = jnp.concatenate([o[:, 0:256], o[:, 256:512], o[:, 512:768], jnp.zeros((64, 256), F32)], axis=0)
        o2 = ot.T
        att[tile(t)] = o2.astype(BF)

    R1 = ReduceX(p, pa, psib, phalf, pfull, rxs.at[0], rxr.at[0])

    def finish(d):
        x = lax.rem(p.x + d, 4)
        lax.fori_loop(x, 4, lambda u, c: (forward(x, u, False), c)[1], 0)
        attended(x)
        for j in range(3):
            n = pl.ds(j * 512, 512)
            pa[tile(x), n] = mm(att[tile(x)], wa[n, 256:512], NT).astype(BF)
        R1.to_sib(d)

    finish(2)
    GO.far()
    finish(1)
    WD.spread(3, 1, 2)
    R1.far()
    finish(3)
    R1.right()
    R1.left()
    finish(0)
    R1.near()
    WD.relay(0)
    for d in range(4):
        GO.sib(d)
    GO.end()
    m = tokens[...].astype(F32) + R1.final()
    mid[...] = m
    b2[own_rows] = (m * rms_inv(m) * ffn_gain[...]).astype(BF)
    G2 = GatherX(p, b2, gxs.at[2], gxr.at[2])
    G2.own()
    WF.end()

    def ffn_up(d):
        r = tile(lax.rem(p.x + d, 4))
        for lo, n in ((0, 512), (512, HP - 512)):
            gate = mm(b2[r], wf[:, lo : lo + n], NN)
            up = mm(b2[r], wf[:, HP + lo : HP + lo + n], NN)
            sig = jax.nn.sigmoid(gate)
            swish = gate * sig
            hid[r, lo : lo + n] = (swish * up).astype(BF)
            dg[r, lo : lo + n] = (up * sig * (1.0 + gate * (1.0 - sig))).astype(BF)
            du[r, lo : lo + n] = swish.astype(BF)

    def ffn_down(d):
        r = tile(lax.rem(p.x + d, 4))
        for lo, n in ((0, 512), (512, HP - 512)):
            dh = mm(og[r], wf[:, 2 * HP + lo : 2 * HP + lo + n], NN)
            dg[r, lo : lo + n] = (dh * dg[r, lo : lo + n].astype(F32)).astype(BF)
            du[r, lo : lo + n] = (dh * du[r, lo : lo + n].astype(F32)).astype(BF)

    G2.sib(0)
    ffn_up(0)
    G2.relay()
    G2.rest()
    WD.relay(3, 1, 2)
    G2.sib(3)
    ffn_up(3)
    G2.far()
    G2.sib(1)
    ffn_up(1)
    G2.sib(2)
    G2.end()
    ffn_up(2)
    WD.end()

    R2 = ReduceX(p, pa, psib, phalf, pfull, rxs.at[1], rxr.at[1])
    R3 = ReduceX(p, pa, psib, phalf, pfull, rxs.at[2], rxr.at[2])

    def back_in(d):
        ffn_down(d)
        r = tile(lax.rem(p.x + d, 4))
        for j in range(3):
            n = pl.ds(j * 512, 512)
            v = mm(dg[r], wf[n, 0:HP], NT) + mm(du[r], wf[n, HP : 2 * HP], NT)
            pa[r, n] = v.astype(BF)
        R2.to_sib(d)

    def branch(d):
        r = tile(lax.rem(p.x + d, 4))
        for j in range(3):
            n = pl.ds(j * 512, 512)
            pa[r, n] = mm(hid[r], wf[n, 2 * HP :], NT).astype(BF)
        R3.to_sib(d)

    def grads(cols, left, right, lo=0, hi=6):
        def body(i, carry):
            c = pl.ds(pl.multiple_of(i * 256, 256), 256)
            wf[tile(i), cols] = mm(left[:, c], right[...], TN).astype(BF)
            return carry

        lax.fori_loop(lo, hi, body, 0)

    back_in(2)
    back_in(1)
    R2.far()
    back_in(3)
    R2.right()
    R2.left()
    back_in(0)
    def reduce_ffn(g):
        cols = pl.ds(g * HP, HP)
        unit = lambda h, u: wf.at[ds(u * 96 + h * 48, 48), cols]
        return ReduceW(
            p, unit, fr.at[g], gf_mine.at[:, cols], gf_other.at[:, cols], fx.at[:, cols], wsx.at[2 + g], rfs.at[g], rfr.at[g], False
        )

    RF0, RF1, RF2 = reduce_ffn(0), reduce_ffn(1), reduce_ffn(2)
    grads(pl.ds(0, HP), b2, dg, 0, 2)
    R2.near()
    grads(pl.ds(0, HP), b2, dg, 2, 6)
    RF0.begin()

    dn = R2.final()
    m = mid[...]
    r = rms_inv(m)
    n = m * r
    e = dn * ffn_gain[...]
    dm = out_grad[...].astype(F32) + r * (e - n * jnp.mean(e * n, axis=-1, keepdims=True))
    dmid[...] = dm
    gbuf[...] = jnp.zeros_like(gbuf)
    by_col = jnp.sum(dn * n, axis=0, keepdims=True)
    for i in range(12):
        gbuf[pl.ds(12 + i, 1)] = by_col[:, i * 128 : i * 128 + 128]
    mr[own_rows] = dm.astype(BF)
    G3 = GatherX(p, mr, gxs.at[3], gxr.at[3])
    G3.own()

    grads(pl.ds(HP, HP), b2, du, 0, 3)
    G3.relay()
    grads(pl.ds(HP, HP), b2, du, 3, 6)
    RF1.begin()
    G3.rest()
    RF0.pass_on()
    G3.sib(0)
    for d in (2, 1, 3, 0):
        branch(d)
    G3.far()
    grads(pl.ds(2 * HP, HP), og, hid)
    RF2.begin()
    RF1.pass_on()
    for d in (3, 1, 2):
        G3.sib(d)
    G3.end()
    R3.far()
    RF0.over_a()

    head_row = lax.broadcasted_iota(jnp.int32, (8, 256), 0)
    head_lane = lanes((8, 256)) // 64
    per_head = jnp.where(head_row == head_lane, 1.0, 0.0).astype(F32)

    def d_attended(t):
        d = mm(mr[tile(t)], wa[:, 256:512], NN).astype(BF).astype(F32)
        sums = mm(per_head, d * att[tile(t)].astype(F32), NT, HI)
        for h in range(3):
            dlt[pl.ds(t, 1), pl.ds(h * 256, 256)] = sums[h : h + 1]
        a0, a1 = d[:, :128], d[:, 128:]
        high = lanes((TILE, 128)) >= 64
        do[0, tile(t)] = jnp.where(high, pltpu.roll(a0, 64, 1), 0.0).astype(BF)
        do[1, tile(t)] = jnp.where(high, a0, 0.0).astype(BF)
        do[2, tile(t)] = jnp.where(high, pltpu.roll(a1, 64, 1), 0.0).astype(BF)
        acc[t] = jnp.zeros((128, 768), F32)

    loop(4, d_attended)
    R3.right()
    R3.left()
    dkv[...] = jnp.zeros_like(dkv)
    RF1.over_a()
    RF2.pass_on()

    def backward(t, u, diag):
        k = kvw[tile(u)]
        q3 = q[:, tile(t)].reshape(3 * TILE, 128)
        do3 = do[:, tile(t)].reshape(3 * TILE, 128)
        s = mm(k, q3, NT)
        pr = jnp.where(mask_of(t, u, diag), jnp.exp2(s * (scale * LOG2E) - lse[pl.ds(t, 1)]), 0.0)
        dp = mm(k, do3, NT)
        dsc = (pr * (dp - dlt[pl.ds(t, 1)])).astype(BF)
        dkv[u] = dkv[u] + mm(dsc, q3, NN) + mm(pr.astype(BF), do3, NN)
        acc[t] = acc[t] + mm(kvt[u], dsc, NN)

    def scaled(v):
        return jnp.where(lanes(v.shape) < 64, v * scale, v)

    dk_sent = []

    def dk_send(j):
        def body(t):
            dks[j - 1, tile(t)] = scaled(dkv[8 - 4 * j + t]).astype(BF)

        loop(4, body)
        k = rcopy(dks.at[j - 1], dkr.at[j - 1], kvs.at[1 + j], kvr.at[1 + j], p.at_sb(-j))
        k.start()
        dk_sent.append(k)

    loop(4, lambda i: lax.fori_loop(0, i + 1, lambda t, c: (backward(t, i, False), c)[1], 0))
    dk_send(2)
    R3.near()
    RF0.last()
    loop(4, lambda t: backward(t, 4, False))
    loop(4, lambda t: backward(t, 5, False))
    RF2.over_a()
    RF1.last()
    loop(4, lambda t: backward(t, 6, False))
    loop(4, lambda t: backward(t, 7, False))
    dk_send(1)
    result[...] = (mid[...] + R3.final()).astype(BF)
    for dev in (p.sib, p.at_x(1), p.at_x(3)):
        pl.semaphore_signal(free, inc=1, device_id=dev, device_id_type=MESH)
    loop(3, lambda i: lax.fori_loop(0, i + 1, lambda j, c: (backward(i + 1, 8 + j, False), c)[1], 0))
    RF2.last()
    RF0.end()
    RF1.end()
    loop(4, lambda t: backward(t, t + 8, True))
    RF2.end()
    for j in (1, 2):
        rcopy(dkr.at[j - 1], dkr.at[j - 1], kvs.at[1 + j], kvr.at[1 + j], p.sib).wait_recv()
    for k in dk_sent:
        k.wait_send()

    def unproject(t):
        a = acc[t][0:64]
        at = jnp.concatenate([a[:, 0:256], a[:, 256:512], a[:, 512:768], jnp.zeros((64, 256), F32)], axis=0)
        dq = at.T * scale
        dk = scaled(dkv[8 + t]) + dkr[0, tile(t)].astype(F32) + dkr[1, tile(t)].astype(F32)
        low = lanes((TILE, 128)) < 64
        d = jnp.concatenate([dq[:, :128], jnp.where(low, dq[:, 128:], pltpu.roll(dk, 64, 1))], 1)
        d = d.astype(BF).astype(F32)
        c1, s1 = ctab[tile(t)], stab[tile(t)]
        c2, s2 = jnp.concatenate([c1, c1], 1), jnp.concatenate([s1, s1], 1)
        dn = d * c2 + swap(d * s2)
        raw = qkraw[tile(t)]
        r = lax.rsqrt(head_mean(raw * raw) + EPS)
        n = raw * r
        e = dn * gqk
        dx = r * (e - n * head_mean(e * n))
        by_lane = jnp.sum(dn * n, axis=0, keepdims=True)
        for j in range(2):
            gbuf[pl.ds(24 + j, 1)] = gbuf[pl.ds(24 + j, 1)] + by_lane[:, j * 128 : j * 128 + 128]
        dall[tile(t), 0:256] = dx.astype(BF)
        dall[tile(t), 256:384] = jnp.zeros((TILE, 128), BF)
        dall[tile(t), 384:512] = jnp.where(low, 0.0, dk).astype(BF)

    def attn_grads(i):
        c = pl.ds(pl.multiple_of(i * 384, 128), 384)
        for lo in (0, 256):
            v = mm(bo[:, c], dall[:, lo : lo + 256], TN)
            if lo:
                v = v + mm(mr[:, c], att[...], TN)
            v = v.astype(BF)
            for j in range(8):
                fr[0, j % 2, i * 4 + j // 2, :, lo : lo + 256] = v[j * 48 : j * 48 + 48]

    pl.semaphore_wait(free, 3)
    R4 = ReduceX(p, pa, psib, phalf, pfull, rxs.at[3], rxr.at[3])
    total = [jnp.zeros((1, 512), F32)] * 3
    for d in (2, 1, 3, 0):
        x = lax.rem(p.x + d, 4)
        unproject(x)
        for j in range(3):
            n = pl.ds(j * 512, 512)
            v = mm(dall[tile(x), 0:512], wa[n, :], NT)
            pa[tile(x), n] = v.astype(BF)
            total[j] = total[j] + jnp.sum(v * bo[tile(x), n].astype(F32), axis=0, keepdims=True)
        R4.to_sib(d)
        if d == 1:
            R4.far()
        if d == 3:
            R4.right()
            R4.left()
    for i in range(12):
        part = total[i // 4][:, i % 4 * 128 : i % 4 * 128 + 128]
        gbuf[pl.ds(i, 1)] = part / attn_gain[:, i * 128 : i * 128 + 128]
    sent = []
    gx[shard] = gbuf[...]
    for i, (d, cc) in enumerate(peers):
        k = rcopy(gbuf, gx.at[shard], gns.at[i], gnr.at[i], p.at_x(d, p.c if cc == 0 else 1 - p.c))
        k.start()
        sent.append(k)
    R4.near()
    loop(4, attn_grads)
    RA = ReduceW(p, lambda h, u: fr.at[0, h, u, :, 0:CA], ar, ga_mine, ga_other, axb, wsx.at[5], ras, rar, True)
    RA.begin()
    for i in range(7):
        rcopy(gx.at[i], gx.at[i], gns.at[i], gnr.at[i], p.sib).wait_recv()
    v = gx[0]
    for i in range(1, 8):
        v = v + gx[i]
    gy[p.y] = v
    for d in (1, 2, 3):
        k = rcopy(gy.at[p.y], gy.at[p.y], gns.at[6 + d], gnr.at[6 + d], p.at("y", d))
        k.start()
        sent.append(k)
    dn = R4.final()
    t = tokens[...].astype(F32)
    r = rms_inv(t)
    n = t * r
    e = dn * attn_gain[...]
    grad_tokens[...] = (dmid[...] + r * (e - n * jnp.mean(e * n, axis=-1, keepdims=True))).astype(BF)
    RA.over_a()
    for d in (1, 2, 3):
        rcopy(gy.at[0], gy.at[0], gns.at[6 + d], gnr.at[6 + d], p.sib).wait_recv()
    v = (gy[0] + gy[1]) + (gy[2] + gy[3])
    gz[p.z] = v
    for d in (1, 2, 3):
        k = rcopy(gz.at[p.z], gz.at[p.z], gns.at[9 + d], gnr.at[9 + d], p.at("z", d))
        k.start()
        sent.append(k)
    RA.last()
    for d in (1, 2, 3):
        rcopy(gz.at[0], gz.at[0], gns.at[9 + d], gnr.at[9 + d], p.sib).wait_recv()
    gains[...] = (gz[0] + gz[1]) + (gz[2] + gz[3])
    for k in sent:
        k.wait_send()
    RA.end()


VMEM_LIMIT = 63 * 2**20
VM = pl.BlockSpec(memory_space=pltpu.VMEM)


def call_kernel(*args):
    S = jax.ShapeDtypeStruct
    V = pltpu.VMEM
    dma = pltpu.SemaphoreType.DMA
    outs = (
        S((128, D), BF), S((128, D), BF), S((48, CA), BF), S((48, CA), BF),
        S((48, CF), BF), S((48, CF), BF), S((32, 128), F32),
    )
    scratch = [
        V((D, CA), BF), V((D, CF), BF), V((ROWS, D), BF), V((ROWS, D), BF), V((ROWS, D), BF), V((ROWS, D), BF),
        V((ROWS, HP), BF), V((ROWS, HP), BF), V((ROWS, HP), BF),
        V((3, 2, 16, 48, HP), BF), V((2, 15, 48, CA), BF), V((48, CF), BF), V((48, CA), BF),
        V((ROWS, D), BF), V((4, 128, D), BF), V((2, 64, D), BF), V((2, 128, D), BF),
        V((3, ROWS, 128), BF), V((3, ROWS, 128), BF), V((3 * ROWS, 128), BF), V((12, 128, TILE), BF),
        V((4, 128, 768), F32), V((12, TILE, 128), F32), V((2, ROWS, 128), BF), V((2, ROWS, 128), BF),
        V((ROWS, 256), BF), V((ROWS, 256), F32),
        V((128, D), F32), V((128, D), F32), V((ROWS, 128), F32), V((ROWS, 128), F32),
        V((64, 128), F32), V((24, 128), F32), V((8, 768), jnp.int32), V((8, 768), F32), V((8, 768), F32),
        V((32, 128), F32), V((8, 32, 128), F32), V((4, 32, 128), F32), V((4, 32, 128), F32),
        dma((7, 2)), dma((2, 15)), dma((2, 15)), dma((2, 2, 15)), dma((2, 2, 15)),
        dma((4, 14)), dma((4, 14)), dma((4, 10)), dma((4, 10)),
        dma((2, 15)), dma((2, 15)), dma((3, 2, 15)), dma((3, 2, 15)),
        dma((4,)), dma((4,)), dma((9,)), dma((9,)), dma((13,)), dma((13,)), pltpu.SemaphoreType.REGULAR,
    ]
    return pl.pallas_call(
        kernel,
        out_shape=outs,
        in_specs=[VM] * len(args),
        out_specs=(VM,) * len(outs),
        scratch_shapes=scratch,
        compiler_params=pltpu.CompilerParams(
            collective_id=0, has_side_effects=True, vmem_limit_bytes=VMEM_LIMIT
        ),
    )(*args)


def last_kernel(
    res, gtok, ga_mine, ga_other, gf_mine, gf_other, gains,
    result, grad_tokens, g_attn, g_query, g_key, g_value, g_qg, g_kg, g_out, g_ffn, g_gate, g_up, g_down,
):
    xh = lax.axis_index("xh")
    result[...] = res[...]
    grad_tokens[...] = gtok[...]
    for i in range(12):
        g_attn[:, i * 128 : i * 128 + 128] = gains[i : i + 1]
        g_ffn[:, i * 128 : i * 128 + 128] = gains[12 + i : 13 + i]
    a0, a1 = gains[24:25], gains[25:26]
    g_qg[...] = a0[:, 0:64] + pltpu.roll(a0, 64, 1)[:, 0:64] + a1[:, 0:64]
    g_kg[...] = pltpu.roll(a1, 64, 1)[:, 0:64]
    low = lanes((48, 128)) < 64
    for base, wide, narrow in ((0, g_query, g_key), (256, g_out, g_value)):
        m = [ga_mine[:, base + j * 128 : base + j * 128 + 128].astype(F32) for j in range(2)]
        o = [ga_other[:, base + j * 128 : base + j * 128 + 128].astype(F32) for j in range(2)]
        h0 = [jnp.where(xh == 0, a, b) for a, b in zip(m, o)]
        h1 = [jnp.where(xh == 0, b, a) for a, b in zip(m, o)]
        turned = [pltpu.roll(v, 64, 1) for v in h1]
        wide[:, 0:128] = h0[0]
        wide[:, 128:256] = jnp.where(low, h0[1], turned[0])
        wide[:, 256:384] = jnp.where(low, turned[0], turned[1])
        narrow[...] = jnp.where(low, pltpu.roll(h0[1], 64, 1), h1[1])
    for at in (0, 1):

        @pl.when(xh == at)
        def _(at=at):
            first, second = (gf_mine, gf_other) if at == 0 else (gf_other, gf_mine)
            for i, out in enumerate((g_gate, g_up, g_down)):
                out[:, 0:HP] = first[:, i * HP : (i + 1) * HP].astype(F32)
                out[:, HP:] = second[:, i * HP : i * HP + HQ].astype(F32)


def call_last(*args):
    S = jax.ShapeDtypeStruct
    outs = (
        S((128, D), BF), S((128, D), BF), S((1, D), F32), S((48, 384), F32), S((48, 128), F32), S((48, 128), F32),
        S((1, 64), F32), S((1, 64), F32), S((48, 384), F32), S((1, D), F32),
        S((48, HP + HQ), F32), S((48, HP + HQ), F32), S((48, HP + HQ), F32),
    )
    return pl.pallas_call(
        last_kernel,
        out_shape=outs,
        in_specs=[VM] * len(args),
        out_specs=(VM,) * len(outs),
        compiler_params=pltpu.CompilerParams(vmem_limit_bytes=VMEM_LIMIT),
    )(*args)


def on_device(
    tokens, segments, attn_gain, w_query, w_key, w_value, query_gain, key_gain, w_out, ffn_gain,
    w_gate, w_up, w_down, out_grad,
):
    steps = np.arange(32, dtype=np.float32) * np.float32(2.0 / 64)
    freqs = np.exp(-np.log(np.float32(THETA)) * steps).astype(np.float32)
    freq = jnp.asarray(np.tile(freqs, 4)[None, :])
    parts = call_kernel(
        tokens, segments[None], jnp.stack([attn_gain, ffn_gain]), query_gain[None], key_gain[None], freq,
        w_query, w_key, w_value, w_out.T, w_gate, w_up, w_down.T, out_grad,
    )
    out = list(call_last(*parts))
    for i in (2, 6, 7, 9):
        out[i] = out[i][0]
    for i in (8, 12):
        out[i] = out[i].T
    return tuple(out)


def solution(mesh):
    finer = Mesh(mesh.devices.reshape(4, 4, 2, 2, 2), AXES)
    rows, blk, narrow = P(AXES), ("z", "y", "xh"), ("xl", "core")
    cols, turned = P(blk, narrow), P(narrow, blk)
    in_specs = (rows, rows, P(), cols, cols, cols, P(), P(), turned, P(), cols, cols, turned, rows)
    out_specs = (rows, rows, P(), cols, cols, cols, P(), P(), turned, P(), cols, cols, turned)
    return jax.shard_map(
        on_device, mesh=finer, in_specs=in_specs, out_specs=out_specs, check_vma=False
    )
```
